32 devices in a mesh: dp: 2 (over y), ctx: 16 (over z, x, core).
Axes of the slice: x: 2, y: 2, z: 4, core: 2. Of those that a mesh axis runs over, the one named last changes fastest.
Arguments:
- tokens: bfloat16 [4, 512, 2, 1024], P('dp', 'ctx'), may hold values from -6 to 6
- segments: int32 [4, 512, 2], P('dp'), may hold values from 0 to 16, as said below
- lengths: int32 [4], P('dp'), may hold values from 512 to 768, as said below
- attn_in: bfloat16 [2048, 1024], P(('dp', 'ctx')), may hold values from -0.1875 to 0.1875
- attn_out: bfloat16 [1024, 1024], P(('dp', 'ctx')), may hold values from -0.75 to 0.75
- gains: bfloat16 [2176], P(('dp', 'ctx')), may hold values from 0.5 to 1.5
- ffn_weights: bfloat16 [4608, 3, 1024], P(('dp', 'ctx')), may hold values from -0.1875 to 0.1875
- cotangent: bfloat16 [4, 512, 2, 1024], P('dp', 'ctx'), may hold values from -6 to 6
Outputs:
- block_out: bfloat16 [4, 512, 2, 1024], P('dp', 'ctx')
- tokens_grad: float32 [4, 512, 2, 1024], P('dp', 'ctx')
- attn_in_grad: float32 [2048, 1024], P(('dp', 'ctx'))
- attn_out_grad: float32 [1024, 1024], P(('dp', 'ctx'))
- gains_grad: float32 [2176], P(('dp', 'ctx'))
- ffn_grad: float32 [4608, 3, 1024], P(('dp', 'ctx'))
The draws below stay inside these ranges and needn't reach their ends.
Inputs may be any that keep to these rules, and one draw needn't show every extreme that they name: `segments`: in each sequence, taken in order of position, the ids never fall and begin at 0. `lengths`: one sequence has exactly the largest length.
All inputs are finite; a program needn't handle non-finite values.
Results may differ from the reference program's by a relative error of at most 0.028.
Values may be sent and summed in bfloat16 or wider, within the bound.
A program may use at most 448 MiB of HBM per device.

```python
import jax
import jax.numpy as jnp
from jax import lax

D = 1024
FF = 4608
HEADS = 16
KV_HEADS = 8
HEAD_DIM = 64
BLK = 32
HALF = 512
SEQ_LEN = 1024
SEQS = 4
QKV_ROWS = 2048
OUT_ROWS = 1024
GAINS = 2176
N_CTX = 16


def mirrored_rows():
    rows = jnp.arange(HALF, dtype=jnp.int32)
    mirror = (2 * (HALF // BLK) - 1 - rows // BLK) * BLK + rows % BLK
    return jnp.stack([rows, mirror], axis=1)


def draw_segments(key, part):
    key = jax.random.fold_in(key, 23)
    rate_key, roll_key, start_key = jax.random.split(key, 3)
    regions = SEQ_LEN // BLK
    level = jax.random.randint(rate_key, (SEQS, regions), 0, 3)
    period = jnp.where(level == 0, 16, jnp.where(level == 1, 128, 1024)).astype(jnp.int32)
    period = jnp.repeat(period, BLK, axis=1)
    roll = jax.random.randint(roll_key, (SEQS, SEQ_LEN), 0, 1 << 30)
    places = jnp.arange(SEQ_LEN, dtype=jnp.int32)[None, :]
    opening = jax.random.randint(start_key, (SEQS, 1), 0, BLK)
    covered = (places > opening) & (places < opening + HALF)
    tail = (places >= 3 * SEQ_LEN // 4) & (places % 16 == 0)
    breaks = ((roll % period == 0) & jnp.logical_not(covered) | tail) & (places > 0)
    natural = jnp.minimum(jnp.cumsum(breaks.astype(jnp.int32), axis=1), SEQ_LEN // 64)
    return natural[:, mirrored_rows()].astype(jnp.int32)


def draw_lengths(key, part):
    key = jax.random.fold_in(key, 11)
    base_key, pick_key = jax.random.split(key)
    most = 3 * SEQ_LEN // 4
    base = jax.random.randint(base_key, (SEQS,), SEQ_LEN // 2, most + 1)
    chosen = jax.random.randint(pick_key, (), 0, SEQS)
    return jnp.where(jnp.arange(SEQS) == chosen, most, base).astype(jnp.int32)


def block_scale(own_key, shape, cuts, low, largest):
    def one(position, parts):
        draws = jax.random.uniform(jax.random.fold_in(jax.random.fold_in(own_key, 6), position), (parts,), jnp.float32, low / len(cuts), largest / len(cuts))
        return jnp.repeat(jnp.exp(draws), shape[position] // parts).reshape((-1,) + (1,) * (len(shape) - position - 1))

    level = one(*cuts[0])
    for cut in cuts[1:]:
        level = level * one(*cut)
    return level


def gaussian(stream_key, extent, deviation, bound, cuts=(), held_as=jnp.bfloat16):
    entries = jax.random.normal(stream_key, extent, jnp.float32) * deviation
    if len(cuts) > 0:
        entries = block_scale(stream_key, extent, cuts, -0.22, 0.18) * entries
    return jnp.clip(entries, min=-bound, max=bound).astype(held_as)


def setup_inputs(seed: int = 0) -> dict:
    key_list = jax.random.split(jax.random.key(seed), 9)
    tokens = gaussian(key_list[0], (SEQS, HALF, 2, D), 1.0, 6.0, ((0, 2), (1, 16)))
    segments = draw_segments(jax.random.fold_in(key_list[8], 71), 0)
    lengths = draw_lengths(jax.random.fold_in(key_list[8], 71), 0)
    attn_in = gaussian(key_list[3], (QKV_ROWS, D), D ** -0.5, 0.1875, ((0, 32),))
    attn_out = gaussian(key_list[4], (OUT_ROWS, D), 64 ** -0.5, 0.75, ((0, 32),))
    gains = jnp.clip(1.0 + 0.1 * jax.random.normal(key_list[5], (GAINS,), jnp.float32), 0.5, 1.5).astype(jnp.bfloat16)
    ffn_weights = gaussian(key_list[6], (FF, 3, D), D ** -0.5, 0.1875, ((0, 32),))
    cotangent = gaussian(key_list[7], (SEQS, HALF, 2, D), 1.0, 6.0, ((0, 2), (1, 16)))
    return dict(tokens=tokens, segments=segments, lengths=lengths, attn_in=attn_in, attn_out=attn_out, gains=gains, ffn_weights=ffn_weights, cotangent=cotangent)


EPS = 1e-05
ROPE_BASE = 1000000.0
MASKED = -1e+30
HIGH = lax.Precision.HIGHEST

@jax.custom_vjp
def low(v):
    return lax.optimization_barrier(v.astype(jnp.bfloat16)).astype(jnp.float32)

@jax.custom_vjp
def low_back(v):
    return v

def low_keep(v):
    return (low(v), None)

def low_pass(kept, grad):
    return (grad,)

def back_keep(v):
    return (v, None)

def back_low(kept, grad):
    return (low(grad),)
low.defvjp(low_keep, low_pass)
low_back.defvjp(back_keep, back_low)

def layout_positions():
    rows = jnp.arange(HALF, dtype=jnp.int32)
    mirror = (2 * N_CTX - 1 - rows // BLK) * BLK + rows % BLK
    return jnp.stack([rows, mirror], axis=1)

def rms(values, gain):
    return values * lax.rsqrt(lax.optimization_barrier(jnp.mean(values * values, axis=-1, keepdims=True)) + EPS) * gain

def rotate(values, cosine, sine):
    width = values.shape[-1] // 2
    first = values[..., :width]
    second = values[..., width:]
    return jnp.concatenate([first * cosine - second * sine, second * cosine + first * sine], axis=-1)

def tables(positions):
    width = HEAD_DIM // 2
    freq = ROPE_BASE ** (-jnp.arange(width, dtype=jnp.float32) * 2.0 / HEAD_DIM)
    angle = positions.astype(jnp.float32)[..., None] * freq
    return (jnp.cos(angle), jnp.sin(angle))

def attend(queries, keys, values, query_place, key_place, query_doc, key_doc, length):
    scores = jnp.einsum('qgjd,kgd->qgjk', queries, keys, precision=HIGH) * HEAD_DIM ** (-0.5)
    scores = low_back(scores)
    causal = key_place[None, :] <= query_place[:, None]
    live = (key_place[None, :] < length) | (key_place[None, :] == query_place[:, None])
    mask = (causal & live & (query_doc[:, None] == key_doc[None, :]))[:, None, None, :]
    scores = jnp.where(mask, scores, MASKED)
    peak = lax.optimization_barrier(jnp.max(scores, axis=-1, keepdims=True))
    expo = jnp.where(mask, jnp.exp(scores - peak), 0.0)
    weights = low(expo / lax.optimization_barrier(jnp.sum(expo, axis=-1, keepdims=True)))
    return jnp.einsum('qgjk,kgd->qgjd', weights, values, precision=HIGH)

def forward(inputs, weight_in, weight_out, gain_all, weight_ffn, segments, lengths, places):
    group = HEADS // KV_HEADS
    attn_gain = gain_all[:D]
    ffn_gain = gain_all[D:2 * D]
    query_gain = gain_all[2 * D:2 * D + HEAD_DIM]
    key_gain = gain_all[2 * D + HEAD_DIM:]
    cosine, sine = tables(places)
    rows = inputs.reshape(SEQS, 2 * HALF, D)
    first = low(rms(rows, attn_gain))
    projected = low_back(jnp.einsum('srd,fd->srf', first, weight_in, precision=HIGH))
    projected = projected.reshape(SEQS, 2 * HALF, KV_HEADS, group + 2, HEAD_DIM)
    queries = low(rotate(rms(projected[:, :, :, :group], query_gain), cosine[None, :, None, None], sine[None, :, None, None]))
    keys = low(rotate(rms(projected[:, :, :, group], key_gain), cosine[None, :, None], sine[None, :, None]))
    values = low(projected[:, :, :, group + 1])
    docs = segments.reshape(SEQS, 2 * HALF)
    span = 8 * BLK
    blocks = 2 * HALF // span

    def one_sequence(item):
        seq_queries, seq_keys, seq_values, seq_docs, length = item

        def one_block(part):
            block_queries, block_places, block_docs = part
            return attend(block_queries, seq_keys, seq_values, block_places, places, block_docs, seq_docs, length)
        mixed_rows = lax.map(jax.checkpoint(one_block), (seq_queries.reshape(blocks, span, KV_HEADS, group, HEAD_DIM), places.reshape(blocks, span), seq_docs.reshape(blocks, span)))
        return mixed_rows.reshape(2 * HALF, HEADS * HEAD_DIM)
    mixed = lax.map(one_sequence, (queries, keys, values, docs, lengths))
    mixed = low(low_back(mixed))
    state = rows + low_back(jnp.einsum('srf,fd->srd', mixed, weight_out, precision=HIGH))
    second = low(rms(state, ffn_gain))
    gate = low_back(jnp.einsum('srd,fd->srf', second, weight_ffn[:, 0], precision=HIGH))
    upward = low_back(jnp.einsum('srd,fd->srf', second, weight_ffn[:, 1], precision=HIGH))
    hidden = low(jax.nn.silu(gate) * upward)
    result = state + low_back(jnp.einsum('srf,fd->srd', hidden, weight_ffn[:, 2], precision=HIGH))
    return result.reshape(SEQS, HALF, 2, D)

def reference(tokens, segments, lengths, attn_in, attn_out, gains, ffn_weights, cotangent):
    places = layout_positions().reshape(2 * HALF)

    def run(inputs, weight_in, weight_out, gain_all, weight_ffn):
        return forward(inputs, weight_in, weight_out, gain_all, weight_ffn, segments, lengths, places)
    result, pull = jax.vjp(run, tokens.astype(jnp.float32), attn_in.astype(jnp.float32), attn_out.astype(jnp.float32), gains.astype(jnp.float32), ffn_weights.astype(jnp.float32))
    valid = (places[None, :] < lengths[:, None]).reshape(SEQS, HALF, 2)
    grad_out = cotangent.astype(jnp.float32) * valid[..., None].astype(jnp.float32)
    grads = pull(grad_out)
    return (result.astype(jnp.bfloat16), grads[0], grads[1], grads[2], grads[3], grads[4])
```

```python
import jax
import jax.numpy as jnp
import numpy as np
from jax import lax
from jax.sharding import Mesh
from jax.sharding import PartitionSpec as P

FF = 4608
HEADS = 16
KV_HEADS = 8
HEAD_DIM = 64
GROUP = HEADS // KV_HEADS
QKV_ROWS = 2048

EPS = 1e-05
ROPE_BASE = 1000000.0
MASKED = -1e30
BF = jnp.bfloat16
F32 = jnp.float32


def root_mean(values):
    return lax.rsqrt(jnp.mean(values * values, axis=-1, keepdims=True) + EPS)


def rotate(values, cosine, sine):
    width = values.shape[-1] // 2
    first = values[..., :width]
    second = values[..., width:]
    return jnp.concatenate(
        [first * cosine - second * sine, second * cosine + first * sine], axis=-1
    )


def tables(positions):
    width = HEAD_DIM // 2
    freq = ROPE_BASE ** (-jnp.arange(width, dtype=F32) * 2.0 / HEAD_DIM)
    angle = positions.astype(F32)[..., None] * freq
    return (jnp.cos(angle), jnp.sin(angle))


def prepare(query_raw, key_raw, query_gain, key_gain, cosine, sine):
    query_norm = query_raw * root_mean(query_raw) * query_gain
    key_norm = key_raw * root_mean(key_raw) * key_gain
    return (
        rotate(query_norm, cosine[:, None], sine[:, None]),
        rotate(key_norm, cosine, sine),
    )


def norm_back(grad, normed, scale_rows, gain):
    weighted = grad * gain
    inner = jnp.mean(weighted * normed, axis=-1, keepdims=True)
    return (scale_rows * (weighted - normed * inner), jnp.sum(grad * normed, axis=0))


def dot(a, b, ca, cb):
    return lax.dot_general(a, b, (((ca,), (cb,)), ((), ())), preferred_element_type=F32)


TEAM = ("dp", "s", "q")
EVERY = ("dp", "s", "q", "g")


def spread(local, block_len):
    mine = lax.all_to_all(local, "s", 0, 0, tiled=True)
    return lax.all_gather(mine, "g", axis=0, tiled=False)


def on_device(tokens, segments, lengths, attn_in, attn_out, gains, ffn_weights, cotangent):
    batches, block_len, halves, width = tokens.shape
    seq = lax.axis_index("s")
    quarter = lax.axis_index("q")
    head = lax.axis_index("g")
    quarters = lax.axis_size("q")
    heads = lax.axis_size("g")
    ctx_count = 2 * quarters * heads
    scale = HEAD_DIM ** (-0.5)
    weight_in = lax.all_gather(attn_in, EVERY, axis=0, tiled=True)
    weight_out = lax.all_gather(attn_out, EVERY, axis=0, tiled=True)
    gain_all = lax.all_gather(gains, EVERY, axis=0, tiled=True).astype(F32)
    attn_gain = gain_all[:width]
    ffn_gain = gain_all[width : 2 * width]
    query_gain = gain_all[2 * width : 2 * width + HEAD_DIM]
    key_gain = gain_all[2 * width + HEAD_DIM :]
    head_rows = (GROUP + 2) * HEAD_DIM
    out_rows = GROUP * HEAD_DIM
    weight_head = lax.dynamic_slice_in_dim(weight_in, head * head_rows, head_rows, 0)
    weight_mix = lax.dynamic_slice_in_dim(weight_out, head * out_rows, out_rows, 0)

    inputs = spread(tokens, block_len)
    count = inputs.size // width
    inputs = inputs.reshape(count, width).astype(F32)
    cot = spread(cotangent, block_len).reshape(count, width).astype(F32)

    def places(which):
        owner_g = jnp.arange(heads, dtype=jnp.int32)[:, None, None, None]
        owner_s = jnp.arange(2, dtype=jnp.int32)[None, :, None, None]
        row = jnp.arange(block_len, dtype=jnp.int32)[None, None, :, None]
        half = jnp.arange(2, dtype=jnp.int32)[None, None, None, :]
        owner = owner_s * (quarters * heads) + which * heads + owner_g
        block = jnp.where(half == 0, owner, 2 * ctx_count - 1 - owner)
        return (
            (block * block_len + row).reshape(count),
            jnp.broadcast_to((owner * block_len + row) * 2 + half, (heads, 2, block_len, 2)).reshape(count),
        )

    docs = lax.dynamic_index_in_dim(segments, seq, 0, False).reshape(-1)
    length = lax.dynamic_index_in_dim(lengths, seq, 0, False)
    place, slot = places(quarter)
    key_place, key_slot = jax.vmap(places)(jnp.arange(quarters, dtype=jnp.int32))
    key_place = key_place.reshape(-1)
    query_doc = docs[slot]
    key_doc = docs[key_slot.reshape(-1)]
    causal = key_place[None, :] <= place[:, None]
    live = (key_place[None, :] < length) | (key_place[None, :] == place[:, None])
    mask = causal & live & (query_doc[:, None] == key_doc[None, :])
    valid = (place < length).astype(F32)[:, None]

    first_scale = root_mean(inputs)
    first_normed = inputs * first_scale
    first = (first_normed * attn_gain).astype(BF)
    projected = dot(first, weight_head, 1, 1).reshape(count, GROUP + 2, HEAD_DIM)
    cosine, sine = tables(place)

    def prepare_here(query_raw, key_raw, gain_query, gain_key):
        return prepare(query_raw, key_raw, gain_query, gain_key, cosine, sine)

    (query_rot, key_rot), prepare_pull = jax.vjp(
        prepare_here, projected[:, :GROUP], projected[:, GROUP], query_gain, key_gain
    )
    queries = query_rot.astype(BF)
    pair = jnp.stack([key_rot.astype(BF), projected[:, GROUP + 1].astype(BF)])
    pair = lax.all_gather(pair, "q", axis=1, tiled=True)
    keys, values = pair[0], pair[1]

    scores = jnp.einsum("qjd,kd->jqk", queries, keys, preferred_element_type=F32) * scale
    scores = jnp.where(mask[None], scores, MASKED)
    peak = jnp.max(scores, axis=-1, keepdims=True)
    expo = jnp.where(mask[None], jnp.exp(scores - peak), 0.0)
    weights = expo / jnp.sum(expo, axis=-1, keepdims=True)
    attended = jnp.einsum("jqk,kd->qjd", weights.astype(BF), values, preferred_element_type=F32)
    mixed_here = attended.astype(BF).reshape(count, out_rows)
    mixed = lax.all_gather(mixed_here, "g", axis=1, tiled=True)
    state = inputs + dot(mixed, weight_out, 1, 0)
    second_scale = root_mean(state)
    second_normed = state * second_scale
    second = (second_normed * ffn_gain).astype(BF)
    grad_out = cot * valid
    grad_low = grad_out.astype(BF)

    units = lax.all_gather(ffn_weights, TEAM, axis=0, tiled=True)
    unit_gate, unit_up, unit_down = units[:, 0], units[:, 1], units[:, 2]
    gate = dot(second, unit_gate, 1, 1)
    upward = dot(second, unit_up, 1, 1)
    sigmoid = jax.nn.sigmoid(gate)
    hidden = (gate * sigmoid * upward).astype(BF)
    d_hidden = dot(grad_low, unit_down, 1, 1)
    d_gate = (d_hidden * upward * sigmoid * (1.0 + gate * (1.0 - sigmoid))).astype(BF)
    d_up = (d_hidden * gate * sigmoid).astype(BF)
    d_second = dot(d_gate, unit_gate, 1, 0) + dot(d_up, unit_up, 1, 0)
    own = count // heads

    def gathered(values):
        return lax.psum_scatter(values.astype(BF), "g", scatter_dimension=0, tiled=True).astype(F32)

    def own_rows(values):
        return lax.dynamic_slice_in_dim(values, head * own, own, 0)

    def home(values):
        back = values.reshape(2, block_len, halves, width)
        return lax.all_to_all(back, "s", 0, 0, tiled=True)

    ffn_sum = gathered(dot(hidden, unit_down, 1, 0))
    block_out = home((own_rows(state) + ffn_sum).astype(BF))
    ffn_grad = lax.psum_scatter(
        jnp.stack([dot(d_gate, second, 0, 0), dot(d_up, second, 0, 0), dot(hidden, grad_low, 0, 0)], axis=1),
        TEAM,
        scatter_dimension=0,
        tiled=True,
    )
    norm_grad, ffn_gain_grad = norm_back(
        gathered(d_second), own_rows(second_normed), own_rows(second_scale), ffn_gain
    )
    state_grad = own_rows(grad_out) + norm_grad
    attended_grad = lax.all_gather(state_grad.astype(BF), "g", axis=0, tiled=True)
    mixed_grad = dot(attended_grad, weight_mix, 1, 1).astype(BF)
    out_term = dot(mixed_here, attended_grad, 0, 0)
    mixed_grad = mixed_grad.reshape(count, GROUP, HEAD_DIM)
    delta = jnp.sum(mixed_grad.astype(F32) * attended, axis=-1).T[:, :, None]
    pulled = jnp.einsum("qjd,kd->jqk", mixed_grad, values, preferred_element_type=F32)
    score_grad = (weights * (pulled - delta)).astype(BF)
    query_grad = jnp.einsum("jqk,kd->qjd", score_grad, keys, preferred_element_type=F32) * scale
    key_grad = jnp.einsum("jqk,qjd->kd", score_grad, queries, preferred_element_type=F32) * scale
    value_grad = jnp.einsum("jqk,qjd->kd", weights.astype(BF), mixed_grad, preferred_element_type=F32)
    if quarters > 1:
        key_grad = lax.psum_scatter(key_grad, "q", scatter_dimension=0, tiled=True)
        value_grad = lax.psum_scatter(value_grad, "q", scatter_dimension=0, tiled=True)
    query_raw_grad, key_raw_grad, query_gain_grad, key_gain_grad = prepare_pull((query_grad, key_grad))
    projected_grad = jnp.concatenate(
        [query_raw_grad.reshape(count, out_rows), key_raw_grad, value_grad], axis=1
    ).astype(BF)
    first_grad = gathered(dot(projected_grad, weight_head, 1, 0))
    in_term = dot(projected_grad, first, 0, 0)
    input_norm_grad, attn_gain_grad = norm_back(
        first_grad, own_rows(first_normed), own_rows(first_scale), attn_gain
    )
    tokens_grad = home(state_grad + input_norm_grad)
    gain_term = jnp.concatenate([attn_gain_grad, ffn_gain_grad, query_gain_grad, key_gain_grad])

    def placed(term, rows):
        whole = jnp.zeros((rows, width), F32)
        return lax.dynamic_update_slice_in_dim(whole, term, head * term.shape[0], 0)

    return (
        block_out,
        tokens_grad,
        lax.psum_scatter(placed(in_term, QKV_ROWS), EVERY, scatter_dimension=0, tiled=True),
        lax.psum_scatter(placed(out_term, HEADS * HEAD_DIM), EVERY, scatter_dimension=0, tiled=True),
        lax.psum_scatter(gain_term, EVERY, scatter_dimension=0, tiled=True),
        ffn_grad,
    )


def solution(mesh):
    dp, ctx = mesh.devices.shape
    team = Mesh(mesh.devices.reshape(dp, 2, ctx // (2 * KV_HEADS), KV_HEADS), EVERY)
    ring = ("s", "q", "g")
    placed = (
        P("dp", ring, None, None),
        P("dp", None, None),
        P("dp"),
        P(EVERY, None),
        P(EVERY, None),
        P(EVERY),
        P(EVERY, None, None),
        P("dp", ring, None, None),
    )
    return jax.shard_map(
        on_device,
        mesh=team,
        in_specs=placed,
        out_specs=(
            P("dp", ring, None, None),
            P("dp", ring, None, None),
            P(EVERY, None),
            P(EVERY, None),
            P(EVERY),
            P(EVERY, None, None),
        ),
        check_vma=False,
    )
```

```python
import jax
import jax.numpy as jnp
import numpy as np
from jax import lax
from jax.experimental import pallas as pl
from jax.experimental.pallas import tpu as pltpu
from jax.sharding import Mesh
from jax.sharding import PartitionSpec as P

FF = 4608
HEADS = 16
KV_HEADS = 8
HEAD_DIM = 64
GROUP = HEADS // KV_HEADS
QKV_ROWS = 2048

EPS = 1e-05
ROPE_BASE = 1000000.0
MASKED = -1e30
BF = jnp.bfloat16
F32 = jnp.float32


def root_mean(values):
    return lax.rsqrt(jnp.mean(values * values, axis=-1, keepdims=True) + EPS)


def rotate(values, cosine, sine):
    width = values.shape[-1] // 2
    first = values[..., :width]
    second = values[..., width:]
    return jnp.concatenate(
        [first * cosine - second * sine, second * cosine + first * sine], axis=-1
    )


def tables(positions):
    width = HEAD_DIM // 2
    freq = ROPE_BASE ** (-jnp.arange(width, dtype=F32) * 2.0 / HEAD_DIM)
    angle = positions.astype(F32)[..., None] * freq
    return (jnp.cos(angle), jnp.sin(angle))


def prepare(query_raw, key_raw, query_gain, key_gain, cosine, sine):
    query_norm = query_raw * root_mean(query_raw) * query_gain
    key_norm = key_raw * root_mean(key_raw) * key_gain
    return (
        rotate(query_norm, cosine[:, None], sine[:, None]),
        rotate(key_norm, cosine, sine),
    )


def norm_back(grad, normed, scale_rows, gain):
    weighted = grad * gain
    inner = jnp.mean(weighted * normed, axis=-1, keepdims=True)
    return (scale_rows * (weighted - normed * inner), jnp.sum(grad * normed, axis=0))


def dot(a, b, ca, cb):
    return lax.dot_general(a, b, (((ca,), (cb,)), ((), ())), preferred_element_type=F32)


TEAM = ("dp", "s", "q")
EVERY = ("dp", "s", "q", "g")


def spread(local, block_len):
    mine = lax.all_to_all(local, "s", 0, 0, tiled=True)
    return lax.all_gather(mine, "g", axis=0, tiled=False)


def on_device(tokens, segments, lengths, attn_in, attn_out, gains, ffn_weights, cotangent):
    batches, block_len, halves, width = tokens.shape
    seq = lax.axis_index("s")
    quarter = lax.axis_index("q")
    head = lax.axis_index("g")
    quarters = lax.axis_size("q")
    heads = lax.axis_size("g")
    ctx_count = 2 * quarters * heads
    scale = HEAD_DIM ** (-0.5)
    weight_in = lax.all_gather(attn_in, EVERY, axis=0, tiled=True)
    weight_out = lax.all_gather(attn_out, EVERY, axis=0, tiled=True)
    gain_all = lax.all_gather(gains, EVERY, axis=0, tiled=True).astype(F32)
    attn_gain = gain_all[:width]
    ffn_gain = gain_all[width : 2 * width]
    query_gain = gain_all[2 * width : 2 * width + HEAD_DIM]
    key_gain = gain_all[2 * width + HEAD_DIM :]
    head_rows = (GROUP + 2) * HEAD_DIM
    out_rows = GROUP * HEAD_DIM
    weight_head = lax.dynamic_slice_in_dim(weight_in, head * head_rows, head_rows, 0)
    weight_mix = lax.dynamic_slice_in_dim(weight_out, head * out_rows, out_rows, 0)

    inputs = spread(tokens, block_len)
    count = inputs.size // width
    inputs = inputs.reshape(count, width).astype(F32)
    cot = spread(cotangent, block_len).reshape(count, width).astype(F32)

    def places(which):
        owner_g = jnp.arange(heads, dtype=jnp.int32)[:, None, None, None]
        owner_s = jnp.arange(2, dtype=jnp.int32)[None, :, None, None]
        row = jnp.arange(block_len, dtype=jnp.int32)[None, None, :, None]
        half = jnp.arange(2, dtype=jnp.int32)[None, None, None, :]
        owner = owner_s * (quarters * heads) + which * heads + owner_g
        block = jnp.where(half == 0, owner, 2 * ctx_count - 1 - owner)
        return (
            (block * block_len + row).reshape(count),
            jnp.broadcast_to((owner * block_len + row) * 2 + half, (heads, 2, block_len, 2)).reshape(count),
        )

    docs = lax.dynamic_index_in_dim(segments, seq, 0, False).reshape(-1)
    length = lax.dynamic_index_in_dim(lengths, seq, 0, False)
    place, slot = places(quarter)
    key_place, key_slot = jax.vmap(places)(jnp.arange(quarters, dtype=jnp.int32))
    key_place = key_place.reshape(-1)
    query_doc = docs[slot]
    key_doc = docs[key_slot.reshape(-1)]
    causal = key_place[None, :] <= place[:, None]
    live = (key_place[None, :] < length) | (key_place[None, :] == place[:, None])
    mask = causal & live & (query_doc[:, None] == key_doc[None, :])
    valid = (place < length).astype(F32)[:, None]

    first_scale = root_mean(inputs)
    first_normed = inputs * first_scale
    first = (first_normed * attn_gain).astype(BF)
    projected = dot(first, weight_head, 1, 1).reshape(count, GROUP + 2, HEAD_DIM)
    cosine, sine = tables(place)

    def prepare_here(query_raw, key_raw, gain_query, gain_key):
        return prepare(query_raw, key_raw, gain_query, gain_key, cosine, sine)

    (query_rot, key_rot), prepare_pull = jax.vjp(
        prepare_here, projected[:, :GROUP], projected[:, GROUP], query_gain, key_gain
    )
    queries = query_rot.astype(BF)
    pair = jnp.stack([key_rot.astype(BF), projected[:, GROUP + 1].astype(BF)])
    pair = lax.all_gather(pair, "q", axis=1, tiled=True)
    keys, values = pair[0], pair[1]

    scores = jnp.einsum("qjd,kd->jqk", queries, keys, preferred_element_type=F32) * scale
    scores = jnp.where(mask[None], scores, MASKED)
    peak = jnp.max(scores, axis=-1, keepdims=True)
    expo = jnp.where(mask[None], jnp.exp(scores - peak), 0.0)
    weights = expo / jnp.sum(expo, axis=-1, keepdims=True)
    attended = jnp.einsum("jqk,kd->qjd", weights.astype(BF), values, preferred_element_type=F32)
    mixed_here = attended.astype(BF).reshape(count, out_rows)
    mixed = lax.all_gather(mixed_here, "g", axis=1, tiled=True)
    state = inputs + dot(mixed, weight_out, 1, 0)
    second_scale = root_mean(state)
    second_normed = state * second_scale
    second = (second_normed * ffn_gain).astype(BF)
    grad_out = cot * valid
    grad_low = grad_out.astype(BF)

    units = lax.all_gather(ffn_weights, TEAM, axis=0, tiled=True)
    unit_gate, unit_up, unit_down = units[:, 0], units[:, 1], units[:, 2]
    gate = dot(second, unit_gate, 1, 1)
    upward = dot(second, unit_up, 1, 1)
    sigmoid = jax.nn.sigmoid(gate)
    hidden = (gate * sigmoid * upward).astype(BF)
    d_hidden = dot(grad_low, unit_down, 1, 1)
    d_gate = (d_hidden * upward * sigmoid * (1.0 + gate * (1.0 - sigmoid))).astype(BF)
    d_up = (d_hidden * gate * sigmoid).astype(BF)
    d_second = dot(d_gate, unit_gate, 1, 0) + dot(d_up, unit_up, 1, 0)
    own = count // heads

    def gathered(values):
        return lax.psum_scatter(values.astype(BF), "g", scatter_dimension=0, tiled=True).astype(F32)

    def own_rows(values):
        return lax.dynamic_slice_in_dim(values, head * own, own, 0)

    def home(values):
        back = values.reshape(2, block_len, halves, width)
        return lax.all_to_all(back, "s", 0, 0, tiled=True)

    ffn_sum = gathered(dot(hidden, unit_down, 1, 0))
    block_out = home((own_rows(state) + ffn_sum).astype(BF))
    ffn_grad = lax.psum_scatter(
        jnp.stack([dot(d_gate, second, 0, 0), dot(d_up, second, 0, 0), dot(hidden, grad_low, 0, 0)], axis=1),
        TEAM,
        scatter_dimension=0,
        tiled=True,
    )
    norm_grad, ffn_gain_grad = norm_back(
        gathered(d_second), own_rows(second_normed), own_rows(second_scale), ffn_gain
    )
    state_grad = own_rows(grad_out) + norm_grad
    attended_grad = lax.all_gather(state_grad.astype(BF), "g", axis=0, tiled=True)
    mixed_grad = dot(attended_grad, weight_mix, 1, 1).astype(BF)
    out_term = dot(mixed_here, attended_grad, 0, 0)
    mixed_grad = mixed_grad.reshape(count, GROUP, HEAD_DIM)
    delta = jnp.sum(mixed_grad.astype(F32) * attended, axis=-1).T[:, :, None]
    pulled = jnp.einsum("qjd,kd->jqk", mixed_grad, values, preferred_element_type=F32)
    score_grad = (weights * (pulled - delta)).astype(BF)
    query_grad = jnp.einsum("jqk,kd->qjd", score_grad, keys, preferred_element_type=F32) * scale
    key_grad = jnp.einsum("jqk,qjd->kd", score_grad, queries, preferred_element_type=F32) * scale
    value_grad = jnp.einsum("jqk,qjd->kd", weights.astype(BF), mixed_grad, preferred_element_type=F32)
    if quarters > 1:
        key_grad = lax.psum_scatter(key_grad, "q", scatter_dimension=0, tiled=True)
        value_grad = lax.psum_scatter(value_grad, "q", scatter_dimension=0, tiled=True)
    query_raw_grad, key_raw_grad, query_gain_grad, key_gain_grad = prepare_pull((query_grad, key_grad))
    projected_grad = jnp.concatenate(
        [query_raw_grad.reshape(count, out_rows), key_raw_grad, value_grad], axis=1
    ).astype(BF)
    first_grad = gathered(dot(projected_grad, weight_head, 1, 0))
    in_term = dot(projected_grad, first, 0, 0)
    input_norm_grad, attn_gain_grad = norm_back(
        first_grad, own_rows(first_normed), own_rows(first_scale), attn_gain
    )
    tokens_grad = home(state_grad + input_norm_grad)
    gain_term = jnp.concatenate([attn_gain_grad, ffn_gain_grad, query_gain_grad, key_gain_grad])

    def placed(term, rows):
        whole = jnp.zeros((rows, width), F32)
        return lax.dynamic_update_slice_in_dim(whole, term, head * term.shape[0], 0)

    return (
        block_out,
        tokens_grad,
        lax.psum_scatter(placed(in_term, QKV_ROWS), EVERY, scatter_dimension=0, tiled=True),
        lax.psum_scatter(placed(out_term, HEADS * HEAD_DIM), EVERY, scatter_dimension=0, tiled=True),
        lax.psum_scatter(gain_term, EVERY, scatter_dimension=0, tiled=True),
        ffn_grad,
    )


LANES = 128
HALF_LANES = 64


def _nt(a, b):
    return lax.dot_general(a, b, (((1,), (1,)), ((), ())), preferred_element_type=F32)


def _nn(a, b):
    return lax.dot_general(a, b, (((1,), (0,)), ((), ())), preferred_element_type=F32)


def _tn(a, b):
    return lax.dot_general(a, b, (((0,), (0,)), ((), ())), preferred_element_type=F32)


MESH = pl.DeviceIdType.MESH
COPIES = 320


class Wires:
    def __init__(self, sems):
        self.sems = sems
        self.used = 0
        self.pending = []

    def sem(self):
        self.used += 1
        return self.sems.at[self.used - 1]

    def send(self, src, dst, to, arrives):
        copy = pltpu.make_async_remote_copy(
            src_ref=src, dst_ref=dst, send_sem=self.sem(), recv_sem=arrives,
            device_id=to, device_id_type=MESH,
        )
        copy.start()
        self.pending.append(copy)
        return copy

    def local(self, src, dst, arrives):
        copy = pltpu.make_async_copy(src, dst, arrives)
        copy.start()
        return copy

    def arrived(self, ref, sem):
        pltpu.make_async_copy(ref, ref, sem).wait()

    def finish(self, copies=None):
        copies = list(self.pending if copies is None else copies)
        for copy in copies:
            copy.wait_send()
        done = {id(copy) for copy in copies}
        self.pending = [copy for copy in self.pending if id(copy) not in done]


def block_kernel(
    tok, cot, win, wout, gain, wffn, doc_col, doc_row, length, cos_t, sin_t,
    o_block, o_tokens, o_in, o_out, o_gain, o_ffn,
    x, rel_t, rel_c, wa, w2, wall, wf, gb, grow, first2, raw, po,
    q0, q1, kk, vv, prob, att, mxs, mix, sec2, dy2, acts, asend,
    dsb, osb, dsr, osr, gr, gs, gt, dstate, dmb, daf, dmix,
    dkk, dvv, dqq, dpj, dpx, dfb, dfr, igs, ags, agr, agz, agt,
    bos, obs, bor, tgs, tgr, gg, ggq, gsum, ggy, ggz, sems,
):
    dp = lax.axis_index("dp")
    c = lax.axis_index("ctx")
    zh = lax.div(c, 8)
    g = lax.rem(c, 8)
    j = lax.div(g, 2)
    k = lax.rem(c, 2)
    chips = (j, j + 1 - 2 * lax.rem(j, 2), j + 2 - 4 * lax.div(j, 2), 3 - j)
    cores = (k, 1 - k)

    def quad(d, e):
        return (dp, zh * 8 + 2 * chips[d] + cores[e])

    sib = quad(0, 1)
    zp = (dp, lax.rem(c + 8, 16))
    zps = (dp, 8 * (1 - zh) + 2 * j + 1 - k)
    yp = (1 - dp, c)
    team = 2 * dp + zh
    team_y = 2 * (1 - dp) + zh
    team_z = 2 * dp + 1 - zh
    team_d = 3 - team
    czp = lax.rem(c + 8, 16)
    w = Wires(sems)
    others = [(d, e) for d in range(4) for e in range(2) if (d, e) != (0, 0)]

    def piece(chip):
        return chip + k * (3 - 2 * chip)

    def row_block(owner, half):
        return owner + half * (15 - 2 * owner)

    barrier = pltpu.get_barrier_semaphore()
    peers = [quad(d, e) for d, e in others] + [zp, zps, yp]
    for peer in peers:
        pl.semaphore_signal(barrier, inc=1, device_id=peer, device_id_type=MESH)
    pl.semaphore_wait(barrier, len(peers))

    def scatter_rows(src_of, dst_of, owner, sem):
        for e in range(2):
            half = cores[e]
            start = pl.multiple_of(row_block(owner, half) * 32, 32)
            for d in range(4):
                dst = dst_of(half, start)
                if (d, e) == (0, 0):
                    w.local(src_of(half), dst, sem)
                else:
                    w.send(src_of(half), dst, quad(d, e), sem)

    x_dst = lambda half, start: x.at[pl.ds(start, 32)]
    dy_dst = lambda half, start: dy2.at[pl.ds(pl.multiple_of(512 * half + start, 32), 32)]
    s_rel_t, s_rel_c, s_x0, s_x1, s_c0, s_c1 = (w.sem() for _ in range(6))
    w.send(tok.at[1 - zh], rel_t, zp, s_rel_t)
    s_wa = [w.sem() for _ in range(4)]
    s_wo = [w.sem() for _ in range(4)]
    s_g = [w.sem() for _ in range(4)]
    exchanges = (
        (win, lambda t: wa.at[t], s_wa),
        (gain, lambda t: gb.at[t, g], s_g),
        (wout, lambda t: wall.at[t, j, k], s_wo),
    )
    for src, at, sem in exchanges[:2]:
        w.send(src, at(team), yp, sem[0])
        w.send(src, at(team), zp, sem[1])
        w.local(src, at(team), sem[3])
    scatter_rows(lambda half: tok.at[zh, half], x_dst, c, s_x0)
    src, at, sem = exchanges[2]
    w.send(src, at(team), yp, sem[0])
    w.send(src, at(team), zp, sem[1])
    w.local(src, at(team), sem[3])
    held = []
    s_f = [[[w.sem() for _ in range(3)] for _ in range(4)] for _ in range(2)]

    def unit(kind, parity, slot):
        return wf.at[kind, parity, pl.ds(144 * slot, 144)]

    for kind in range(3):
        w.send(wffn.at[kind], unit(kind, k, 1), yp, s_f[0][1][kind])
        w.local(wffn.at[kind], unit(kind, k, 0), s_f[0][0][kind])
        w.send(wffn.at[kind], unit(kind, k, 0), sib, s_f[1][0][kind])
    for kind in range(3):
        wf[kind, 0, pl.ds(576, 64), :] = jnp.zeros((64, 1024), BF)
        wf[kind, 1, pl.ds(576, 64), :] = jnp.zeros((64, 1024), BF)

    w.arrived(rel_t, s_rel_t)
    scatter_rows(lambda half: rel_t.at[half], x_dst, czp, s_x1)
    for src, at, sem in exchanges[:2]:
        w.arrived(at(team_z), sem[1])
        w.send(at(team_z), at(team_z), yp, sem[2])
    w.send(cot.at[1 - zh], rel_c, zp, s_rel_c)
    for kind in range(3):
        w.send(wffn.at[kind], unit(kind, k, 2), zp, s_f[0][2][kind])
    for src, at, sem in exchanges[:2]:
        w.arrived(at(team_y), sem[0])
        w.arrived(at(team_d), sem[2])
        w.arrived(at(team), sem[3])
    s_w2 = w.sem()
    s_gq = w.sem()
    w2_rows = pl.ds(pl.multiple_of(64 * g, 64), 64)
    w.local(wa.at[j], w2.at[w2_rows], s_w2)
    for d, e in others:
        w.send(wa.at[chips[d]], w2.at[w2_rows], quad(d, e), s_w2)
        w.send(gb.at[:, g], gb.at[:, g], quad(d, e), s_gq)
    scatter_rows(lambda half: cot.at[zh, half], dy_dst, c, s_c0)
    src, at, sem = exchanges[2]
    w.arrived(at(team_z), sem[1])
    w.send(at(team_z), at(team_z), yp, sem[2])

    lane = lax.broadcasted_iota(jnp.int32, (1, LANES), 1)
    low_row = lane < HALF_LANES
    w.arrived(gb.at[:, pl.ds(0, 7)], s_gq)
    chunks = [jnp.zeros((1, LANES), F32) for _ in range(18)]
    for i in range(32):
        row = gb[i // 8, i % 8, 0:1, :]
        place, shift = divmod(68 * i, LANES)
        moved = pltpu.roll(row, shift, 1) if shift else row
        chunks[place] = chunks[place] + jnp.where(lane >= shift, moved, 0.0)
        if shift + 68 > LANES:
            chunks[place + 1] = chunks[place + 1] + jnp.where(lane < shift, moved, 0.0)
    for n in range(8):
        grow[0:1, LANES * n : LANES * (n + 1)] = chunks[n]
        grow[1:2, LANES * n : LANES * (n + 1)] = chunks[8 + n]
    flipped = pltpu.roll(chunks[16], HALF_LANES, 1)
    grow[2:3, 0:LANES] = jnp.where(low_row, chunks[16], flipped)
    grow[2:3, LANES : 2 * LANES] = jnp.where(low_row, flipped, chunks[16])
    attn_gain = grow[0:1, :]
    ffn_gain = grow[1:2, :]
    query_gain = grow[2:3, 0:LANES]
    key_gain = grow[2:3, LANES : 2 * LANES]

    my_rows = pl.multiple_of(512 * k, 512)
    other_rows = pl.multiple_of(512 * (1 - k), 512)
    w.arrived(x.at[pl.ds(0, 256)], s_x0)
    w.arrived(x.at[pl.ds(256, 256)], s_x1)
    w.arrived(w2, s_w2)
    own_head = pl.ds(pl.multiple_of(256 * k, 256), 256)
    sib_head = pl.ds(pl.multiple_of(256 * (1 - k), 256), 256)

    def project(t, carry):
        rows = pl.multiple_of(t * 256, 256)
        values = x[pl.ds(rows, 256), :].astype(F32)
        scale = lax.rsqrt(jnp.mean(values * values, axis=1, keepdims=True) + EPS)
        first = (values * scale * attn_gain).astype(BF)
        mine = pl.multiple_of(my_rows + rows, 256)
        first2[pl.ds(mine, 256), :] = first
        po[pl.ds(rows, 256), :] = _nt(first, w2[sib_head, :])
        raw[pl.ds(mine, 256), :] = _nt(first, w2[own_head, :])
        return carry

    lax.fori_loop(0, 2, project, 0)
    s_raw, s_first = w.sem(), w.sem()
    w.send(po, raw.at[pl.ds(my_rows, 512)], sib, s_raw)

    src, at, sem = exchanges[2]
    w.arrived(at(team_y), sem[0])
    w.arrived(at(team_d), sem[2])
    w.arrived(at(team), sem[3])
    s_wq, s_ws = [w.sem() for _ in range(3)], w.sem()
    for d in (1, 2, 3):
        w.send(wall.at[:, j, k], wall.at[:, j, k], quad(d, 0), s_wq[d - 1])
    w.arrived(rel_c, s_rel_c)
    scatter_rows(lambda half: rel_c.at[half], dy_dst, czp, s_c1)

    low = lax.broadcasted_iota(jnp.int32, (256, LANES), 1) < HALF_LANES
    quarter = lax.rem(lax.broadcasted_iota(jnp.int32, (256, LANES), 1), HALF_LANES) < 32

    def swap(v):
        return jnp.where(quarter, pltpu.roll(v, 96, 1), pltpu.roll(v, 32, 1))

    def head_sum(v):
        first = jnp.sum(jnp.where(low, v, 0.0), axis=1, keepdims=True)
        second = jnp.sum(jnp.where(low, 0.0, v), axis=1, keepdims=True)
        return jnp.where(low, first, second)

    def inverse_root(v):
        return lax.rsqrt(head_sum(v * v) * (1.0 / HEAD_DIM) + EPS)

    w.arrived(raw.at[pl.ds(0, 512)], s_raw)

    def rotate_rows(t, carry):
        rows = pl.ds(pl.multiple_of(t * 256, 256), 256)
        cosine, sine = cos_t[rows, :], sin_t[rows, :]
        query = raw[rows, 0:LANES]
        both = raw[rows, LANES : 2 * LANES]
        query = query * inverse_root(query) * query_gain
        query = (query * cosine + swap(query) * sine) * (HEAD_DIM**-0.5)
        q0[rows, :] = jnp.where(low, query, 0.0).astype(BF)
        q1[rows, :] = jnp.where(low, 0.0, query).astype(BF)
        key = both * inverse_root(both) * key_gain
        key = key * cosine + swap(key) * sine
        kk[rows, :] = jnp.where(low, key, pltpu.roll(key, HALF_LANES, 1)).astype(BF)
        vv[rows, :] = jnp.where(low, pltpu.roll(both, HALF_LANES, 1), both).astype(BF)
        return carry

    lax.fori_loop(0, 4, rotate_rows, 0)
    w.send(first2.at[pl.ds(my_rows, 512)], first2.at[pl.ds(my_rows, 512)], sib, s_first)

    s_mix = w.sem()
    head_lanes = pl.ds(pl.multiple_of(LANES * g, LANES), LANES)

    def forward_tile(t):
        lo, n = 256 * t, 256 * (t + 1)
        place = lax.broadcasted_iota(jnp.int32, (256, n), 0) + lo
        key_place = lax.broadcasted_iota(jnp.int32, (256, n), 1)
        same = doc_col[lo : lo + 256, :] == doc_row[0:1, 0:n]
        mask = (same & (key_place <= place)) | (key_place == place)
        outs = []
        for h, q in enumerate((q0, q1)):
            scores = jnp.where(mask, _nt(q[lo : lo + 256, :], kk[0:n, :]), MASKED)
            peak = jnp.max(scores, axis=1, keepdims=True)
            expo = jnp.exp(scores - peak)
            weights = (expo * (1.0 / jnp.sum(expo, axis=1, keepdims=True))).astype(BF)
            prob[h, lo : lo + 256, 0:n] = weights
            outs.append(_nn(weights, vv[0:n, :]))
        attended = jnp.where(low, outs[0], outs[1])
        att[lo : lo + 256, :] = attended
        mxs[lo : lo + 256, :] = attended.astype(BF)
        half = t // 2
        dst = mix.at[pl.ds(256 * (t % 2), 256), head_lanes]
        src = mxs.at[pl.ds(lo, 256)]
        for d in (1, 2, 3):
            w.send(src, dst, (dp, zh * 8 + 2 * chips[d] + half), s_mix)
        away = pltpu.make_async_remote_copy(
            src_ref=src, dst_ref=dst, send_sem=w.sem(), recv_sem=s_mix, device_id=sib, device_id_type=MESH
        )
        pl.when(k == half)(lambda: pltpu.make_async_copy(src, dst, s_mix).start())
        pl.when(k != half)(away.start)
        late.append((half, away))

    late, late_grads = [], []
    forward_tile(3)
    for d in (1, 2, 3):
        w.arrived(wall.at[:, j, k], s_wq[d - 1])
    w.send(wall.at[:, :, k], wall.at[:, :, k], sib, s_ws)
    w.arrived(unit(0, k, 2), s_f[0][2][0])
    held.append(w.send(unit(0, k, 2), unit(0, k, 3), yp, s_f[0][3][0]))
    forward_tile(1)
    forward_tile(2)
    forward_tile(0)

    w.arrived(dy2.at[pl.ds(0, 256)], s_c0)
    w.arrived(dy2.at[pl.ds(0, 256)], s_c1)
    limit = length[0:1, 0:1]

    def drop_rows(t, carry):
        rows = pl.ds(pl.multiple_of(my_rows + t * 128, 128), 128)
        place = lax.broadcasted_iota(jnp.int32, (128, 1), 0) + (my_rows + t * 128)
        kept = (place < limit).astype(F32)
        dy2[rows, :] = (dy2[rows, :].astype(F32) * kept).astype(BF)
        return carry

    lax.fori_loop(0, 4, drop_rows, 0)
    s_dy, s_sec = w.sem(), w.sem()
    w.send(dy2.at[pl.ds(my_rows, 512)], dy2.at[pl.ds(my_rows, 512)], sib, s_dy)
    w.arrived(unit(1, k, 2), s_f[0][2][1])
    held.append(w.send(unit(1, k, 2), unit(1, k, 3), yp, s_f[0][3][1]))

    w.arrived(wall.at[:, :, 0], s_ws)
    w.arrived(mix, s_mix)

    def attended_rows(rows):
        total = None
        for n in range(4):
            term = _nn(mix[rows, 256 * n : 256 * (n + 1)], wall[n].reshape(256, 1024))
            total = term if total is None else total + term
        return total

    def project_out(t, carry):
        rows = pl.ds(pl.multiple_of(t * 256, 256), 256)
        state = x[rows, :].astype(F32) + attended_rows(rows)
        scale = lax.rsqrt(jnp.mean(state * state, axis=1, keepdims=True) + EPS)
        mine = pl.ds(pl.multiple_of(my_rows + t * 256, 256), 256)
        sec2[mine, :] = (state * scale * ffn_gain).astype(BF)
        return carry

    lax.fori_loop(0, 2, project_out, 0)
    w.send(sec2.at[pl.ds(my_rows, 512)], sec2.at[pl.ds(my_rows, 512)], sib, s_sec)

    for kind in range(3):
        for slot in (1, 2, 3):
            if not (slot == 2 and kind < 2):
                w.arrived(unit(kind, k, slot), s_f[0][slot][kind])
            if slot == 2 and kind == 2:
                held.append(w.send(unit(kind, k, 2), unit(kind, k, 3), yp, s_f[0][3][kind]))
            held.append(w.send(unit(kind, k, slot), unit(kind, k, slot), sib, s_f[1][slot][kind]))
    for kind in range(3):
        w.arrived(unit(kind, k, 0), s_f[0][0][kind])
        for slot in range(4):
            w.arrived(unit(kind, 1 - k, slot), s_f[1][slot][kind])
    s_act = w.sem()
    s_ds = [[w.sem() for _ in range(2)] for _ in range(3)]
    s_os = [[w.sem() for _ in range(2)] for _ in range(3)]
    s_da = [w.sem() for _ in range(3)]

    def send_pieces(buf, into, t, sem):
        for d in (1, 2, 3):
            rows = pl.ds(pl.multiple_of(256 * t + 64 * piece(chips[d]), 64), 64)
            w.send(buf.at[rows], into.at[d - 1, t], quad(d, 0), sem[d - 1][t])

    for t in range(2):
        rows = pl.ds(pl.multiple_of(my_rows + 256 * t, 256), 256)
        here = pl.ds(256 * t, 256)
        for e in (1, 0):
            parity = cores[e]
            gate = _nt(sec2[rows, :], wf[0, parity])
            up = _nt(sec2[rows, :], wf[1, parity])
            d_hidden = _nt(dy2[rows, :], wf[2, parity])
            sigmoid = 1.0 / (1.0 + jnp.exp(-gate))
            silu = gate * sigmoid
            d_gate = (d_hidden * up * (sigmoid + silu * (1.0 - sigmoid))).astype(BF)
            d_up = (d_hidden * silu).astype(BF)
            hidden = (silu * up).astype(BF)
            for n, value in enumerate((d_gate, d_up, hidden)):
                if e == 1:
                    asend[n, here, :] = value
                else:
                    acts[n, rows, :] = value
            if e == 1:
                w.send(asend.at[:, here], acts.at[:, rows], sib, s_act)
        own = tuple(acts[n, rows, :] for n in range(3))
        far = tuple(asend[n, here, :] for n in range(3))
        dsb[here, :] = (
            _nn(own[0], wf[0, k]) + _nn(far[0], wf[0, 1 - k])
            + _nn(own[1], wf[1, k]) + _nn(far[1], wf[1, 1 - k])
        ).astype(BF)
        send_pieces(dsb, dsr, t, s_ds)
        osb[here, :] = (_nn(own[2], wf[2, k]) + _nn(far[2], wf[2, 1 - k])).astype(BF)
    w.finish(held)
    w.arrived(acts.at[:, pl.ds(0, 512)], s_act)
    w.arrived(sec2.at[pl.ds(0, 512)], s_sec)
    w.arrived(dy2.at[pl.ds(0, 512)], s_dy)
    s_gr = [[w.sem() for _ in range(3)] for _ in range(2)]
    s_gt = [w.sem() for _ in range(3)]
    for kind in range(3):
        right = dy2 if kind == 2 else sec2
        def columns(n, carry, kind=kind, right=right):
            cols = pl.ds(pl.multiple_of(n * 256, 256), 256)
            term = _tn(acts[kind], right[:, cols])
            for slot in range(4):
                wf[kind, 0, 144 * slot : 144 * (slot + 1), cols] = term[144 * slot : 144 * (slot + 1), :].astype(BF)
            return carry
        lax.fori_loop(0, 4, columns, 0)
        w.send(unit(kind, 0, 3), gr.at[1, kind], yp, s_gr[1][kind])
    for t in range(2):
        send_pieces(osb, osr, t, s_os)
    mine = piece(j)
    s_dm = w.sem()
    ffn_gain_grad = jnp.zeros((1, 1024), F32)
    for t in range(2):
        start = 256 * t + 64 * mine
        rows = pl.ds(pl.multiple_of(start, 64), 64)
        state = x[rows, :].astype(F32) + attended_rows(rows)
        scale = lax.rsqrt(jnp.mean(state * state, axis=1, keepdims=True) + EPS)
        normed = state * scale
        total = dsb[rows, :].astype(F32)
        for d in range(3):
            w.arrived(dsr.at[d, t], s_ds[d][t])
            total = total + dsr[d, t].astype(F32)
        ffn_gain_grad = ffn_gain_grad + jnp.sum(total * normed, axis=0, keepdims=True)
        weighted = total * ffn_gain
        inner = jnp.mean(weighted * normed, axis=1, keepdims=True)
        grad = dy2[pl.ds(pl.multiple_of(my_rows + start, 64), 64), :].astype(F32) + scale * (weighted - normed * inner)
        dstate[t] = grad
        low_grad = grad.astype(BF)
        daf[k, t, mine] = low_grad
        for n in range(4):
            dmb[t, :, 256 * n : 256 * (n + 1)] = _nt(low_grad, wall[n].reshape(256, 1024)).astype(BF)
        bos[t] = state
        for d, e in others:
            lanes = pl.ds(pl.multiple_of(LANES * (2 * chips[d] + cores[e]), LANES), LANES)
            w.send(dmb.at[t, :, lanes], dmix.at[k, t, mine], quad(d, e), s_dm)
        w.local(dmb.at[t, :, head_lanes], dmix.at[k, t, mine], s_dm)
    gg[...] = jnp.zeros_like(gg)
    gg[1:2, :] = ffn_gain_grad
    for d in (1, 2, 3):
        w.send(daf.at[k, :, mine], daf.at[k, :, mine], quad(d, 0), s_da[d - 1])

    def pass_grads(kind):
        w.arrived(gr.at[1, kind], s_gr[1][kind])
        gs[kind] = (wf[kind, 0, 288:432, :].astype(F32) + gr[1, kind].astype(F32)).astype(BF)
        w.send(gs.at[kind], gt.at[kind], zp, s_gt[kind])
        w.send(unit(kind, 0, 1), gr.at[0, kind], yp, s_gr[0][kind])

    home = zh + k * (1 - 2 * zh)

    def send_home(buf, into, sem):
        w.local(buf.at[home, 0], into.at[zh, k], sem)
        w.send(buf.at[1 - home, 0], into.at[zh, k], zp, sem)
        w.send(buf.at[1 - home, 1], into.at[zh, k], zps, sem)
        w.send(buf.at[home, 1], into.at[zh, k], sib, sem)

    s_bo = w.sem()

    def finish_blocks():
        for t in range(2):
            rows = pl.ds(pl.multiple_of(256 * t + 64 * mine, 64), 64)
            total = bos[t] + osb[rows, :].astype(F32)
            for d in range(3):
                w.arrived(osr.at[d, t], s_os[d][t])
                total = total + osr[d, t].astype(F32)
            obs[t] = total.astype(BF).reshape(2, 32, 1024)
        send_home(obs, bor, s_bo)

    s_das = w.sem()

    def share_state_grads():
        for d in range(3):
            w.arrived(daf.at[k, :, mine], s_da[d])
        w.send(daf.at[k], daf.at[k], sib, s_das)

    w.arrived(dmix, s_dm)

    def backward_tile(t):
        lo, n = 256 * t, 256 * (t + 1)
        d_out = dmix[...].reshape(1024, LANES)[lo : lo + 256, :].astype(F32)
        product = d_out * att[lo : lo + 256, :]
        parts = []
        for h, q in enumerate((q0, q1)):
            here = low if h == 0 else jnp.logical_not(low)
            d_head = jnp.where(here, d_out, 0.0).astype(BF)
            delta = jnp.sum(jnp.where(here, product, 0.0), axis=1, keepdims=True)
            weights = prob[h, lo : lo + 256, 0:n]
            pulled = _nt(d_head, vv[0:n, :])
            d_scores = (weights.astype(F32) * (pulled - delta)).astype(BF)
            parts.append(_nn(d_scores, kk[0:n, :]))
            dkk[0:n, :] += _tn(d_scores, q[lo : lo + 256, :])
            dvv[0:n, :] += _tn(weights, d_head)
        dqq[lo : lo + 256, :] = jnp.where(low, parts[0], parts[1]) * (HEAD_DIM**-0.5)

    dkk[...] = jnp.zeros_like(dkk)
    dvv[...] = jnp.zeros_like(dvv)
    backward_tile(3)
    pass_grads(0)
    finish_blocks()
    backward_tile(2)
    share_state_grads()
    pass_grads(1)
    backward_tile(1)
    backward_tile(0)

    def back_rows(t, carry):
        query_sum, key_sum = carry
        rows = pl.ds(pl.multiple_of(t * 256, 256), 256)
        cosine, sine = cos_t[rows, :], sin_t[rows, :]
        query = raw[rows, 0:LANES]
        both = raw[rows, LANES : 2 * LANES]

        def through(values, grads, gain_row):
            scale = inverse_root(values)
            normed = values * scale
            grads = grads * cosine - swap(grads) * sine
            weighted = grads * gain_row
            inner = head_sum(weighted * normed) * (1.0 / HEAD_DIM)
            return scale * (weighted - normed * inner), jnp.sum(grads * normed, axis=0, keepdims=True)

        query_back, query_term = through(query, dqq[rows, :], query_gain)
        d_key = dkk[rows, :]
        d_key = d_key + pltpu.roll(d_key, HALF_LANES, 1)
        key_back, key_term = through(both, d_key, key_gain)
        d_value = dvv[rows, :]
        d_value = d_value + pltpu.roll(d_value, HALF_LANES, 1)
        dpj[rows, 0:LANES] = query_back.astype(BF)
        dpj[rows, LANES : 2 * LANES] = jnp.where(low, key_back, d_value).astype(BF)
        return query_sum + query_term, key_sum + key_term

    zero_row = jnp.zeros((1, LANES), F32)
    query_sum, key_sum = lax.fori_loop(0, 4, back_rows, (zero_row, zero_row))
    s_dpx = w.sem()
    w.send(dpj.at[pl.ds(other_rows, 512)], dpx, sib, s_dpx)
    gg[2:3, 0:LANES] = query_sum + pltpu.roll(query_sum, HALF_LANES, 1)
    gg[2:3, LANES : 2 * LANES] = key_sum
    pass_grads(2)

    w.arrived(daf.at[0], s_das)
    flat_da = daf[...].reshape(1024, 1024)
    out_term = _tn(mxs[...], flat_da)
    s_df = [[w.sem() for _ in range(2)] for _ in range(3)]
    w.arrived(dpx, s_dpx)
    for t in range(2):
        here = pl.ds(256 * t, 256)
        rows = pl.ds(pl.multiple_of(my_rows + 256 * t, 256), 256)
        dfb[here, :] = (_nn(dpj[rows, :], w2[own_head, :]) + _nn(dpx[here, :], w2[sib_head, :])).astype(BF)
        send_pieces(dfb, dfr, t, s_df)
    w.arrived(first2.at[pl.ds(0, 512)], s_first)
    in_term = _tn(dpj[...], first2[...])
    s_ag = w.sem()
    for p in range(4):
        igs[p, 0:64, :] = in_term[64 * p : 64 * (p + 1), :].astype(BF)
        igs[p, 64:96, :] = out_term[32 * p : 32 * (p + 1), :].astype(BF)
        target = 4 * k + p
        away = pltpu.make_async_remote_copy(
            src_ref=igs.at[p], dst_ref=ags.at[j], send_sem=w.sem(), recv_sem=s_ag,
            device_id=(dp, zh * 8 + target), device_id_type=MESH,
        )
        pl.when(target == g)(lambda p=p: pltpu.make_async_copy(igs.at[p], ags.at[j], s_ag).start())
        pl.when(target != g)(away.start)
        late_grads.append((target, away))

    s_ar = [w.sem(), w.sem()]
    s_at = w.sem()
    w.arrived(ags, s_ag)
    w.send(ags.at[team_d], agr.at[1], yp, s_ar[1])
    w.send(ags.at[team_y], agr.at[0], yp, s_ar[0])

    attn_gain_grad = jnp.zeros((1, 1024), F32)
    for t in range(2):
        rows = pl.ds(pl.multiple_of(256 * t + 64 * mine, 64), 64)
        values = x[rows, :].astype(F32)
        scale = lax.rsqrt(jnp.mean(values * values, axis=1, keepdims=True) + EPS)
        normed = values * scale
        total = dfb[rows, :].astype(F32)
        for d in range(3):
            w.arrived(dfr.at[d, t], s_df[d][t])
            total = total + dfr[d, t].astype(F32)
        attn_gain_grad = attn_gain_grad + jnp.sum(total * normed, axis=0, keepdims=True)
        weighted = total * attn_gain
        inner = jnp.mean(weighted * normed, axis=1, keepdims=True)
        grad = dstate[t] + scale * (weighted - normed * inner)
        tgs[t] = grad.astype(BF).reshape(2, 32, 1024)
    s_tg = w.sem()
    send_home(tgs, tgr, s_tg)
    gg[0:1, :] = attn_gain_grad

    s_gg, s_gy, s_gz = w.sem(), w.sem(), w.sem()
    for d, e in others:
        w.send(gg, ggq.at[g], quad(d, e), s_gg)
    w.local(gg, ggq.at[g], s_gg)
    w.arrived(agr.at[1], s_ar[1])
    agz[...] = (ags[team_z].astype(F32) + agr[1].astype(F32)).astype(BF)
    w.send(agz, agt, zp, s_at)
    w.arrived(ggq, s_gg)
    total = ggq[0]
    for n in range(1, 8):
        total = total + ggq[n]
    gsum[0] = total
    w.send(gsum.at[0], ggy, yp, s_gy)

    for kind in range(3):
        w.arrived(gr.at[0, kind], s_gr[0][kind])
        w.arrived(gt.at[kind], s_gt[kind])
        o_ffn[kind] = wf[kind, 0, 0:144, :].astype(F32) + gr[0, kind].astype(F32) + gt[kind].astype(F32)
    w.arrived(bor, s_bo)
    o_block[...] = bor[...]
    w.arrived(ggy, s_gy)
    gsum[1] = total + ggy[...]
    w.send(gsum.at[1], ggz, zp, s_gz)
    w.arrived(agr.at[0], s_ar[0])
    w.arrived(agt, s_at)
    attn = ags[team].astype(F32) + agr[0].astype(F32) + agt[...].astype(F32)
    o_in[...] = attn[0:64, :]
    o_out[...] = attn[64:96, :]
    w.arrived(tgr, s_tg)
    o_tokens[...] = tgr[...].astype(F32)
    w.arrived(ggz, s_gz)
    o_gain[...] = gsum[1] + ggz[...]
    w.finish()
    for half, away in late:
        pl.when(k != half)(away.wait_send)
    for target, away in late_grads:
        pl.when(target != g)(away.wait_send)


TEAM_SCRATCH = (
    ((512, 1024), BF), ((2, 32, 1024), BF), ((2, 32, 1024), BF), ((4, 64, 1024), BF), ((512, 1024), BF),
    ((4, 4, 2, 32, 1024), BF), ((3, 2, 640, 1024), BF), ((4, 8, 8, 128), F32), ((8, 1024), F32),
    ((1024, 1024), BF), ((1024, 256), F32), ((512, 256), F32),
    ((1024, 128), BF), ((1024, 128), BF), ((1024, 128), BF), ((1024, 128), BF), ((2, 1024, 1024), BF),
    ((1024, 128), F32), ((1024, 128), BF), ((512, 1024), BF), ((1024, 1024), BF), ((1024, 1024), BF),
    ((3, 1024, 640), BF), ((3, 512, 640), BF),
    ((512, 1024), BF), ((512, 1024), BF), ((3, 2, 64, 1024), BF), ((3, 2, 64, 1024), BF),
    ((2, 3, 144, 1024), BF), ((3, 144, 1024), BF), ((3, 144, 1024), BF),
    ((2, 64, 1024), F32), ((2, 64, 1024), BF), ((2, 2, 4, 64, 1024), BF), ((2, 2, 4, 64, 128), BF),
    ((1024, 128), F32), ((1024, 128), F32), ((1024, 128), F32), ((1024, 256), BF), ((512, 256), BF),
    ((512, 1024), BF), ((3, 2, 64, 1024), BF),
    ((4, 96, 1024), BF), ((4, 96, 1024), BF), ((2, 96, 1024), BF), ((96, 1024), BF), ((96, 1024), BF),
    ((2, 64, 1024), F32), ((2, 2, 32, 1024), BF), ((2, 2, 32, 1024), BF), ((2, 2, 32, 1024), BF),
    ((2, 2, 32, 1024), BF),
    ((8, 1024), F32), ((8, 8, 1024), F32), ((2, 8, 1024), F32), ((8, 1024), F32), ((8, 1024), F32),
)


def rotary_lanes(rows):
    width = HEAD_DIM // 2
    freq = (ROPE_BASE ** (-np.arange(width, dtype=np.float32) * np.float32(2.0 / HEAD_DIM))).astype(np.float32)
    angle = (np.arange(rows, dtype=np.float32)[:, None] * freq).astype(np.float32).astype(np.float64)
    cosine, sine = np.cos(angle), np.sin(angle)
    return (
        np.tile(np.concatenate([cosine, cosine], 1), (1, 2)).astype(np.float32),
        np.tile(np.concatenate([-sine, sine], 1), (1, 2)).astype(np.float32),
    )


def on_team(tokens, segments, lengths, attn_in, attn_out, gains, ffn_weights, cotangent):
    batches, block_len, halves, width = tokens.shape
    here = lax.axis_index("ctx")
    seq = here // 8
    rows = segments.shape[1]
    docs = lax.dynamic_index_in_dim(segments, seq, 0, False)
    back = docs[:, 1].reshape(rows // block_len, block_len)[::-1].reshape(rows)
    docs = jnp.concatenate([docs[:, 0], back])
    limit = lax.dynamic_index_in_dim(lengths, seq, 0, False)
    doc_row = jnp.where(jnp.arange(2 * rows, dtype=jnp.int32) < limit, docs, -1)
    cosine, sine = rotary_lanes(2 * rows)
    args = (
        tokens.transpose(0, 2, 1, 3),
        cotangent.transpose(0, 2, 1, 3),
        attn_in,
        attn_out,
        jnp.pad(gains.astype(F32)[None], ((0, 7), (0, LANES - gains.shape[0]))),
        ffn_weights.transpose(1, 0, 2),
        docs[:, None],
        doc_row[None],
        jnp.broadcast_to(limit, (8, LANES)),
        jnp.asarray(cosine),
        jnp.asarray(sine),
    )
    vmem = pl.BlockSpec(memory_space=pltpu.VMEM)
    outs = pl.pallas_call(
        block_kernel,
        out_shape=(
            jax.ShapeDtypeStruct((2, 2, 32, 1024), BF),
            jax.ShapeDtypeStruct((2, 2, 32, 1024), F32),
            jax.ShapeDtypeStruct((64, 1024), F32),
            jax.ShapeDtypeStruct((32, 1024), F32),
            jax.ShapeDtypeStruct((8, 1024), F32),
            jax.ShapeDtypeStruct((3, 144, 1024), F32),
        ),
        in_specs=[vmem] * len(args),
        out_specs=(vmem,) * 6,
        scratch_shapes=[pltpu.VMEM(shape, kind) for shape, kind in TEAM_SCRATCH]
        + [pltpu.SemaphoreType.DMA((COPIES,))],
        compiler_params=pltpu.CompilerParams(
            collective_id=0, has_side_effects=True, vmem_limit_bytes=VMEM_BYTES
        ),
    )(*args)
    block, token_grad, in_grad, out_grad, gain_grad, unit_grad = outs
    every = jnp.concatenate([gain_grad[0], gain_grad[1], gain_grad[2, :64], gain_grad[2, 128:192]])
    own = lax.axis_index("dp") * lax.axis_size("ctx") + here
    return (
        block.transpose(0, 2, 1, 3),
        token_grad.transpose(0, 2, 1, 3),
        in_grad,
        out_grad,
        lax.dynamic_slice_in_dim(every, own * gains.shape[0], gains.shape[0], 0),
        unit_grad.transpose(1, 0, 2),
    )


VMEM_BYTES = 62 << 20


def solution(mesh):
    dp, ctx = mesh.devices.shape
    if ctx == 2 * KV_HEADS:
        ring = "ctx"
        every = ("dp", "ctx")
        team, run = mesh, on_team
    else:
        ring = ("s", "q", "g")
        every = EVERY
        team = Mesh(mesh.devices.reshape(dp, 2, ctx // (2 * KV_HEADS), KV_HEADS), EVERY)
        run = on_device
    placed = (
        P("dp", ring, None, None),
        P("dp", None, None),
        P("dp"),
        P(every, None),
        P(every, None),
        P(every),
        P(every, None, None),
        P("dp", ring, None, None),
    )
    return jax.shard_map(
        run,
        mesh=team,
        in_specs=placed,
        out_specs=(
            P("dp", ring, None, None),
            P("dp", ring, None, None),
            P(every, None),
            P(every, None),
            P(every),
            P(every, None, None),
        ),
        check_vma=False,
    )
```

```python
import jax
import jax.numpy as jnp
import numpy as np
from jax import lax
from jax.experimental import pallas as pl
from jax.experimental.pallas import tpu as pltpu
from jax.sharding import Mesh
from jax.sharding import PartitionSpec as P

FF = 4608
HEADS = 16
KV_HEADS = 8
HEAD_DIM = 64
GROUP = HEADS // KV_HEADS
QKV_ROWS = 2048

EPS = 1e-05
ROPE_BASE = 1000000.0
MASKED = -1e30
BF = jnp.bfloat16
F32 = jnp.float32


def root_mean(values):
    return lax.rsqrt(jnp.mean(values * values, axis=-1, keepdims=True) + EPS)


def rotate(values, cosine, sine):
    width = values.shape[-1] // 2
    first = values[..., :width]
    second = values[..., width:]
    return jnp.concatenate(
        [first * cosine - second * sine, second * cosine + first * sine], axis=-1
    )


def tables(positions):
    width = HEAD_DIM // 2
    freq = ROPE_BASE ** (-jnp.arange(width, dtype=F32) * 2.0 / HEAD_DIM)
    angle = positions.astype(F32)[..., None] * freq
    return (jnp.cos(angle), jnp.sin(angle))


def prepare(query_raw, key_raw, query_gain, key_gain, cosine, sine):
    query_norm = query_raw * root_mean(query_raw) * query_gain
    key_norm = key_raw * root_mean(key_raw) * key_gain
    return (
        rotate(query_norm, cosine[:, None], sine[:, None]),
        rotate(key_norm, cosine, sine),
    )


def norm_back(grad, normed, scale_rows, gain):
    weighted = grad * gain
    inner = jnp.mean(weighted * normed, axis=-1, keepdims=True)
    return (scale_rows * (weighted - normed * inner), jnp.sum(grad * normed, axis=0))


def dot(a, b, ca, cb):
    return lax.dot_general(a, b, (((ca,), (cb,)), ((), ())), preferred_element_type=F32)


TEAM = ("dp", "s", "q")
EVERY = ("dp", "s", "q", "g")


def spread(local, block_len):
    mine = lax.all_to_all(local, "s", 0, 0, tiled=True)
    return lax.all_gather(mine, "g", axis=0, tiled=False)


def on_device(tokens, segments, lengths, attn_in, attn_out, gains, ffn_weights, cotangent):
    batches, block_len, halves, width = tokens.shape
    seq = lax.axis_index("s")
    quarter = lax.axis_index("q")
    head = lax.axis_index("g")
    quarters = lax.axis_size("q")
    heads = lax.axis_size("g")
    ctx_count = 2 * quarters * heads
    scale = HEAD_DIM ** (-0.5)
    weight_in = lax.all_gather(attn_in, EVERY, axis=0, tiled=True)
    weight_out = lax.all_gather(attn_out, EVERY, axis=0, tiled=True)
    gain_all = lax.all_gather(gains, EVERY, axis=0, tiled=True).astype(F32)
    attn_gain = gain_all[:width]
    ffn_gain = gain_all[width : 2 * width]
    query_gain = gain_all[2 * width : 2 * width + HEAD_DIM]
    key_gain = gain_all[2 * width + HEAD_DIM :]
    head_rows = (GROUP + 2) * HEAD_DIM
    out_rows = GROUP * HEAD_DIM
    weight_head = lax.dynamic_slice_in_dim(weight_in, head * head_rows, head_rows, 0)
    weight_mix = lax.dynamic_slice_in_dim(weight_out, head * out_rows, out_rows, 0)

    inputs = spread(tokens, block_len)
    count = inputs.size // width
    inputs = inputs.reshape(count, width).astype(F32)
    cot = spread(cotangent, block_len).reshape(count, width).astype(F32)

    def places(which):
        owner_g = jnp.arange(heads, dtype=jnp.int32)[:, None, None, None]
        owner_s = jnp.arange(2, dtype=jnp.int32)[None, :, None, None]
        row = jnp.arange(block_len, dtype=jnp.int32)[None, None, :, None]
        half = jnp.arange(2, dtype=jnp.int32)[None, None, None, :]
        owner = owner_s * (quarters * heads) + which * heads + owner_g
        block = jnp.where(half == 0, owner, 2 * ctx_count - 1 - owner)
        return (
            (block * block_len + row).reshape(count),
            jnp.broadcast_to((owner * block_len + row) * 2 + half, (heads, 2, block_len, 2)).reshape(count),
        )

    docs = lax.dynamic_index_in_dim(segments, seq, 0, False).reshape(-1)
    length = lax.dynamic_index_in_dim(lengths, seq, 0, False)
    place, slot = places(quarter)
    key_place, key_slot = jax.vmap(places)(jnp.arange(quarters, dtype=jnp.int32))
    key_place = key_place.reshape(-1)
    query_doc = docs[slot]
    key_doc = docs[key_slot.reshape(-1)]
    causal = key_place[None, :] <= place[:, None]
    live = (key_place[None, :] < length) | (key_place[None, :] == place[:, None])
    mask = causal & live & (query_doc[:, None] == key_doc[None, :])
    valid = (place < length).astype(F32)[:, None]

    first_scale = root_mean(inputs)
    first_normed = inputs * first_scale
    first = (first_normed * attn_gain).astype(BF)
    projected = dot(first, weight_head, 1, 1).reshape(count, GROUP + 2, HEAD_DIM)
    cosine, sine = tables(place)

    def prepare_here(query_raw, key_raw, gain_query, gain_key):
        return prepare(query_raw, key_raw, gain_query, gain_key, cosine, sine)

    (query_rot, key_rot), prepare_pull = jax.vjp(
        prepare_here, projected[:, :GROUP], projected[:, GROUP], query_gain, key_gain
    )
    queries = query_rot.astype(BF)
    pair = jnp.stack([key_rot.astype(BF), projected[:, GROUP + 1].astype(BF)])
    pair = lax.all_gather(pair, "q", axis=1, tiled=True)
    keys, values = pair[0], pair[1]

    scores = jnp.einsum("qjd,kd->jqk", queries, keys, preferred_element_type=F32) * scale
    scores = jnp.where(mask[None], scores, MASKED)
    peak = jnp.max(scores, axis=-1, keepdims=True)
    expo = jnp.where(mask[None], jnp.exp(scores - peak), 0.0)
    weights = expo / jnp.sum(expo, axis=-1, keepdims=True)
    attended = jnp.einsum("jqk,kd->qjd", weights.astype(BF), values, preferred_element_type=F32)
    mixed_here = attended.astype(BF).reshape(count, out_rows)
    mixed = lax.all_gather(mixed_here, "g", axis=1, tiled=True)
    state = inputs + dot(mixed, weight_out, 1, 0)
    second_scale = root_mean(state)
    second_normed = state * second_scale
    second = (second_normed * ffn_gain).astype(BF)
    grad_out = cot * valid
    grad_low = grad_out.astype(BF)

    units = lax.all_gather(ffn_weights, TEAM, axis=0, tiled=True)
    unit_gate, unit_up, unit_down = units[:, 0], units[:, 1], units[:, 2]
    gate = dot(second, unit_gate, 1, 1)
    upward = dot(second, unit_up, 1, 1)
    sigmoid = jax.nn.sigmoid(gate)
    hidden = (gate * sigmoid * upward).astype(BF)
    d_hidden = dot(grad_low, unit_down, 1, 1)
    d_gate = (d_hidden * upward * sigmoid * (1.0 + gate * (1.0 - sigmoid))).astype(BF)
    d_up = (d_hidden * gate * sigmoid).astype(BF)
    d_second = dot(d_gate, unit_gate, 1, 0) + dot(d_up, unit_up, 1, 0)
    own = count // heads

    def gathered(values):
        return lax.psum_scatter(values.astype(BF), "g", scatter_dimension=0, tiled=True).astype(F32)

    def own_rows(values):
        return lax.dynamic_slice_in_dim(values, head * own, own, 0)

    def home(values):
        back = values.reshape(2, block_len, halves, width)
        return lax.all_to_all(back, "s", 0, 0, tiled=True)

    ffn_sum = gathered(dot(hidden, unit_down, 1, 0))
    block_out = home((own_rows(state) + ffn_sum).astype(BF))
    ffn_grad = lax.psum_scatter(
        jnp.stack([dot(d_gate, second, 0, 0), dot(d_up, second, 0, 0), dot(hidden, grad_low, 0, 0)], axis=1),
        TEAM,
        scatter_dimension=0,
        tiled=True,
    )
    norm_grad, ffn_gain_grad = norm_back(
        gathered(d_second), own_rows(second_normed), own_rows(second_scale), ffn_gain
    )
    state_grad = own_rows(grad_out) + norm_grad
    attended_grad = lax.all_gather(state_grad.astype(BF), "g", axis=0, tiled=True)
    mixed_grad = dot(attended_grad, weight_mix, 1, 1).astype(BF)
    out_term = dot(mixed_here, attended_grad, 0, 0)
    mixed_grad = mixed_grad.reshape(count, GROUP, HEAD_DIM)
    delta = jnp.sum(mixed_grad.astype(F32) * attended, axis=-1).T[:, :, None]
    pulled = jnp.einsum("qjd,kd->jqk", mixed_grad, values, preferred_element_type=F32)
    score_grad = (weights * (pulled - delta)).astype(BF)
    query_grad = jnp.einsum("jqk,kd->qjd", score_grad, keys, preferred_element_type=F32) * scale
    key_grad = jnp.einsum("jqk,qjd->kd", score_grad, queries, preferred_element_type=F32) * scale
    value_grad = jnp.einsum("jqk,qjd->kd", weights.astype(BF), mixed_grad, preferred_element_type=F32)
    if quarters > 1:
        key_grad = lax.psum_scatter(key_grad, "q", scatter_dimension=0, tiled=True)
        value_grad = lax.psum_scatter(value_grad, "q", scatter_dimension=0, tiled=True)
    query_raw_grad, key_raw_grad, query_gain_grad, key_gain_grad = prepare_pull((query_grad, key_grad))
    projected_grad = jnp.concatenate(
        [query_raw_grad.reshape(count, out_rows), key_raw_grad, value_grad], axis=1
    ).astype(BF)
    first_grad = gathered(dot(projected_grad, weight_head, 1, 0))
    in_term = dot(projected_grad, first, 0, 0)
    input_norm_grad, attn_gain_grad = norm_back(
        first_grad, own_rows(first_normed), own_rows(first_scale), attn_gain
    )
    tokens_grad = home(state_grad + input_norm_grad)
    gain_term = jnp.concatenate([attn_gain_grad, ffn_gain_grad, query_gain_grad, key_gain_grad])

    def placed(term, rows):
        whole = jnp.zeros((rows, width), F32)
        return lax.dynamic_update_slice_in_dim(whole, term, head * term.shape[0], 0)

    return (
        block_out,
        tokens_grad,
        lax.psum_scatter(placed(in_term, QKV_ROWS), EVERY, scatter_dimension=0, tiled=True),
        lax.psum_scatter(placed(out_term, HEADS * HEAD_DIM), EVERY, scatter_dimension=0, tiled=True),
        lax.psum_scatter(gain_term, EVERY, scatter_dimension=0, tiled=True),
        ffn_grad,
    )


LANES = 128
HALF_LANES = 64


def _nt(a, b):
    return lax.dot_general(a, b, (((1,), (1,)), ((), ())), preferred_element_type=F32)


def _nn(a, b):
    return lax.dot_general(a, b, (((1,), (0,)), ((), ())), preferred_element_type=F32)


def _tn(a, b):
    return lax.dot_general(a, b, (((0,), (0,)), ((), ())), preferred_element_type=F32)


MESH = pl.DeviceIdType.MESH
COPIES = 400


class Wires:
    def __init__(self, sems):
        self.sems = sems
        self.used = 0
        self.pending = []

    def sem(self):
        self.used += 1
        return self.sems.at[self.used - 1]

    def send(self, src, dst, to, arrives):
        copy = pltpu.make_async_remote_copy(
            src_ref=src, dst_ref=dst, send_sem=self.sem(), recv_sem=arrives,
            device_id=to, device_id_type=MESH,
        )
        copy.start()
        self.pending.append(copy)
        return copy

    def local(self, src, dst, arrives):
        copy = pltpu.make_async_copy(src, dst, arrives)
        copy.start()
        return copy

    def arrived(self, ref, sem):
        pltpu.make_async_copy(ref, ref, sem).wait()

    def finish(self, copies=None):
        copies = list(self.pending if copies is None else copies)
        for copy in copies:
            copy.wait_send()
        done = {id(copy) for copy in copies}
        self.pending = [copy for copy in self.pending if id(copy) not in done]


def block_kernel(
    tok, cot, win, wout, gain, wffn, doc_col, doc_row, length, cos_t, sin_t,
    o_block, o_tokens, o_in, o_out, o_gain, o_ffn,
    x, rel_t, rel_c, w2, wall, wfa, wfb, gb, grow, first2, raw, po,
    q0, q1, kk, vv, prob, att, mxs, mix, sec2, dy2, acta, actb, asend,
    dsb, osb, dsr, osr, rsz, gr, gs, gt, dstate, dmb, daf, dmix,
    dkk, dvv, dqq, dpj, dpx, dfb, dfr, igs, agr, agz, agt, agh, ago,
    bos, obs, bor, tgs, tgr, gg, ggq, gsum, ggt, sems,
):
    dp = lax.axis_index("dp")
    c = lax.axis_index("ctx")
    zh = lax.div(c, 8)
    g = lax.rem(c, 8)
    j = lax.div(g, 2)
    k = lax.rem(c, 2)
    chips = (j, j + 1 - 2 * lax.rem(j, 2), j + 2 - 4 * lax.div(j, 2), 3 - j)
    cores = (k, 1 - k)

    def quad(d, e):
        return (dp, zh * 8 + 2 * chips[d] + cores[e])

    sib = quad(0, 1)
    czp = lax.rem(c + 8, 16)
    zp = (dp, lax.rem(c + 8, 16))
    zps = (dp, 8 * (1 - zh) + 2 * j + 1 - k)
    yp = (1 - dp, c)
    diag = (1 - dp, lax.rem(c + 8, 16))
    team = 2 * dp + zh
    team_y = 2 * (1 - dp) + zh
    team_z = 2 * dp + 1 - zh
    team_d = 3 - team
    w = Wires(sems)
    others = [(d, e) for d in range(4) for e in range(2) if (d, e) != (0, 0)]

    zl, xx = lax.div(j, 2), lax.rem(j, 2)
    keeper = (xx, 8 * k + 4 * dp + 2 * zh + zl)
    owner_of = (zl, 8 * xx + 4 * k + 2 * dp + zh)
    alone = jnp.logical_and(keeper[0] == dp, keeper[1] == c)
    apart = jnp.logical_not(alone)

    barrier = pltpu.get_barrier_semaphore()
    peers = [quad(d, e) for d, e in others] + [zp, zps, yp, diag]
    for peer in peers:
        pl.semaphore_signal(barrier, inc=1, device_id=peer, device_id_type=MESH)

    @pl.when(apart)
    def _():
        pl.semaphore_signal(barrier, inc=1, device_id=keeper, device_id_type=MESH)
        pl.semaphore_signal(barrier, inc=1, device_id=owner_of, device_id_type=MESH)
        pl.semaphore_wait(barrier, len(peers) + 2)

    @pl.when(alone)
    def _():
        pl.semaphore_wait(barrier, len(peers))

    def many(*shape):
        return [many(*shape[1:]) for _ in range(shape[0])] if shape else w.sem()

    def piece(chip):
        return chip + k * (3 - 2 * chip)

    def row_block(owner, half):
        return owner + half * (15 - 2 * owner)

    my_rows = pl.multiple_of(512 * k, 512)
    other_rows = pl.multiple_of(512 * (1 - k), 512)
    own_head, sib_head = pl.ds(0, 256), pl.ds(256, 256)
    mine = piece(j)
    steps = {}

    def step(name):
        def keep(body):
            steps[name] = body
            return body
        return keep

    def rows_of(buf, offset):
        def at(half, start, count):
            return buf.at[pl.ds(pl.multiple_of(offset * half + start, 32), count)]
        return at

    def rows_steps(name, source, relay, at):
        s_rel, s_here, s_z, s_d = many(2), w.sem(), many(2), w.sem()
        passed = []

        def scatter(src, owner, e, which):
            half = cores[e]
            dst = at(half, pl.multiple_of(row_block(owner, half) * 32, 32), 32)
            w.send(src, dst, quad(2, e), s_z[which])
            w.send(src, dst, quad(1, e), s_here)
            if e == 0:
                w.local(src, dst, s_here)
            else:
                w.send(src, dst, sib, s_here)

        def halves(e):
            @step(f"{name}_out{e}")
            def _():
                w.send(source.at[1 - zh, cores[e]], relay.at[cores[e]], zp, s_rel[e])

            @step(f"{name}_own{e}")
            def _():
                scatter(source.at[zh, cores[e]], c, e, 0)

            @step(f"{name}_rel{e}")
            def _():
                w.arrived(relay.at[cores[e]], s_rel[e])
                scatter(relay.at[cores[e]], czp, e, 1)

            @step(f"{name}_fwd{e}")
            def _():
                first = (zh if e == 0 else 1 - zh) * 8 + 2 * chips[2]
                rows = at(k, pl.multiple_of(32 * (first + k * (14 - 2 * first)), 64), 64)
                w.arrived(rows, s_z[e])
                passed.append(w.send(rows, rows, quad(1, 0), s_d))

        halves(0)
        halves(1)
        return s_here, s_d, passed

    s_x, s_xd, _ = rows_steps("tok", tok, rel_t, rows_of(x, 0))
    s_c, s_cd, cot_passed = rows_steps("cot", cot, rel_c, rows_of(dy2, 512))

    def head_rows(t):
        return w2.at[pl.ds(pl.multiple_of(64 * t, 64), 64)]

    def exchange(name, src, at, keep):
        sem = many(4)

        @step(f"{name}_start")
        def _():
            w.send(src, at(team), zp, sem[1])
            w.send(src, at(team), yp, sem[0])
            if keep:
                w.local(src, at(team), sem[3])

        @step(f"{name}_pass")
        def _():
            w.arrived(at(team_z), sem[1])
            w.send(at(team_z), at(team_z), yp, sem[2])

        def end():
            w.arrived(at(team_y), sem[0])
            w.arrived(at(team_d), sem[2])
            if keep:
                w.arrived(at(team), sem[3])

        return end

    s_move, s_w2, s_gq, s_wq, s_ws = w.sem(), w.sem(), w.sem(), many(3), w.sem()
    gains_end = exchange("gain", gain, lambda t: gb.at[t, g], True)
    heads_end = exchange("win", head_rows(team), head_rows, False)
    wout_end = exchange("wout", wout, lambda t: wall.at[t, j, k], True)
    move = pltpu.make_async_remote_copy(
        src_ref=win, dst_ref=head_rows(lax.rem(g, 4)), send_sem=w.sem(), recv_sem=s_move,
        device_id=keeper, device_id_type=MESH,
    )

    @step("move")
    def _():
        pl.when(apart)(move.start)
        pl.when(alone)(lambda: pltpu.make_async_copy(win, head_rows(team), s_move).start())

    @step("moved")
    def _():
        w.arrived(head_rows(team), s_move)

    @step("gain_end")
    def _():
        gains_end()
        for d, e in others:
            w.send(gb.at[:, g], gb.at[:, g], quad(d, e), s_gq)

    @step("win_end")
    def _():
        heads_end()
        w.send(w2.at[own_head], w2.at[sib_head], sib, s_w2)

    @step("wout_end")
    def _():
        wout_end()
        for d in (2, 1):
            w.send(wall.at[:, j, k], wall.at[:, j, k], quad(d, 0), s_wq[d - 1])

    @step("wout_fwd")
    def _():
        w.arrived(wall.at[:, chips[2], k], s_wq[1])
        w.send(wall.at[:, chips[2], k], wall.at[:, chips[2], k], quad(1, 0), s_wq[2])

    @step("wout_sib")
    def _():
        for d in (1, 3):
            w.arrived(wall.at[:, j, k], s_wq[d - 1])
        w.send(wall.at[:, :, k], wall.at[:, :, k], sib, s_ws)

    parts = ((0, 80, wfa, acta, 320, 384), (80, 64, wfb, actb, 256, 256))
    s_f = many(2, 2, 4, 3)
    held = [[], []]

    def source(part, kind):
        return wffn.at[kind, pl.ds(parts[part][0], parts[part][1])]

    def unit(part, kind, far, slot):
        _, rows, buf, _, _, second = parts[part]
        return buf.at[kind, pl.ds(second * far + rows * slot, rows)]

    def unit_steps(part):
        sem = s_f[part]

        @step(f"u{part}_own")
        def _():
            for kind in range(3):
                w.local(source(part, kind), unit(part, kind, 0, 0), sem[0][0][kind])
                w.send(source(part, kind), unit(part, kind, 1, 0), sib, sem[1][0][kind])
                if part == 0:
                    wfa[kind, 320:384, :] = jnp.zeros((64, 1024), BF)

        @step(f"u{part}_y")
        def _():
            for kind in range(3):
                w.send(source(part, kind), unit(part, kind, 0, 1), yp, sem[0][1][kind])

        def from_z(kind):
            @step(f"u{part}_z{kind}")
            def _():
                w.send(source(part, kind), unit(part, kind, 0, 2), zp, sem[0][2][kind])

            @step(f"u{part}_f{kind}")
            def _():
                here = unit(part, kind, 0, 2)
                w.arrived(here, sem[0][2][kind])
                held[part].append(w.send(here, unit(part, kind, 0, 3), yp, sem[0][3][kind]))
                held[part].append(w.send(here, unit(part, kind, 1, 2), sib, sem[1][2][kind]))

        def ready(slot):
            @step(f"u{part}_s{slot}")
            def _():
                for kind in range(3):
                    here = unit(part, kind, 0, slot)
                    w.arrived(here, sem[0][slot][kind])
                    held[part].append(w.send(here, unit(part, kind, 1, slot), sib, sem[1][slot][kind]))

        for kind in range(3):
            from_z(kind)
        ready(1)
        ready(3)

        @step(f"u{part}_all")
        def _():
            for kind in range(3):
                w.arrived(unit(part, kind, 0, 0), sem[0][0][kind])
                for slot in range(4):
                    w.arrived(unit(part, kind, 1, slot), sem[1][slot][kind])

    unit_steps(0)
    unit_steps(1)

    lane = lax.broadcasted_iota(jnp.int32, (1, LANES), 1)
    low_row = lane < HALF_LANES

    @step("gains")
    def _():
        w.arrived(gb.at[:, pl.ds(0, 7)], s_gq)
        chunks = [jnp.zeros((1, LANES), F32) for _ in range(18)]
        for i in range(32):
            row = gb[i // 8, i % 8, 0:1, :]
            place, shift = divmod(68 * i, LANES)
            moved = pltpu.roll(row, shift, 1) if shift else row
            chunks[place] = chunks[place] + jnp.where(lane >= shift, moved, 0.0)
            if shift + 68 > LANES:
                chunks[place + 1] = chunks[place + 1] + jnp.where(lane < shift, moved, 0.0)
        for n in range(8):
            grow[0:1, LANES * n : LANES * (n + 1)] = chunks[n]
            grow[1:2, LANES * n : LANES * (n + 1)] = chunks[8 + n]
        flipped = pltpu.roll(chunks[16], HALF_LANES, 1)
        grow[2:3, 0:LANES] = jnp.where(low_row, chunks[16], flipped)
        grow[2:3, LANES : 2 * LANES] = jnp.where(low_row, flipped, chunks[16])

    def attn_gain():
        return grow[0:1, :]

    def ffn_gain():
        return grow[1:2, :]

    def query_gain():
        return grow[2:3, 0:LANES]

    def key_gain():
        return grow[2:3, LANES : 2 * LANES]

    s_raw, s_first = w.sem(), w.sem()

    @step("project")
    def _():
        w.arrived(x.at[pl.ds(0, 256)], s_x)
        w.arrived(x.at[pl.ds(0, 128)], s_xd)
        w.arrived(w2.at[sib_head], s_w2)
        weight = attn_gain()

        def rows_of_256(t, carry):
            rows = pl.multiple_of(t * 256, 256)
            values = x[pl.ds(rows, 256), :].astype(F32)
            scale = lax.rsqrt(jnp.mean(values * values, axis=1, keepdims=True) + EPS)
            first = (values * scale * weight).astype(BF)
            here = pl.multiple_of(my_rows + rows, 256)
            first2[pl.ds(here, 256), :] = first
            po[pl.ds(rows, 256), :] = _nt(first, w2[sib_head, :])
            raw[pl.ds(here, 256), :] = _nt(first, w2[own_head, :])
            return carry

        lax.fori_loop(0, 2, rows_of_256, 0)
        w.send(po, raw.at[pl.ds(my_rows, 512)], sib, s_raw)

    @step("first_sib")
    def _():
        w.send(first2.at[pl.ds(my_rows, 512)], first2.at[pl.ds(my_rows, 512)], sib, s_first)

    low = lax.broadcasted_iota(jnp.int32, (256, LANES), 1) < HALF_LANES
    quarter = lax.rem(lax.broadcasted_iota(jnp.int32, (256, LANES), 1), HALF_LANES) < 32

    def swap(v):
        return jnp.where(quarter, pltpu.roll(v, 96, 1), pltpu.roll(v, 32, 1))

    def head_sum(v):
        first = jnp.sum(jnp.where(low, v, 0.0), axis=1, keepdims=True)
        second = jnp.sum(jnp.where(low, 0.0, v), axis=1, keepdims=True)
        return jnp.where(low, first, second)

    def inverse_root(v):
        return lax.rsqrt(head_sum(v * v) * (1.0 / HEAD_DIM) + EPS)

    @step("rotate")
    def _():
        w.arrived(raw.at[pl.ds(0, 512)], s_raw)
        query_weight, key_weight = query_gain(), key_gain()

        def rotate_rows(t, carry):
            rows = pl.ds(pl.multiple_of(t * 256, 256), 256)
            cosine, sine = cos_t[rows, :], sin_t[rows, :]
            query = raw[rows, 0:LANES]
            both = raw[rows, LANES : 2 * LANES]
            query = query * inverse_root(query) * query_weight
            query = (query * cosine + swap(query) * sine) * (HEAD_DIM**-0.5)
            q0[rows, :] = jnp.where(low, query, 0.0).astype(BF)
            q1[rows, :] = jnp.where(low, 0.0, query).astype(BF)
            key = both * inverse_root(both) * key_weight
            key = key * cosine + swap(key) * sine
            kk[rows, :] = jnp.where(low, key, pltpu.roll(key, HALF_LANES, 1)).astype(BF)
            vv[rows, :] = jnp.where(low, pltpu.roll(both, HALF_LANES, 1), both).astype(BF)
            return carry

        lax.fori_loop(0, 4, rotate_rows, 0)

    s_mix, s_md, s_mz = w.sem(), w.sem(), many(2)
    head_lanes = pl.ds(pl.multiple_of(LANES * g, LANES), LANES)
    z_lanes = pl.ds(pl.multiple_of(256 * chips[2], 256), 256)
    late = []

    def forward_tile(t):
        @step(f"at{t}")
        def _():
            lo, n = 256 * t, 256 * (t + 1)
            place = lax.broadcasted_iota(jnp.int32, (256, n), 0) + lo
            key_place = lax.broadcasted_iota(jnp.int32, (256, n), 1)
            same = doc_col[lo : lo + 256, :] == doc_row[0:1, 0:n]
            mask = (same & (key_place <= place)) | (key_place == place)
            outs = []
            for h, q in enumerate((q0, q1)):
                scores = jnp.where(mask, _nt(q[lo : lo + 256, :], kk[0:n, :]), MASKED)
                peak = jnp.max(scores, axis=1, keepdims=True)
                expo = jnp.exp(scores - peak)
                weights = (expo * (1.0 / jnp.sum(expo, axis=1, keepdims=True))).astype(BF)
                prob[h, lo : lo + 256, 0:n] = weights
                outs.append(_nn(weights, vv[0:n, :]))
            attended = jnp.where(low, outs[0], outs[1])
            att[lo : lo + 256, :] = attended
            mxs[lo : lo + 256, :] = attended.astype(BF)
            half = t // 2
            dst = mix.at[pl.ds(256 * (t % 2), 256), head_lanes]
            src = mxs.at[pl.ds(lo, 256)]
            w.send(src, dst, (dp, zh * 8 + 2 * chips[2] + half), s_mz[t % 2])
            w.send(src, dst, (dp, zh * 8 + 2 * chips[1] + half), s_mix)
            away = pltpu.make_async_remote_copy(
                src_ref=src, dst_ref=dst, send_sem=w.sem(), recv_sem=s_mix, device_id=sib, device_id_type=MESH
            )
            pl.when(k == half)(lambda: pltpu.make_async_copy(src, dst, s_mix).start())
            pl.when(k != half)(away.start)
            late.append((half, away))

    def pass_mixed(r):
        @step(f"mix_fwd{r}")
        def _():
            part = mix.at[pl.ds(256 * r, 256), z_lanes]
            w.arrived(part, s_mz[r])
            w.send(part, part, quad(1, 0), s_md)

    for t in range(4):
        forward_tile(t)
    pass_mixed(0)
    pass_mixed(1)

    s_dy, s_sec = w.sem(), w.sem()

    @step("dy")
    def _():
        w.arrived(dy2.at[pl.ds(0, 256)], s_c)
        w.arrived(dy2.at[pl.ds(0, 128)], s_cd)
        w.finish(cot_passed)
        limit = length[0:1, 0:1]

        def drop_rows(t, carry):
            rows = pl.ds(pl.multiple_of(my_rows + t * 128, 128), 128)
            place = lax.broadcasted_iota(jnp.int32, (128, 1), 0) + (my_rows + t * 128)
            kept = (place < limit).astype(F32)
            dy2[rows, :] = (dy2[rows, :].astype(F32) * kept).astype(BF)
            return carry

        lax.fori_loop(0, 4, drop_rows, 0)
        w.send(dy2.at[pl.ds(my_rows, 512)], dy2.at[pl.ds(my_rows, 512)], sib, s_dy)

    def attended_rows(rows):
        total = None
        for n in range(4):
            term = _nn(mix[rows, 256 * n : 256 * (n + 1)], wall[n].reshape(256, 1024))
            total = term if total is None else total + term
        return total

    @step("second")
    def _():
        w.arrived(wall.at[:, :, 0], s_ws)
        w.arrived(mix.at[pl.ds(0, 256)], s_mix)
        w.arrived(mix.at[:, pl.ds(0, 256)], s_md)
        weight = ffn_gain()

        def project_out(t, carry):
            rows = pl.ds(pl.multiple_of(t * 256, 256), 256)
            state = x[rows, :].astype(F32) + attended_rows(rows)
            scale = lax.rsqrt(jnp.mean(state * state, axis=1, keepdims=True) + EPS)
            here = pl.ds(pl.multiple_of(my_rows + t * 256, 256), 256)
            sec2[here, :] = (state * scale * weight).astype(BF)
            return carry

        lax.fori_loop(0, 2, project_out, 0)
        w.send(sec2.at[pl.ds(my_rows, 512)], sec2.at[pl.ds(my_rows, 512)], sib, s_sec)

    class Sum:
        def __init__(self, name, buf, into, which):
            self.buf, self.into, self.which = buf, into, which
            self.sems = many(3, 2)
            for t in range(2):
                if name == "os":
                    step(f"{name}_x{t}")(lambda t=t: self.over_x(t))
                step(f"{name}_z{t}")(lambda t=t: self.over_z(t))

        def rows(self, d, t):
            return pl.ds(pl.multiple_of(256 * t + 64 * piece(chips[d]), 64), 64)

        def over_x(self, t):
            for d, slot in ((3, 1), (1, 0)):
                w.send(self.buf.at[self.rows(d, t)], self.into.at[slot, t], quad(1, 0), self.sems[slot][t])

        def over_z(self, t):
            w.arrived(self.into.at[1, t], self.sems[1][t])
            total = self.buf[self.rows(2, t), :].astype(F32) + self.into[1, t].astype(F32)
            rsz[self.which, t] = total.astype(BF)
            w.send(rsz.at[self.which, t], self.into.at[2, t], quad(2, 0), self.sems[2][t])

        def result(self, t):
            total = self.buf[self.rows(0, t), :].astype(F32)
            for slot in (0, 2):
                w.arrived(self.into.at[slot, t], self.sems[slot][t])
                total = total + self.into[slot, t].astype(F32)
            return total

    sum_ds, sum_os, sum_df = Sum("ds", dsb, dsr, 0), Sum("os", osb, osr, 1), Sum("df", dfb, dfr, 2)

    s_act, s_gr, s_gt = many(2), many(2, 2), many(2)
    acted = []

    def part_steps(part):
        start, rows_kept, buf, acts, count, second = parts[part]
        span = pl.ds(start, rows_kept)

        def feed_forward(t):
            @step(f"ff{part}{t}")
            def _():
                if part == 1 and t == 0:
                    w.finish(acted)
                rows = pl.ds(pl.multiple_of(my_rows + 256 * t, 256), 256)
                here = pl.ds(256 * t, 256)
                gate = _nt(sec2[rows, :], buf[0])
                up = _nt(sec2[rows, :], buf[1])
                d_hidden = _nt(dy2[rows, :], buf[2])
                sigmoid = 1.0 / (1.0 + jnp.exp(-gate))
                silu = gate * sigmoid
                d_gate = (d_hidden * up * (sigmoid + silu * (1.0 - sigmoid))).astype(BF)
                d_up = (d_hidden * silu).astype(BF)
                hidden = (silu * up).astype(BF)
                for n, value in enumerate((d_gate, d_up, hidden)):
                    acts[n, rows, :] = value[:, 0:second]
                    asend[n, here, 0:count] = value[:, second : second + count]
                lanes = pl.ds(0, second)
                acted.append(w.send(asend.at[:, here, lanes], acts.at[:, rows], sib, s_act[part]))
                d_second = _nn(d_gate, buf[0]) + _nn(d_up, buf[1])
                result = _nn(hidden, buf[2])
                if part == 1:
                    d_second = d_second + dsb[here, :].astype(F32)
                    result = result + osb[here, :].astype(F32)
                dsb[here, :] = d_second.astype(BF)
                osb[here, :] = result.astype(BF)
                if part == 1:
                    sum_ds.over_x(t)

        @step(f"wg{part}_in")
        def _():
            w.finish(held[part])
            w.arrived(acts.at[:, pl.ds(0, 512)], s_act[part])
            if part == 0:
                w.arrived(sec2.at[pl.ds(0, 512)], s_sec)
                w.arrived(dy2.at[pl.ds(0, 512)], s_dy)

        def weight_grads(kind):
            @step(f"wg{part}{kind}")
            def _():
                right = dy2 if kind == 2 else sec2

                def columns(n, carry):
                    cols = pl.ds(pl.multiple_of(n * 512, 512), 512)
                    buf[kind, 0:count, cols] = _tn(acts[kind], right[:, cols])[0:count, :].astype(BF)
                    return carry

                lax.fori_loop(0, 2, columns, 0)

        def send_grads(slot, to_slot):
            @step(f"gr{part}_y{to_slot}")
            def _():
                rows = buf.at[:, pl.ds(rows_kept * slot, rows_kept)]
                w.send(rows, gr.at[to_slot, :, span], yp, s_gr[to_slot][part])

        @step(f"gr{part}_z")
        def _():
            w.arrived(gr.at[1, :, span], s_gr[1][part])
            for kind in range(3):
                gs[kind, span, :] = (
                    buf[kind, 2 * rows_kept : 3 * rows_kept, :].astype(F32) + gr[1, kind, span, :].astype(F32)
                ).astype(BF)
            w.send(gs.at[:, span], gt.at[:, span], zp, s_gt[part])

        @step(f"gr{part}_end")
        def _():
            w.arrived(gr.at[0, :, span], s_gr[0][part])
            w.arrived(gt.at[:, span], s_gt[part])
            for kind in range(3):
                o_ffn[kind, span, :] = (
                    buf[kind, 0:rows_kept, :].astype(F32)
                    + gr[0, kind, span, :].astype(F32) + gt[kind, span, :].astype(F32)
                )

        feed_forward(0)
        feed_forward(1)
        for kind in range(3):
            weight_grads(kind)
        send_grads(3, 1)
        send_grads(1, 0)

    part_steps(0)
    part_steps(1)

    s_dm, s_da, s_das = w.sem(), many(3), w.sem()
    terms = {"ffn": jnp.zeros((1, 1024), F32), "attn": jnp.zeros((1, 1024), F32)}

    def state_steps(t):
        @step(f"st{t}")
        def _():
            start = 256 * t + 64 * mine
            rows = pl.ds(pl.multiple_of(start, 64), 64)
            state = x[rows, :].astype(F32) + attended_rows(rows)
            bos[t] = state
            scale = lax.rsqrt(jnp.mean(state * state, axis=1, keepdims=True) + EPS)
            normed = state * scale
            total = sum_ds.result(t)
            terms["ffn"] = terms["ffn"] + jnp.sum(total * normed, axis=0, keepdims=True)
            weighted = total * ffn_gain()
            inner = jnp.mean(weighted * normed, axis=1, keepdims=True)
            grad = dy2[pl.ds(pl.multiple_of(my_rows + start, 64), 64), :].astype(F32) + scale * (weighted - normed * inner)
            dstate[t] = grad
            low_grad = grad.astype(BF)
            daf[k, t, mine] = low_grad
            for n in range(4):
                dmb[t, :, 256 * n : 256 * (n + 1)] = _nt(low_grad, wall[n].reshape(256, 1024)).astype(BF)
            for d, e in others:
                lanes = pl.ds(pl.multiple_of(LANES * (2 * chips[d] + cores[e]), LANES), LANES)
                w.send(dmb.at[t, :, lanes], dmix.at[k, t, mine], quad(d, e), s_dm)
            w.local(dmb.at[t, :, head_lanes], dmix.at[k, t, mine], s_dm)

    state_steps(0)
    state_steps(1)

    @step("da_out")
    def _():
        for d in (2, 1):
            w.send(daf.at[k, :, mine], daf.at[k, :, mine], quad(d, 0), s_da[d - 1])

    @step("da_fwd")
    def _():
        far = piece(chips[2])
        w.arrived(daf.at[k, :, far], s_da[1])
        w.send(daf.at[k, :, far], daf.at[k, :, far], quad(1, 0), s_da[2])

    @step("da_sib")
    def _():
        for d in (1, 3):
            w.arrived(daf.at[k, :, mine], s_da[d - 1])
        w.send(daf.at[k], daf.at[k], sib, s_das)

    home = zh + k * (1 - 2 * zh)

    def send_home(buf, into, sem):
        w.send(buf.at[1 - home, 0], into.at[zh, k], zp, sem)
        w.send(buf.at[1 - home, 1], into.at[zh, k], zps, sem)
        w.send(buf.at[home, 1], into.at[zh, k], sib, sem)
        w.local(buf.at[home, 0], into.at[zh, k], sem)

    s_bo, s_tg = w.sem(), w.sem()

    @step("block")
    def _():
        for t in range(2):
            total = bos[t] + sum_os.result(t)
            obs[t] = total.astype(BF).reshape(2, 32, 1024)
        send_home(obs, bor, s_bo)

    @step("block_end")
    def _():
        w.arrived(bor, s_bo)
        o_block[...] = bor[...]

    @step("bw_in")
    def _():
        w.arrived(dmix, s_dm)
        dkk[...] = jnp.zeros_like(dkk)
        dvv[...] = jnp.zeros_like(dvv)

    def backward_tile(t):
        @step(f"bw{t}")
        def _():
            lo, n = 256 * t, 256 * (t + 1)
            d_out = dmix[...].reshape(1024, LANES)[lo : lo + 256, :].astype(F32)
            product = d_out * att[lo : lo + 256, :]
            results = []
            for h, q in enumerate((q0, q1)):
                here = low if h == 0 else jnp.logical_not(low)
                d_head = jnp.where(here, d_out, 0.0).astype(BF)
                delta = jnp.sum(jnp.where(here, product, 0.0), axis=1, keepdims=True)
                weights = prob[h, lo : lo + 256, 0:n]
                pulled = _nt(d_head, vv[0:n, :])
                d_scores = (weights.astype(F32) * (pulled - delta)).astype(BF)
                results.append(_nn(d_scores, kk[0:n, :]))
                dkk[0:n, :] += _tn(d_scores, q[lo : lo + 256, :])
                dvv[0:n, :] += _tn(weights, d_head)
            dqq[lo : lo + 256, :] = jnp.where(low, results[0], results[1]) * (HEAD_DIM**-0.5)

    for t in range(4):
        backward_tile(t)
    s_dpx = w.sem()

    @step("back")
    def _():
        query_weight, key_weight = query_gain(), key_gain()

        def back_rows(t, carry):
            query_sum, key_sum = carry
            rows = pl.ds(pl.multiple_of(t * 256, 256), 256)
            cosine, sine = cos_t[rows, :], sin_t[rows, :]
            query = raw[rows, 0:LANES]
            both = raw[rows, LANES : 2 * LANES]

            def through(values, grads, gain_row):
                scale = inverse_root(values)
                normed = values * scale
                grads = grads * cosine - swap(grads) * sine
                weighted = grads * gain_row
                inner = head_sum(weighted * normed) * (1.0 / HEAD_DIM)
                return scale * (weighted - normed * inner), jnp.sum(grads * normed, axis=0, keepdims=True)

            query_back, query_term = through(query, dqq[rows, :], query_weight)
            d_key = dkk[rows, :]
            d_key = d_key + pltpu.roll(d_key, HALF_LANES, 1)
            key_back, key_term = through(both, d_key, key_weight)
            d_value = dvv[rows, :]
            d_value = d_value + pltpu.roll(d_value, HALF_LANES, 1)
            dpj[rows, 0:LANES] = query_back.astype(BF)
            dpj[rows, LANES : 2 * LANES] = jnp.where(low, key_back, d_value).astype(BF)
            return query_sum + query_term, key_sum + key_term

        zero_row = jnp.zeros((1, LANES), F32)
        query_sum, key_sum = lax.fori_loop(0, 4, back_rows, (zero_row, zero_row))
        w.send(dpj.at[pl.ds(other_rows, 512)], dpx, sib, s_dpx)
        gg[:, 2 * LANES : 3 * LANES] = jnp.zeros((8, LANES), F32)
        gg[0:1, 2 * LANES : 3 * LANES] = query_sum + pltpu.roll(query_sum, HALF_LANES, 1)
        gg[1:2, 2 * LANES : 3 * LANES] = key_sum

    def first_steps(t):
        @step(f"df{t}")
        def _():
            if t == 0:
                w.arrived(dpx, s_dpx)
            here = pl.ds(256 * t, 256)
            rows = pl.ds(pl.multiple_of(my_rows + 256 * t, 256), 256)
            dfb[here, :] = (_nn(dpj[rows, :], w2[own_head, :]) + _nn(dpx[here, :], w2[sib_head, :])).astype(BF)
            sum_df.over_x(t)

    first_steps(0)
    first_steps(1)
    s_back = w.sem()

    def term_steps(name, rows, value):
        sem = many(3)

        @step(f"{name}_y")
        def _():
            term = value()
            count = rows.stop - rows.start
            for p in range(4):
                igs[p, rows, :] = term[count * p : count * (p + 1), :].astype(BF)
            at = pl.ds(rows.start, count)
            w.send(igs.at[team_d, at], agr.at[1, at], yp, sem[1])
            w.send(igs.at[team_y, at], agr.at[0, at], yp, sem[0])

        at = pl.ds(rows.start, rows.stop - rows.start)

        @step(f"{name}_z")
        def _():
            w.arrived(agr.at[1, at], sem[1])
            agz[rows, :] = (igs[team_z, rows, :].astype(F32) + agr[1, rows, :].astype(F32)).astype(BF)
            w.send(agz.at[at], agt.at[at], zp, sem[2])

        @step(f"{name}_sum")
        def _():
            w.arrived(agr.at[0, at], sem[0])
            w.arrived(agt.at[at], sem[2])
            agh[rows, :] = (
                igs[team, rows, :].astype(F32) + agr[0, rows, :].astype(F32) + agt[rows, :].astype(F32)
            ).astype(BF)

    def in_value():
        w.arrived(first2.at[pl.ds(0, 512)], s_first)
        return _tn(dpj[...], first2[...])

    def out_value():
        w.arrived(daf.at[0], s_das)
        return _tn(mxs[...], daf[...].reshape(1024, 1024))

    term_steps("in", slice(0, 64), in_value)
    term_steps("out", slice(64, 96), out_value)
    give = pltpu.make_async_remote_copy(
        src_ref=agh, dst_ref=ago, send_sem=w.sem(), recv_sem=s_back, device_id=owner_of, device_id_type=MESH,
    )

    @step("give")
    def _():
        pl.when(apart)(give.start)
        pl.when(alone)(lambda: pltpu.make_async_copy(agh, ago, s_back).start())

    @step("given")
    def _():
        w.arrived(ago, s_back)
        o_in[...] = ago[0:64, :].astype(F32)
        o_out[...] = ago[64:96, :].astype(F32)

    def token_steps(t):
        @step(f"tg{t}")
        def _():
            rows = pl.ds(pl.multiple_of(256 * t + 64 * mine, 64), 64)
            values = x[rows, :].astype(F32)
            scale = lax.rsqrt(jnp.mean(values * values, axis=1, keepdims=True) + EPS)
            normed = values * scale
            total = sum_df.result(t)
            terms["attn"] = terms["attn"] + jnp.sum(total * normed, axis=0, keepdims=True)
            weighted = total * attn_gain()
            inner = jnp.mean(weighted * normed, axis=1, keepdims=True)
            grad = dstate[t] + scale * (weighted - normed * inner)
            tgs[t] = grad.astype(BF).reshape(2, 32, 1024)

    token_steps(0)
    token_steps(1)

    @step("tok_home")
    def _():
        send_home(tgs, tgr, s_tg)

    @step("tok_end")
    def _():
        w.arrived(tgr, s_tg)
        o_tokens[...] = tgr[...].astype(F32)

    s_gg, s_gt4 = w.sem(), many(3)

    @step("gg_out")
    def _():
        for n in range(8):
            gg[n : n + 1, 0:LANES] = terms["attn"][:, LANES * n : LANES * (n + 1)]
            gg[n : n + 1, LANES : 2 * LANES] = terms["ffn"][:, LANES * n : LANES * (n + 1)]
        for d, e in others:
            w.send(gg, ggq.at[g], quad(d, e), s_gg)
        w.local(gg, ggq.at[g], s_gg)

    @step("gg_sum")
    def _():
        w.arrived(ggq, s_gg)
        total = ggq[0]
        for n in range(1, 8):
            total = total + ggq[n]
        gsum[...] = total
        for n, peer in enumerate((yp, zp, diag)):
            w.send(gsum, ggt.at[n], peer, s_gt4[n])

    @step("gg_end")
    def _():
        total = gsum[...]
        for n in range(3):
            w.arrived(ggt.at[n], s_gt4[n])
            total = total + ggt[n]
        o_gain[...] = total

    for name in ORDER:
        steps.pop(name)()
    assert not steps, sorted(steps)
    w.finish()
    for half, away in late:
        pl.when(k != half)(away.wait_send)
    pl.when(apart)(move.wait_send)
    pl.when(apart)(give.wait_send)


ORDER = (
    "tok_out0", "wout_start", "u1_own", "tok_out1", "u0_z0", "move", "u0_y", "tok_own0", "cot_own1",
    "wout_pass", "tok_rel1", "gain_start", "tok_rel0", "cot_out1", "moved", "win_start", "u0_f0", "u1_y",
    "u0_z2", "u0_s1", "wout_end", "tok_fwd1", "tok_own1", "tok_fwd0", "gain_pass", "u1_z1", "win_pass",
    "u0_f2", "u1_z0", "gain_end", "win_end", "cot_rel1", "cot_own0", "wout_fwd", "cot_out0", "gains", "u1_s1",
    "u1_z2", "project", "rotate", "at1", "at3", "wout_sib", "at0", "u1_f1", "cot_fwd0", "u0_z1", "u1_f0",
    "at2", "mix_fwd1", "u1_f2", "cot_rel0", "mix_fwd0", "u0_own", "u0_f1", "u1_s3", "cot_fwd1", "second",
    "u0_s3", "u1_all", "dy", "u0_all", "ff00", "ff01", "ff10", "wg0_in", "wg01", "wg02", "wg00", "gr0_y1",
    "ff11", "ds_z0", "st0", "ds_z1", "wg1_in", "wg10", "wg11", "wg12", "os_x0", "gr0_z", "st1", "os_z0",
    "gr1_y1", "os_x1", "bw_in", "bw3", "bw2", "da_out", "first_sib", "bw1", "bw0", "back", "gr0_y0", "df0",
    "gr1_z", "in_y", "da_fwd", "df_z0", "da_sib", "os_z1", "df1", "in_z", "out_y", "tg0", "df_z1", "out_z",
    "in_sum", "gr1_y0", "block", "tg1", "gg_out", "tok_home", "gr0_end", "out_sum", "give", "block_end",
    "gr1_end", "gg_sum", "tok_end", "gg_end", "given",
)


TEAM_SCRATCH = (
    ((512, 1024), BF), ((2, 32, 1024), BF), ((2, 32, 1024), BF), ((512, 1024), BF),
    ((4, 4, 2, 32, 1024), BF), ((3, 704, 1024), BF), ((3, 512, 1024), BF), ((4, 8, 8, 128), F32), ((8, 1024), F32),
    ((1024, 1024), BF), ((1024, 256), F32), ((512, 256), F32),
    ((1024, 128), BF), ((1024, 128), BF), ((1024, 128), BF), ((1024, 128), BF), ((2, 1024, 1024), BF),
    ((1024, 128), F32), ((1024, 128), BF), ((512, 1024), BF), ((1024, 1024), BF), ((1024, 1024), BF),
    ((3, 1024, 384), BF), ((3, 1024, 256), BF), ((3, 512, 384), BF),
    ((512, 1024), BF), ((512, 1024), BF), ((3, 2, 64, 1024), BF), ((3, 2, 64, 1024), BF), ((3, 2, 64, 1024), BF),
    ((2, 3, 144, 1024), BF), ((3, 144, 1024), BF), ((3, 144, 1024), BF),
    ((2, 64, 1024), F32), ((2, 64, 1024), BF), ((2, 2, 4, 64, 1024), BF), ((2, 2, 4, 64, 128), BF),
    ((1024, 128), F32), ((1024, 128), F32), ((1024, 128), F32), ((1024, 256), BF), ((512, 256), BF),
    ((512, 1024), BF), ((3, 2, 64, 1024), BF),
    ((4, 96, 1024), BF), ((2, 96, 1024), BF), ((96, 1024), BF), ((96, 1024), BF), ((96, 1024), BF), ((96, 1024), BF),
    ((2, 64, 1024), F32), ((2, 2, 32, 1024), BF), ((2, 2, 32, 1024), BF), ((2, 2, 32, 1024), BF),
    ((2, 2, 32, 1024), BF),
    ((8, 384), F32), ((8, 8, 384), F32), ((8, 384), F32), ((3, 8, 384), F32),
)


def rotary_lanes(rows):
    width = HEAD_DIM // 2
    freq = (ROPE_BASE ** (-np.arange(width, dtype=np.float32) * np.float32(2.0 / HEAD_DIM))).astype(np.float32)
    angle = (np.arange(rows, dtype=np.float32)[:, None] * freq).astype(np.float32).astype(np.float64)
    cosine, sine = np.cos(angle), np.sin(angle)
    return (
        np.tile(np.concatenate([cosine, cosine], 1), (1, 2)).astype(np.float32),
        np.tile(np.concatenate([-sine, sine], 1), (1, 2)).astype(np.float32),
    )


def on_team(tokens, segments, lengths, attn_in, attn_out, gains, ffn_weights, cotangent):
    batches, block_len, halves, width = tokens.shape
    here = lax.axis_index("ctx")
    seq = here // 8
    rows = segments.shape[1]
    docs = lax.dynamic_index_in_dim(segments, seq, 0, False)
    back = docs[:, 1].reshape(rows // block_len, block_len)[::-1].reshape(rows)
    docs = jnp.concatenate([docs[:, 0], back])
    limit = lax.dynamic_index_in_dim(lengths, seq, 0, False)
    doc_row = jnp.where(jnp.arange(2 * rows, dtype=jnp.int32) < limit, docs, -1)
    cosine, sine = rotary_lanes(2 * rows)
    args = (
        tokens.transpose(0, 2, 1, 3),
        cotangent.transpose(0, 2, 1, 3),
        attn_in,
        attn_out,
        jnp.pad(gains.astype(F32)[None], ((0, 7), (0, LANES - gains.shape[0]))),
        ffn_weights.transpose(1, 0, 2),
        docs[:, None],
        doc_row[None],
        jnp.broadcast_to(limit, (8, LANES)),
        jnp.asarray(cosine),
        jnp.asarray(sine),
    )
    vmem = pl.BlockSpec(memory_space=pltpu.VMEM)
    outs = pl.pallas_call(
        block_kernel,
        out_shape=(
            jax.ShapeDtypeStruct((2, 2, 32, 1024), BF),
            jax.ShapeDtypeStruct((2, 2, 32, 1024), F32),
            jax.ShapeDtypeStruct((64, 1024), F32),
            jax.ShapeDtypeStruct((32, 1024), F32),
            jax.ShapeDtypeStruct((8, 384), F32),
            jax.ShapeDtypeStruct((3, 144, 1024), F32),
        ),
        in_specs=[vmem] * len(args),
        out_specs=(vmem,) * 6,
        scratch_shapes=[pltpu.VMEM(shape, kind) for shape, kind in TEAM_SCRATCH]
        + [pltpu.SemaphoreType.DMA((COPIES,))],
        compiler_params=pltpu.CompilerParams(
            collective_id=0, has_side_effects=True, vmem_limit_bytes=VMEM_BYTES
        ),
    )(*args)
    block, token_grad, in_grad, out_grad, gain_grad, unit_grad = outs
    every = jnp.concatenate(
        [gain_grad[:, :128].reshape(-1), gain_grad[:, 128:256].reshape(-1), gain_grad[0, 256:320], gain_grad[1, 256:320]]
    )
    own = lax.axis_index("dp") * lax.axis_size("ctx") + here
    return (
        block.transpose(0, 2, 1, 3),
        token_grad.transpose(0, 2, 1, 3),
        in_grad,
        out_grad,
        lax.dynamic_slice_in_dim(every, own * gains.shape[0], gains.shape[0], 0),
        unit_grad.transpose(1, 0, 2),
    )


VMEM_BYTES = 62 << 20


def solution(mesh):
    dp, ctx = mesh.devices.shape
    if ctx == 2 * KV_HEADS:
        ring = "ctx"
        every = ("dp", "ctx")
        team, run = mesh, on_team
    else:
        ring = ("s", "q", "g")
        every = EVERY
        team = Mesh(mesh.devices.reshape(dp, 2, ctx // (2 * KV_HEADS), KV_HEADS), EVERY)
        run = on_device
    placed = (
        P("dp", ring, None, None),
        P("dp", None, None),
        P("dp"),
        P(every, None),
        P(every, None),
        P(every),
        P(every, None, None),
        P("dp", ring, None, None),
    )
    return jax.shard_map(
        run,
        mesh=team,
        in_specs=placed,
        out_specs=(
            P("dp", ring, None, None),
            P("dp", ring, None, None),
            P(every, None),
            P(every, None),
            P(every),
            P(every, None, None),
        ),
        check_vma=False,
    )
```

```python
import jax
import jax.numpy as jnp
import numpy as np
from jax import lax
from jax.experimental import pallas as pl
from jax.experimental.pallas import tpu as pltpu
from jax.sharding import Mesh
from jax.sharding import PartitionSpec as P

FF = 4608
HEADS = 16
KV_HEADS = 8
HEAD_DIM = 64
GROUP = HEADS // KV_HEADS
QKV_ROWS = 2048

EPS = 1e-05
ROPE_BASE = 1000000.0
MASKED = -1e30
BF = jnp.bfloat16
F32 = jnp.float32


def root_mean(values):
    return lax.rsqrt(jnp.mean(values * values, axis=-1, keepdims=True) + EPS)


def rotate(values, cosine, sine):
    width = values.shape[-1] // 2
    first = values[..., :width]
    second = values[..., width:]
    return jnp.concatenate(
        [first * cosine - second * sine, second * cosine + first * sine], axis=-1
    )


def tables(positions):
    width = HEAD_DIM // 2
    freq = ROPE_BASE ** (-jnp.arange(width, dtype=F32) * 2.0 / HEAD_DIM)
    angle = positions.astype(F32)[..., None] * freq
    return (jnp.cos(angle), jnp.sin(angle))


def prepare(query_raw, key_raw, query_gain, key_gain, cosine, sine):
    query_norm = query_raw * root_mean(query_raw) * query_gain
    key_norm = key_raw * root_mean(key_raw) * key_gain
    return (
        rotate(query_norm, cosine[:, None], sine[:, None]),
        rotate(key_norm, cosine, sine),
    )


def norm_back(grad, normed, scale_rows, gain):
    weighted = grad * gain
    inner = jnp.mean(weighted * normed, axis=-1, keepdims=True)
    return (scale_rows * (weighted - normed * inner), jnp.sum(grad * normed, axis=0))


def dot(a, b, ca, cb):
    return lax.dot_general(a, b, (((ca,), (cb,)), ((), ())), preferred_element_type=F32)


TEAM = ("dp", "s", "q")
EVERY = ("dp", "s", "q", "g")


def spread(local, block_len):
    mine = lax.all_to_all(local, "s", 0, 0, tiled=True)
    return lax.all_gather(mine, "g", axis=0, tiled=False)


def on_device(tokens, segments, lengths, attn_in, attn_out, gains, ffn_weights, cotangent):
    batches, block_len, halves, width = tokens.shape
    seq = lax.axis_index("s")
    quarter = lax.axis_index("q")
    head = lax.axis_index("g")
    quarters = lax.axis_size("q")
    heads = lax.axis_size("g")
    ctx_count = 2 * quarters * heads
    scale = HEAD_DIM ** (-0.5)
    weight_in = lax.all_gather(attn_in, EVERY, axis=0, tiled=True)
    weight_out = lax.all_gather(attn_out, EVERY, axis=0, tiled=True)
    gain_all = lax.all_gather(gains, EVERY, axis=0, tiled=True).astype(F32)
    attn_gain = gain_all[:width]
    ffn_gain = gain_all[width : 2 * width]
    query_gain = gain_all[2 * width : 2 * width + HEAD_DIM]
    key_gain = gain_all[2 * width + HEAD_DIM :]
    head_rows = (GROUP + 2) * HEAD_DIM
    out_rows = GROUP * HEAD_DIM
    weight_head = lax.dynamic_slice_in_dim(weight_in, head * head_rows, head_rows, 0)
    weight_mix = lax.dynamic_slice_in_dim(weight_out, head * out_rows, out_rows, 0)

    inputs = spread(tokens, block_len)
    count = inputs.size // width
    inputs = inputs.reshape(count, width).astype(F32)
    cot = spread(cotangent, block_len).reshape(count, width).astype(F32)

    def places(which):
        owner_g = jnp.arange(heads, dtype=jnp.int32)[:, None, None, None]
        owner_s = jnp.arange(2, dtype=jnp.int32)[None, :, None, None]
        row = jnp.arange(block_len, dtype=jnp.int32)[None, None, :, None]
        half = jnp.arange(2, dtype=jnp.int32)[None, None, None, :]
        owner = owner_s * (quarters * heads) + which * heads + owner_g
        block = jnp.where(half == 0, owner, 2 * ctx_count - 1 - owner)
        return (
            (block * block_len + row).reshape(count),
            jnp.broadcast_to((owner * block_len + row) * 2 + half, (heads, 2, block_len, 2)).reshape(count),
        )

    docs = lax.dynamic_index_in_dim(segments, seq, 0, False).reshape(-1)
    length = lax.dynamic_index_in_dim(lengths, seq, 0, False)
    place, slot = places(quarter)
    key_place, key_slot = jax.vmap(places)(jnp.arange(quarters, dtype=jnp.int32))
    key_place = key_place.reshape(-1)
    query_doc = docs[slot]
    key_doc = docs[key_slot.reshape(-1)]
    causal = key_place[None, :] <= place[:, None]
    live = (key_place[None, :] < length) | (key_place[None, :] == place[:, None])
    mask = causal & live & (query_doc[:, None] == key_doc[None, :])
    valid = (place < length).astype(F32)[:, None]

    first_scale = root_mean(inputs)
    first_normed = inputs * first_scale
    first = (first_normed * attn_gain).astype(BF)
    projected = dot(first, weight_head, 1, 1).reshape(count, GROUP + 2, HEAD_DIM)
    cosine, sine = tables(place)

    def prepare_here(query_raw, key_raw, gain_query, gain_key):
        return prepare(query_raw, key_raw, gain_query, gain_key, cosine, sine)

    (query_rot, key_rot), prepare_pull = jax.vjp(
        prepare_here, projected[:, :GROUP], projected[:, GROUP], query_gain, key_gain
    )
    queries = query_rot.astype(BF)
    pair = jnp.stack([key_rot.astype(BF), projected[:, GROUP + 1].astype(BF)])
    pair = lax.all_gather(pair, "q", axis=1, tiled=True)
    keys, values = pair[0], pair[1]

    scores = jnp.einsum("qjd,kd->jqk", queries, keys, preferred_element_type=F32) * scale
    scores = jnp.where(mask[None], scores, MASKED)
    peak = jnp.max(scores, axis=-1, keepdims=True)
    expo = jnp.where(mask[None], jnp.exp(scores - peak), 0.0)
    weights = expo / jnp.sum(expo, axis=-1, keepdims=True)
    attended = jnp.einsum("jqk,kd->qjd", weights.astype(BF), values, preferred_element_type=F32)
    mixed_here = attended.astype(BF).reshape(count, out_rows)
    mixed = lax.all_gather(mixed_here, "g", axis=1, tiled=True)
    state = inputs + dot(mixed, weight_out, 1, 0)
    second_scale = root_mean(state)
    second_normed = state * second_scale
    second = (second_normed * ffn_gain).astype(BF)
    grad_out = cot * valid
    grad_low = grad_out.astype(BF)

    units = lax.all_gather(ffn_weights, TEAM, axis=0, tiled=True)
    unit_gate, unit_up, unit_down = units[:, 0], units[:, 1], units[:, 2]
    gate = dot(second, unit_gate, 1, 1)
    upward = dot(second, unit_up, 1, 1)
    sigmoid = jax.nn.sigmoid(gate)
    hidden = (gate * sigmoid * upward).astype(BF)
    d_hidden = dot(grad_low, unit_down, 1, 1)
    d_gate = (d_hidden * upward * sigmoid * (1.0 + gate * (1.0 - sigmoid))).astype(BF)
    d_up = (d_hidden * gate * sigmoid).astype(BF)
    d_second = dot(d_gate, unit_gate, 1, 0) + dot(d_up, unit_up, 1, 0)
    own = count // heads

    def gathered(values):
        return lax.psum_scatter(values.astype(BF), "g", scatter_dimension=0, tiled=True).astype(F32)

    def own_rows(values):
        return lax.dynamic_slice_in_dim(values, head * own, own, 0)

    def home(values):
        back = values.reshape(2, block_len, halves, width)
        return lax.all_to_all(back, "s", 0, 0, tiled=True)

    ffn_sum = gathered(dot(hidden, unit_down, 1, 0))
    block_out = home((own_rows(state) + ffn_sum).astype(BF))
    ffn_grad = lax.psum_scatter(
        jnp.stack([dot(d_gate, second, 0, 0), dot(d_up, second, 0, 0), dot(hidden, grad_low, 0, 0)], axis=1),
        TEAM,
        scatter_dimension=0,
        tiled=True,
    )
    norm_grad, ffn_gain_grad = norm_back(
        gathered(d_second), own_rows(second_normed), own_rows(second_scale), ffn_gain
    )
    state_grad = own_rows(grad_out) + norm_grad
    attended_grad = lax.all_gather(state_grad.astype(BF), "g", axis=0, tiled=True)
    mixed_grad = dot(attended_grad, weight_mix, 1, 1).astype(BF)
    out_term = dot(mixed_here, attended_grad, 0, 0)
    mixed_grad = mixed_grad.reshape(count, GROUP, HEAD_DIM)
    delta = jnp.sum(mixed_grad.astype(F32) * attended, axis=-1).T[:, :, None]
    pulled = jnp.einsum("qjd,kd->jqk", mixed_grad, values, preferred_element_type=F32)
    score_grad = (weights * (pulled - delta)).astype(BF)
    query_grad = jnp.einsum("jqk,kd->qjd", score_grad, keys, preferred_element_type=F32) * scale
    key_grad = jnp.einsum("jqk,qjd->kd", score_grad, queries, preferred_element_type=F32) * scale
    value_grad = jnp.einsum("jqk,qjd->kd", weights.astype(BF), mixed_grad, preferred_element_type=F32)
    if quarters > 1:
        key_grad = lax.psum_scatter(key_grad, "q", scatter_dimension=0, tiled=True)
        value_grad = lax.psum_scatter(value_grad, "q", scatter_dimension=0, tiled=True)
    query_raw_grad, key_raw_grad, query_gain_grad, key_gain_grad = prepare_pull((query_grad, key_grad))
    projected_grad = jnp.concatenate(
        [query_raw_grad.reshape(count, out_rows), key_raw_grad, value_grad], axis=1
    ).astype(BF)
    first_grad = gathered(dot(projected_grad, weight_head, 1, 0))
    in_term = dot(projected_grad, first, 0, 0)
    input_norm_grad, attn_gain_grad = norm_back(
        first_grad, own_rows(first_normed), own_rows(first_scale), attn_gain
    )
    tokens_grad = home(state_grad + input_norm_grad)
    gain_term = jnp.concatenate([attn_gain_grad, ffn_gain_grad, query_gain_grad, key_gain_grad])

    def placed(term, rows):
        whole = jnp.zeros((rows, width), F32)
        return lax.dynamic_update_slice_in_dim(whole, term, head * term.shape[0], 0)

    return (
        block_out,
        tokens_grad,
        lax.psum_scatter(placed(in_term, QKV_ROWS), EVERY, scatter_dimension=0, tiled=True),
        lax.psum_scatter(placed(out_term, HEADS * HEAD_DIM), EVERY, scatter_dimension=0, tiled=True),
        lax.psum_scatter(gain_term, EVERY, scatter_dimension=0, tiled=True),
        ffn_grad,
    )


LANES = 128
HALF_LANES = 64


def _nt(a, b):
    return lax.dot_general(a, b, (((1,), (1,)), ((), ())), preferred_element_type=F32)


def _nn(a, b):
    return lax.dot_general(a, b, (((1,), (0,)), ((), ())), preferred_element_type=F32)


def _tn(a, b):
    return lax.dot_general(a, b, (((0,), (0,)), ((), ())), preferred_element_type=F32)


MESH = pl.DeviceIdType.MESH
COPIES = 400


class Wires:
    def __init__(self, sems):
        self.sems = sems
        self.used = 0
        self.pending = []

    def sem(self):
        self.used += 1
        return self.sems.at[self.used - 1]

    def send(self, src, dst, to, arrives):
        copy = pltpu.make_async_remote_copy(
            src_ref=src, dst_ref=dst, send_sem=self.sem(), recv_sem=arrives,
            device_id=to, device_id_type=MESH,
        )
        copy.start()
        self.pending.append(copy)
        return copy

    def local(self, src, dst, arrives):
        copy = pltpu.make_async_copy(src, dst, arrives)
        copy.start()
        return copy

    def arrived(self, ref, sem):
        pltpu.make_async_copy(ref, ref, sem).wait()

    def finish(self, copies=None):
        copies = list(self.pending if copies is None else copies)
        for copy in copies:
            copy.wait_send()
        done = {id(copy) for copy in copies}
        self.pending = [copy for copy in self.pending if id(copy) not in done]


def block_kernel(
    tok, cot, win, wout, gain_in, wffn, segments, lengths, cos_t, sin_t,
    o_block, o_tokens, o_in, o_out, o_gain, o_ffn,
    x, rel_t, rel_c, w2, wall, wfa, wfb, gb, grow, first2, raw, po,
    q0, q1, kk, vv, prob, att, mxs, mix, sec2, dy2, acta, actb, asend,
    dsb, osb, dsr, osr, rsz, gr, gs, gt, dstate, dmb, daf, dmix,
    dkk, dvv, dqq, dpj, dpx, dfb, dfr, igs, agr, agz, agt, agh, ago,
    bos, obs, bor, tgs, tgr, gg, ggq, gsum, ggt, gain, gflat, doc_col, doc_row, sems,
):
    dp = lax.axis_index("dp")
    c = lax.axis_index("ctx")
    zh = lax.div(c, 8)
    g = lax.rem(c, 8)
    j = lax.div(g, 2)
    k = lax.rem(c, 2)
    chips = (j, j + 1 - 2 * lax.rem(j, 2), j + 2 - 4 * lax.div(j, 2), 3 - j)
    cores = (k, 1 - k)

    def quad(d, e):
        return (dp, zh * 8 + 2 * chips[d] + cores[e])

    sib = quad(0, 1)
    czp = lax.rem(c + 8, 16)
    zp = (dp, lax.rem(c + 8, 16))
    zps = (dp, 8 * (1 - zh) + 2 * j + 1 - k)
    yp = (1 - dp, c)
    diag = (1 - dp, lax.rem(c + 8, 16))
    team = 2 * dp + zh
    team_y = 2 * (1 - dp) + zh
    team_z = 2 * dp + 1 - zh
    team_d = 3 - team
    w = Wires(sems)
    others = [(d, e) for d in range(4) for e in range(2) if (d, e) != (0, 0)]

    zl, xx = lax.div(j, 2), lax.rem(j, 2)
    keeper = (xx, 8 * k + 4 * dp + 2 * zh + zl)
    owner_of = (zl, 8 * xx + 4 * k + 2 * dp + zh)
    alone = jnp.logical_and(keeper[0] == dp, keeper[1] == c)
    apart = jnp.logical_not(alone)

    barrier = pltpu.get_barrier_semaphore()
    peers = [quad(d, e) for d, e in others] + [zp, zps, yp, diag]
    for peer in peers:
        pl.semaphore_signal(barrier, inc=1, device_id=peer, device_id_type=MESH)

    limit = lengths[zh]
    docs = segments[zh].astype(F32).astype(BF)
    line = lax.broadcasted_iota(jnp.int32, (512, 512), 0)
    cell = lax.broadcasted_iota(jnp.int32, (512, 512), 1)
    same_place = (line == cell).astype(F32).astype(BF)
    mirrored = (line + 480 - 2 * (line - lax.rem(line, 32)) == cell).astype(F32).astype(BF)
    for half, order in enumerate((same_place, mirrored)):
        ids = jnp.broadcast_to(docs[half : half + 1, :], (16, 512))
        key = lax.broadcasted_iota(jnp.int32, (1, 512), 1) + 512 * half
        doc_row[0:1, 512 * half : 512 * (half + 1)] = jnp.where(key < limit, _nn(ids, order)[0:1, :], -1.0)
        doc_col[512 * half : 512 * (half + 1), :] = _nt(order, ids)[:, 0:8]
    gain[...] = jnp.zeros_like(gain)
    gain[0:1, 0:68] = gain_in[...].astype(F32)

    @pl.when(apart)
    def _():
        pl.semaphore_signal(barrier, inc=1, device_id=keeper, device_id_type=MESH)
        pl.semaphore_signal(barrier, inc=1, device_id=owner_of, device_id_type=MESH)
        pl.semaphore_wait(barrier, len(peers) + 2)

    @pl.when(alone)
    def _():
        pl.semaphore_wait(barrier, len(peers))

    def many(*shape):
        return [many(*shape[1:]) for _ in range(shape[0])] if shape else w.sem()

    def piece(chip):
        return chip + k * (3 - 2 * chip)

    def row_block(owner, half):
        return owner + half * (15 - 2 * owner)

    my_rows = pl.multiple_of(512 * k, 512)
    other_rows = pl.multiple_of(512 * (1 - k), 512)
    own_head, sib_head = pl.ds(0, 256), pl.ds(256, 256)
    mine = piece(j)
    steps = {}

    def step(name):
        def keep(body):
            steps[name] = body
            return body
        return keep

    def rows_of(buf, offset):
        def at(half, start, count):
            return buf.at[pl.ds(pl.multiple_of(offset * half + start, 32), count)]
        return at

    def rows_steps(name, source, relay, at):
        s_rel, s_here, s_z, s_d = many(2), w.sem(), many(2), w.sem()
        passed = []

        def scatter(src, owner, e, which):
            half = cores[e]
            dst = at(half, pl.multiple_of(row_block(owner, half) * 32, 32), 32)
            w.send(src, dst, quad(2, e), s_z[which])
            w.send(src, dst, quad(1, e), s_here)
            if e == 0:
                w.local(src, dst, s_here)
            else:
                w.send(src, dst, sib, s_here)

        def halves(e):
            @step(f"{name}_out{e}")
            def _():
                w.send(source.at[1 - zh, cores[e]], relay.at[cores[e]], zp, s_rel[e])

            @step(f"{name}_own{e}")
            def _():
                scatter(source.at[zh, cores[e]], c, e, 0)

            @step(f"{name}_rel{e}")
            def _():
                w.arrived(relay.at[cores[e]], s_rel[e])
                scatter(relay.at[cores[e]], czp, e, 1)

            @step(f"{name}_fwd{e}")
            def _():
                first = (zh if e == 0 else 1 - zh) * 8 + 2 * chips[2]
                rows = at(k, pl.multiple_of(32 * (first + k * (14 - 2 * first)), 64), 64)
                w.arrived(rows, s_z[e])
                passed.append(w.send(rows, rows, quad(1, 0), s_d))

        halves(0)
        halves(1)
        return s_here, s_d, passed

    s_x, s_xd, _ = rows_steps("tok", tok, rel_t, rows_of(x, 0))
    s_c, s_cd, cot_passed = rows_steps("cot", cot, rel_c, rows_of(dy2, 512))

    def head_rows(t):
        return w2.at[pl.ds(pl.multiple_of(64 * t, 64), 64)]

    def exchange(name, src, at, keep):
        sem = many(4)

        @step(f"{name}_start")
        def _():
            w.send(src, at(team), zp, sem[1])
            w.send(src, at(team), yp, sem[0])
            if keep:
                w.local(src, at(team), sem[3])

        @step(f"{name}_pass")
        def _():
            w.arrived(at(team_z), sem[1])
            w.send(at(team_z), at(team_z), yp, sem[2])

        def end():
            w.arrived(at(team_y), sem[0])
            w.arrived(at(team_d), sem[2])
            if keep:
                w.arrived(at(team), sem[3])

        return end

    s_move, s_w2, s_gq, s_wq, s_ws = w.sem(), w.sem(), w.sem(), many(3), w.sem()
    gains_end = exchange("gain", gain, lambda t: gb.at[t, g], True)
    heads_end = exchange("win", head_rows(team), head_rows, False)
    wout_end = exchange("wout", wout, lambda t: wall.at[t, j, k], True)
    move = pltpu.make_async_remote_copy(
        src_ref=win, dst_ref=head_rows(lax.rem(g, 4)), send_sem=w.sem(), recv_sem=s_move,
        device_id=keeper, device_id_type=MESH,
    )

    @step("move")
    def _():
        pl.when(apart)(move.start)
        pl.when(alone)(lambda: pltpu.make_async_copy(win, head_rows(team), s_move).start())

    @step("moved")
    def _():
        w.arrived(head_rows(team), s_move)

    @step("gain_end")
    def _():
        gains_end()
        for d, e in others:
            w.send(gb.at[:, g], gb.at[:, g], quad(d, e), s_gq)

    @step("win_end")
    def _():
        heads_end()
        w.send(w2.at[own_head], w2.at[sib_head], sib, s_w2)

    @step("wout_end")
    def _():
        wout_end()
        for d in (2, 1):
            w.send(wall.at[:, j, k], wall.at[:, j, k], quad(d, 0), s_wq[d - 1])

    @step("wout_fwd")
    def _():
        w.arrived(wall.at[:, chips[2], k], s_wq[1])
        w.send(wall.at[:, chips[2], k], wall.at[:, chips[2], k], quad(1, 0), s_wq[2])

    @step("wout_sib")
    def _():
        for d in (1, 3):
            w.arrived(wall.at[:, j, k], s_wq[d - 1])
        w.send(wall.at[:, :, k], wall.at[:, :, k], sib, s_ws)

    parts = ((0, 80, wfa, acta, 320, 384), (80, 64, wfb, actb, 256, 256))
    s_f = many(2, 2, 4, 3)
    held = [[], []]

    def source(part, kind):
        return wffn.at[kind, pl.ds(parts[part][0], parts[part][1])]

    def unit(part, kind, far, slot):
        _, rows, buf, _, _, second = parts[part]
        return buf.at[kind, pl.ds(second * far + rows * slot, rows)]

    def unit_steps(part):
        sem = s_f[part]

        @step(f"u{part}_own")
        def _():
            for kind in range(3):
                w.local(source(part, kind), unit(part, kind, 0, 0), sem[0][0][kind])
                w.send(source(part, kind), unit(part, kind, 1, 0), sib, sem[1][0][kind])
                if part == 0:
                    wfa[kind, 320:384, :] = jnp.zeros((64, 1024), BF)

        @step(f"u{part}_y")
        def _():
            for kind in range(3):
                w.send(source(part, kind), unit(part, kind, 0, 1), yp, sem[0][1][kind])

        def from_z(kind):
            @step(f"u{part}_z{kind}")
            def _():
                w.send(source(part, kind), unit(part, kind, 0, 2), zp, sem[0][2][kind])

            @step(f"u{part}_f{kind}")
            def _():
                here = unit(part, kind, 0, 2)
                w.arrived(here, sem[0][2][kind])
                held[part].append(w.send(here, unit(part, kind, 0, 3), yp, sem[0][3][kind]))
                held[part].append(w.send(here, unit(part, kind, 1, 2), sib, sem[1][2][kind]))

        def ready(slot):
            @step(f"u{part}_s{slot}")
            def _():
                for kind in range(3):
                    here = unit(part, kind, 0, slot)
                    w.arrived(here, sem[0][slot][kind])
                    held[part].append(w.send(here, unit(part, kind, 1, slot), sib, sem[1][slot][kind]))

        for kind in range(3):
            from_z(kind)
        ready(1)
        ready(3)

        @step(f"u{part}_all")
        def _():
            for kind in range(3):
                w.arrived(unit(part, kind, 0, 0), sem[0][0][kind])
                for slot in range(4):
                    w.arrived(unit(part, kind, 1, slot), sem[1][slot][kind])

    unit_steps(0)
    unit_steps(1)

    lane = lax.broadcasted_iota(jnp.int32, (1, LANES), 1)
    low_row = lane < HALF_LANES

    @step("gains")
    def _():
        w.arrived(gb.at[:, pl.ds(0, 7)], s_gq)
        chunks = [jnp.zeros((1, LANES), F32) for _ in range(18)]
        for i in range(32):
            row = gb[i // 8, i % 8, 0:1, :]
            place, shift = divmod(68 * i, LANES)
            moved = pltpu.roll(row, shift, 1) if shift else row
            chunks[place] = chunks[place] + jnp.where(lane >= shift, moved, 0.0)
            if shift + 68 > LANES:
                chunks[place + 1] = chunks[place + 1] + jnp.where(lane < shift, moved, 0.0)
        for n in range(8):
            grow[0:1, LANES * n : LANES * (n + 1)] = chunks[n]
            grow[1:2, LANES * n : LANES * (n + 1)] = chunks[8 + n]
        flipped = pltpu.roll(chunks[16], HALF_LANES, 1)
        grow[2:3, 0:LANES] = jnp.where(low_row, chunks[16], flipped)
        grow[2:3, LANES : 2 * LANES] = jnp.where(low_row, flipped, chunks[16])

    def attn_gain():
        return grow[0:1, :]

    def ffn_gain():
        return grow[1:2, :]

    def query_gain():
        return grow[2:3, 0:LANES]

    def key_gain():
        return grow[2:3, LANES : 2 * LANES]

    s_raw, s_first = w.sem(), w.sem()

    @step("project")
    def _():
        w.arrived(x.at[pl.ds(0, 256)], s_x)
        w.arrived(x.at[pl.ds(0, 128)], s_xd)
        w.arrived(w2.at[sib_head], s_w2)
        weight = attn_gain()

        def rows_of_256(t, carry):
            rows = pl.multiple_of(t * 256, 256)
            values = x[pl.ds(rows, 256), :].astype(F32)
            scale = lax.rsqrt(jnp.mean(values * values, axis=1, keepdims=True) + EPS)
            first = (values * scale * weight).astype(BF)
            here = pl.multiple_of(my_rows + rows, 256)
            first2[pl.ds(here, 256), :] = first
            po[pl.ds(rows, 256), :] = _nt(first, w2[sib_head, :])
            raw[pl.ds(here, 256), :] = _nt(first, w2[own_head, :])
            return carry

        lax.fori_loop(0, 2, rows_of_256, 0)
        w.send(po, raw.at[pl.ds(my_rows, 512)], sib, s_raw)

    @step("first_sib")
    def _():
        w.send(first2.at[pl.ds(my_rows, 512)], first2.at[pl.ds(my_rows, 512)], sib, s_first)

    low = lax.broadcasted_iota(jnp.int32, (256, LANES), 1) < HALF_LANES
    quarter = lax.rem(lax.broadcasted_iota(jnp.int32, (256, LANES), 1), HALF_LANES) < 32

    def swap(v):
        return jnp.where(quarter, pltpu.roll(v, 96, 1), pltpu.roll(v, 32, 1))

    def head_sum(v):
        first = jnp.sum(jnp.where(low, v, 0.0), axis=1, keepdims=True)
        second = jnp.sum(jnp.where(low, 0.0, v), axis=1, keepdims=True)
        return jnp.where(low, first, second)

    def inverse_root(v):
        return lax.rsqrt(head_sum(v * v) * (1.0 / HEAD_DIM) + EPS)

    @step("rotate")
    def _():
        w.arrived(raw.at[pl.ds(0, 512)], s_raw)
        query_weight, key_weight = query_gain(), key_gain()

        def rotate_rows(t, carry):
            rows = pl.ds(pl.multiple_of(t * 256, 256), 256)
            cosine, sine = cos_t[rows, :], sin_t[rows, :]
            query = raw[rows, 0:LANES]
            both = raw[rows, LANES : 2 * LANES]
            query = query * inverse_root(query) * query_weight
            query = (query * cosine + swap(query) * sine) * (HEAD_DIM**-0.5)
            q0[rows, :] = jnp.where(low, query, 0.0).astype(BF)
            q1[rows, :] = jnp.where(low, 0.0, query).astype(BF)
            key = both * inverse_root(both) * key_weight
            key = key * cosine + swap(key) * sine
            kk[rows, :] = jnp.where(low, key, pltpu.roll(key, HALF_LANES, 1)).astype(BF)
            vv[rows, :] = jnp.where(low, pltpu.roll(both, HALF_LANES, 1), both).astype(BF)
            return carry

        lax.fori_loop(0, 4, rotate_rows, 0)

    s_mix, s_md, s_mz = w.sem(), w.sem(), many(2)
    head_lanes = pl.ds(pl.multiple_of(LANES * g, LANES), LANES)
    z_lanes = pl.ds(pl.multiple_of(256 * chips[2], 256), 256)
    late = []

    def forward_tile(t):
        @step(f"at{t}")
        def _():
            lo, n = 256 * t, 256 * (t + 1)
            place = lax.broadcasted_iota(jnp.int32, (256, n), 0) + lo
            key_place = lax.broadcasted_iota(jnp.int32, (256, n), 1)
            same = doc_col[lo : lo + 256, 0:1] == doc_row[0:1, 0:n]
            mask = (same & (key_place <= place)) | (key_place == place)
            outs = []
            for h, q in enumerate((q0, q1)):
                scores = jnp.where(mask, _nt(q[lo : lo + 256, :], kk[0:n, :]), MASKED)
                peak = jnp.max(scores, axis=1, keepdims=True)
                expo = jnp.exp(scores - peak)
                weights = (expo * (1.0 / jnp.sum(expo, axis=1, keepdims=True))).astype(BF)
                prob[h, lo : lo + 256, 0:n] = weights
                outs.append(_nn(weights, vv[0:n, :]))
            attended = jnp.where(low, outs[0], outs[1])
            att[lo : lo + 256, :] = attended
            mxs[lo : lo + 256, :] = attended.astype(BF)
            half = t // 2
            dst = mix.at[pl.ds(256 * (t % 2), 256), head_lanes]
            src = mxs.at[pl.ds(lo, 256)]
            w.send(src, dst, (dp, zh * 8 + 2 * chips[2] + half), s_mz[t % 2])
            w.send(src, dst, (dp, zh * 8 + 2 * chips[1] + half), s_mix)
            away = pltpu.make_async_remote_copy(
                src_ref=src, dst_ref=dst, send_sem=w.sem(), recv_sem=s_mix, device_id=sib, device_id_type=MESH
            )
            pl.when(k == half)(lambda: pltpu.make_async_copy(src, dst, s_mix).start())
            pl.when(k != half)(away.start)
            late.append((half, away))

    def pass_mixed(r):
        @step(f"mix_fwd{r}")
        def _():
            part = mix.at[pl.ds(256 * r, 256), z_lanes]
            w.arrived(part, s_mz[r])
            w.send(part, part, quad(1, 0), s_md)

    for t in range(4):
        forward_tile(t)
    pass_mixed(0)
    pass_mixed(1)

    s_dy, s_sec = w.sem(), w.sem()

    @step("dy")
    def _():
        w.arrived(dy2.at[pl.ds(0, 256)], s_c)
        w.arrived(dy2.at[pl.ds(0, 128)], s_cd)
        w.finish(cot_passed)

        def drop_rows(t, carry):
            rows = pl.ds(pl.multiple_of(my_rows + t * 128, 128), 128)
            place = lax.broadcasted_iota(jnp.int32, (128, 1), 0) + (my_rows + t * 128)
            kept = (place < limit).astype(F32)
            dy2[rows, :] = (dy2[rows, :].astype(F32) * kept).astype(BF)
            return carry

        lax.fori_loop(0, 4, drop_rows, 0)
        w.send(dy2.at[pl.ds(my_rows, 512)], dy2.at[pl.ds(my_rows, 512)], sib, s_dy)

    def attended_rows(rows):
        total = None
        for n in range(4):
            term = _nn(mix[rows, 256 * n : 256 * (n + 1)], wall[n].reshape(256, 1024))
            total = term if total is None else total + term
        return total

    @step("second")
    def _():
        w.arrived(wall.at[:, :, 0], s_ws)
        w.arrived(mix.at[pl.ds(0, 256)], s_mix)
        w.arrived(mix.at[:, pl.ds(0, 256)], s_md)
        weight = ffn_gain()

        def project_out(t, carry):
            rows = pl.ds(pl.multiple_of(t * 256, 256), 256)
            state = x[rows, :].astype(F32) + attended_rows(rows)
            scale = lax.rsqrt(jnp.mean(state * state, axis=1, keepdims=True) + EPS)
            here = pl.ds(pl.multiple_of(my_rows + t * 256, 256), 256)
            sec2[here, :] = (state * scale * weight).astype(BF)
            return carry

        lax.fori_loop(0, 2, project_out, 0)
        w.send(sec2.at[pl.ds(my_rows, 512)], sec2.at[pl.ds(my_rows, 512)], sib, s_sec)

    class Sum:
        def __init__(self, name, buf, into, which):
            self.buf, self.into, self.which = buf, into, which
            self.sems = many(3, 2)
            for t in range(2):
                if name == "os":
                    step(f"{name}_x{t}")(lambda t=t: self.over_x(t))
                step(f"{name}_z{t}")(lambda t=t: self.over_z(t))

        def rows(self, d, t):
            return pl.ds(pl.multiple_of(256 * t + 64 * piece(chips[d]), 64), 64)

        def over_x(self, t):
            for d, slot in ((3, 1), (1, 0)):
                w.send(self.buf.at[self.rows(d, t)], self.into.at[slot, t], quad(1, 0), self.sems[slot][t])

        def over_z(self, t):
            w.arrived(self.into.at[1, t], self.sems[1][t])
            total = self.buf[self.rows(2, t), :].astype(F32) + self.into[1, t].astype(F32)
            rsz[self.which, t] = total.astype(BF)
            w.send(rsz.at[self.which, t], self.into.at[2, t], quad(2, 0), self.sems[2][t])

        def result(self, t):
            total = self.buf[self.rows(0, t), :].astype(F32)
            for slot in (0, 2):
                w.arrived(self.into.at[slot, t], self.sems[slot][t])
                total = total + self.into[slot, t].astype(F32)
            return total

    sum_ds, sum_os, sum_df = Sum("ds", dsb, dsr, 0), Sum("os", osb, osr, 1), Sum("df", dfb, dfr, 2)

    s_act, s_gr, s_gt = many(2), many(2, 2), many(2)
    acted = []

    def part_steps(part):
        start, rows_kept, buf, acts, count, second = parts[part]
        span = pl.ds(start, rows_kept)

        def feed_forward(t):
            @step(f"ff{part}{t}")
            def _():
                if part == 1 and t == 0:
                    w.finish(acted)
                rows = pl.ds(pl.multiple_of(my_rows + 256 * t, 256), 256)
                here = pl.ds(256 * t, 256)
                gate = _nt(sec2[rows, :], buf[0])
                up = _nt(sec2[rows, :], buf[1])
                d_hidden = _nt(dy2[rows, :], buf[2])
                sigmoid = 1.0 / (1.0 + jnp.exp(-gate))
                silu = gate * sigmoid
                d_gate = (d_hidden * up * (sigmoid + silu * (1.0 - sigmoid))).astype(BF)
                d_up = (d_hidden * silu).astype(BF)
                hidden = (silu * up).astype(BF)
                for n, value in enumerate((d_gate, d_up, hidden)):
                    acts[n, rows, :] = value[:, 0:second]
                    asend[n, here, 0:count] = value[:, second : second + count]
                lanes = pl.ds(0, second)
                acted.append(w.send(asend.at[:, here, lanes], acts.at[:, rows], sib, s_act[part]))
                d_second = _nn(d_gate, buf[0]) + _nn(d_up, buf[1])
                result = _nn(hidden, buf[2])
                if part == 1:
                    d_second = d_second + dsb[here, :].astype(F32)
                    result = result + osb[here, :].astype(F32)
                dsb[here, :] = d_second.astype(BF)
                osb[here, :] = result.astype(BF)
                if part == 1:
                    sum_ds.over_x(t)

        @step(f"wg{part}_in")
        def _():
            w.finish(held[part])
            w.arrived(acts.at[:, pl.ds(0, 512)], s_act[part])
            if part == 0:
                w.arrived(sec2.at[pl.ds(0, 512)], s_sec)
                w.arrived(dy2.at[pl.ds(0, 512)], s_dy)

        def weight_grads(kind):
            @step(f"wg{part}{kind}")
            def _():
                right = dy2 if kind == 2 else sec2

                def columns(n, carry):
                    cols = pl.ds(pl.multiple_of(n * 512, 512), 512)
                    buf[kind, 0:count, cols] = _tn(acts[kind], right[:, cols])[0:count, :].astype(BF)
                    return carry

                lax.fori_loop(0, 2, columns, 0)

        def send_grads(slot, to_slot):
            @step(f"gr{part}_y{to_slot}")
            def _():
                rows = buf.at[:, pl.ds(rows_kept * slot, rows_kept)]
                w.send(rows, gr.at[to_slot, :, span], yp, s_gr[to_slot][part])

        @step(f"gr{part}_z")
        def _():
            w.arrived(gr.at[1, :, span], s_gr[1][part])
            for kind in range(3):
                gs[kind, span, :] = (
                    buf[kind, 2 * rows_kept : 3 * rows_kept, :].astype(F32) + gr[1, kind, span, :].astype(F32)
                ).astype(BF)
            w.send(gs.at[:, span], gt.at[:, span], zp, s_gt[part])

        @step(f"gr{part}_end")
        def _():
            w.arrived(gr.at[0, :, span], s_gr[0][part])
            w.arrived(gt.at[:, span], s_gt[part])
            for kind in range(3):
                o_ffn[kind, span, :] = (
                    buf[kind, 0:rows_kept, :].astype(F32)
                    + gr[0, kind, span, :].astype(F32) + gt[kind, span, :].astype(F32)
                )

        feed_forward(0)
        feed_forward(1)
        for kind in range(3):
            weight_grads(kind)
        send_grads(3, 1)
        send_grads(1, 0)

    part_steps(0)
    part_steps(1)

    s_dm, s_da, s_das = w.sem(), many(3), w.sem()
    terms = {"ffn": jnp.zeros((1, 1024), F32), "attn": jnp.zeros((1, 1024), F32)}

    def state_steps(t):
        @step(f"st{t}")
        def _():
            start = 256 * t + 64 * mine
            rows = pl.ds(pl.multiple_of(start, 64), 64)
            state = x[rows, :].astype(F32) + attended_rows(rows)
            bos[t] = state
            scale = lax.rsqrt(jnp.mean(state * state, axis=1, keepdims=True) + EPS)
            normed = state * scale
            total = sum_ds.result(t)
            terms["ffn"] = terms["ffn"] + jnp.sum(total * normed, axis=0, keepdims=True)
            weighted = total * ffn_gain()
            inner = jnp.mean(weighted * normed, axis=1, keepdims=True)
            grad = dy2[pl.ds(pl.multiple_of(my_rows + start, 64), 64), :].astype(F32) + scale * (weighted - normed * inner)
            dstate[t] = grad
            low_grad = grad.astype(BF)
            daf[k, t, mine] = low_grad
            for n in range(4):
                dmb[t, :, 256 * n : 256 * (n + 1)] = _nt(low_grad, wall[n].reshape(256, 1024)).astype(BF)
            for d, e in others:
                lanes = pl.ds(pl.multiple_of(LANES * (2 * chips[d] + cores[e]), LANES), LANES)
                w.send(dmb.at[t, :, lanes], dmix.at[k, t, mine], quad(d, e), s_dm)
            w.local(dmb.at[t, :, head_lanes], dmix.at[k, t, mine], s_dm)

    state_steps(0)
    state_steps(1)

    @step("da_out")
    def _():
        for d in (2, 1):
            w.send(daf.at[k, :, mine], daf.at[k, :, mine], quad(d, 0), s_da[d - 1])

    @step("da_fwd")
    def _():
        far = piece(chips[2])
        w.arrived(daf.at[k, :, far], s_da[1])
        w.send(daf.at[k, :, far], daf.at[k, :, far], quad(1, 0), s_da[2])

    @step("da_sib")
    def _():
        for d in (1, 3):
            w.arrived(daf.at[k, :, mine], s_da[d - 1])
        w.send(daf.at[k], daf.at[k], sib, s_das)

    home = zh + k * (1 - 2 * zh)

    def send_home(buf, into, sem):
        w.send(buf.at[1 - home, 0], into.at[zh, k], zp, sem)
        w.send(buf.at[1 - home, 1], into.at[zh, k], zps, sem)
        w.send(buf.at[home, 1], into.at[zh, k], sib, sem)
        w.local(buf.at[home, 0], into.at[zh, k], sem)

    s_bo, s_tg = w.sem(), w.sem()

    @step("block")
    def _():
        for t in range(2):
            total = bos[t] + sum_os.result(t)
            obs[t] = total.astype(BF).reshape(2, 32, 1024)
        send_home(obs, bor, s_bo)

    @step("block_end")
    def _():
        w.arrived(bor, s_bo)
        o_block[...] = bor[...]

    @step("bw_in")
    def _():
        w.arrived(dmix, s_dm)
        dkk[...] = jnp.zeros_like(dkk)
        dvv[...] = jnp.zeros_like(dvv)

    def backward_tile(t):
        @step(f"bw{t}")
        def _():
            lo, n = 256 * t, 256 * (t + 1)
            d_out = dmix[...].reshape(1024, LANES)[lo : lo + 256, :].astype(F32)
            product = d_out * att[lo : lo + 256, :]
            results = []
            for h, q in enumerate((q0, q1)):
                here = low if h == 0 else jnp.logical_not(low)
                d_head = jnp.where(here, d_out, 0.0).astype(BF)
                delta = jnp.sum(jnp.where(here, product, 0.0), axis=1, keepdims=True)
                weights = prob[h, lo : lo + 256, 0:n]
                pulled = _nt(d_head, vv[0:n, :])
                d_scores = (weights.astype(F32) * (pulled - delta)).astype(BF)
                results.append(_nn(d_scores, kk[0:n, :]))
                dkk[0:n, :] += _tn(d_scores, q[lo : lo + 256, :])
                dvv[0:n, :] += _tn(weights, d_head)
            dqq[lo : lo + 256, :] = jnp.where(low, results[0], results[1]) * (HEAD_DIM**-0.5)

    for t in range(4):
        backward_tile(t)
    s_dpx = w.sem()

    @step("back")
    def _():
        query_weight, key_weight = query_gain(), key_gain()

        def back_rows(t, carry):
            query_sum, key_sum = carry
            rows = pl.ds(pl.multiple_of(t * 256, 256), 256)
            cosine, sine = cos_t[rows, :], sin_t[rows, :]
            query = raw[rows, 0:LANES]
            both = raw[rows, LANES : 2 * LANES]

            def through(values, grads, gain_row):
                scale = inverse_root(values)
                normed = values * scale
                grads = grads * cosine - swap(grads) * sine
                weighted = grads * gain_row
                inner = head_sum(weighted * normed) * (1.0 / HEAD_DIM)
                return scale * (weighted - normed * inner), jnp.sum(grads * normed, axis=0, keepdims=True)

            query_back, query_term = through(query, dqq[rows, :], query_weight)
            d_key = dkk[rows, :]
            d_key = d_key + pltpu.roll(d_key, HALF_LANES, 1)
            key_back, key_term = through(both, d_key, key_weight)
            d_value = dvv[rows, :]
            d_value = d_value + pltpu.roll(d_value, HALF_LANES, 1)
            dpj[rows, 0:LANES] = query_back.astype(BF)
            dpj[rows, LANES : 2 * LANES] = jnp.where(low, key_back, d_value).astype(BF)
            return query_sum + query_term, key_sum + key_term

        zero_row = jnp.zeros((1, LANES), F32)
        query_sum, key_sum = lax.fori_loop(0, 4, back_rows, (zero_row, zero_row))
        w.send(dpj.at[pl.ds(other_rows, 512)], dpx, sib, s_dpx)
        gg[:, 2 * LANES : 3 * LANES] = jnp.zeros((8, LANES), F32)
        gg[0:1, 2 * LANES : 3 * LANES] = query_sum + pltpu.roll(query_sum, HALF_LANES, 1)
        gg[1:2, 2 * LANES : 3 * LANES] = key_sum

    def first_steps(t):
        @step(f"df{t}")
        def _():
            if t == 0:
                w.arrived(dpx, s_dpx)
            here = pl.ds(256 * t, 256)
            rows = pl.ds(pl.multiple_of(my_rows + 256 * t, 256), 256)
            dfb[here, :] = (_nn(dpj[rows, :], w2[own_head, :]) + _nn(dpx[here, :], w2[sib_head, :])).astype(BF)
            sum_df.over_x(t)

    first_steps(0)
    first_steps(1)
    s_back = w.sem()

    def term_steps(name, rows, value):
        sem = many(3)

        @step(f"{name}_y")
        def _():
            term = value()
            count = rows.stop - rows.start
            for p in range(4):
                igs[p, rows, :] = term[count * p : count * (p + 1), :].astype(BF)
            at = pl.ds(rows.start, count)
            w.send(igs.at[team_d, at], agr.at[1, at], yp, sem[1])
            w.send(igs.at[team_y, at], agr.at[0, at], yp, sem[0])

        at = pl.ds(rows.start, rows.stop - rows.start)

        @step(f"{name}_z")
        def _():
            w.arrived(agr.at[1, at], sem[1])
            agz[rows, :] = (igs[team_z, rows, :].astype(F32) + agr[1, rows, :].astype(F32)).astype(BF)
            w.send(agz.at[at], agt.at[at], zp, sem[2])

        @step(f"{name}_sum")
        def _():
            w.arrived(agr.at[0, at], sem[0])
            w.arrived(agt.at[at], sem[2])
            agh[rows, :] = (
                igs[team, rows, :].astype(F32) + agr[0, rows, :].astype(F32) + agt[rows, :].astype(F32)
            ).astype(BF)

    def in_value():
        w.arrived(first2.at[pl.ds(0, 512)], s_first)
        return _tn(dpj[...], first2[...])

    def out_value():
        w.arrived(daf.at[0], s_das)
        return _tn(mxs[...], daf[...].reshape(1024, 1024))

    term_steps("in", slice(0, 64), in_value)
    term_steps("out", slice(64, 96), out_value)
    give = pltpu.make_async_remote_copy(
        src_ref=agh, dst_ref=ago, send_sem=w.sem(), recv_sem=s_back, device_id=owner_of, device_id_type=MESH,
    )

    @step("give")
    def _():
        pl.when(apart)(give.start)
        pl.when(alone)(lambda: pltpu.make_async_copy(agh, ago, s_back).start())

    @step("given")
    def _():
        w.arrived(ago, s_back)
        o_in[...] = ago[0:64, :]
        o_out[...] = ago[64:96, :]

    def token_steps(t):
        @step(f"tg{t}")
        def _():
            rows = pl.ds(pl.multiple_of(256 * t + 64 * mine, 64), 64)
            values = x[rows, :].astype(F32)
            scale = lax.rsqrt(jnp.mean(values * values, axis=1, keepdims=True) + EPS)
            normed = values * scale
            total = sum_df.result(t)
            terms["attn"] = terms["attn"] + jnp.sum(total * normed, axis=0, keepdims=True)
            weighted = total * attn_gain()
            inner = jnp.mean(weighted * normed, axis=1, keepdims=True)
            grad = dstate[t] + scale * (weighted - normed * inner)
            tgs[t] = grad.astype(BF).reshape(2, 32, 1024)

    token_steps(0)
    token_steps(1)

    @step("tok_home")
    def _():
        send_home(tgs, tgr, s_tg)

    @step("tok_end")
    def _():
        w.arrived(tgr, s_tg)
        o_tokens[...] = tgr[...]

    s_gg, s_gt4 = w.sem(), many(3)

    @step("gg_out")
    def _():
        for n in range(8):
            gg[n : n + 1, 0:LANES] = terms["attn"][:, LANES * n : LANES * (n + 1)]
            gg[n : n + 1, LANES : 2 * LANES] = terms["ffn"][:, LANES * n : LANES * (n + 1)]
        for d, e in others:
            w.send(gg, ggq.at[g], quad(d, e), s_gg)
        w.local(gg, ggq.at[g], s_gg)

    @step("gg_sum")
    def _():
        w.arrived(ggq, s_gg)
        total = ggq[0]
        for n in range(1, 8):
            total = total + ggq[n]
        gsum[...] = total
        for n, peer in enumerate((yp, zp, diag)):
            w.send(gsum, ggt.at[n], peer, s_gt4[n])

    @step("gg_end")
    def _():
        total = gsum[...]
        for n in range(3):
            w.arrived(ggt.at[n], s_gt4[n])
            total = total + ggt[n]
        gflat[0:8, :] = total[:, 0:LANES]
        gflat[8:16, :] = total[:, LANES : 2 * LANES]
        key_part = pltpu.roll(total[1:2, 2 * LANES : 3 * LANES], HALF_LANES, 1)
        gflat[16:17, :] = jnp.where(low_row, total[0:1, 2 * LANES : 3 * LANES], key_part)
        place = 68 * (8 * team + g)
        line, shift = lax.div(place, LANES), lax.rem(place, LANES)
        back = lax.rem(LANES - shift, LANES)
        left = pltpu.roll(gflat[pl.ds(line, 1), :], back, 1)
        right = pltpu.roll(gflat[pl.ds(line + 1, 1), :], back, 1)
        o_gain[...] = jnp.where(lane < LANES - shift, left, right)[:, 0:68]

    for name in ORDER:
        steps.pop(name)()
    assert not steps, sorted(steps)
    w.finish()
    for half, away in late:
        pl.when(k != half)(away.wait_send)
    pl.when(apart)(move.wait_send)
    pl.when(apart)(give.wait_send)


ORDER = (
    "tok_own1", "tok_out0", "tok_out1", "gain_start", "move", "tok_own0", "tok_rel0", "wout_start",
    "gain_pass", "moved", "win_start", "cot_out1", "tok_rel1", "tok_fwd0", "wout_pass", "u0_own", "gain_end",
    "cot_own0", "cot_own1", "win_pass", "tok_fwd1", "u0_z0", "win_end", "u1_y", "wout_end", "gains",
    "project", "u0_z2", "cot_out0", "rotate", "at2", "at0", "u0_z1", "u0_y", "cot_fwd0", "u0_f0", "at3",
    "wout_fwd", "u1_s1", "at1", "u1_own", "cot_rel0", "u0_f2", "u0_f1", "u0_s1", "mix_fwd0", "cot_rel1",
    "u1_z0", "u1_z1", "wout_sib", "mix_fwd1", "cot_fwd1", "u0_s3", "u1_f0", "u1_z2", "second", "u0_all",
    "u1_f1", "dy", "ff00", "u1_f2", "ff01", "wg0_in", "wg00", "u1_s3", "wg02", "u1_all", "wg01", "gr0_y1",
    "ff10", "ff11", "wg1_in", "wg11", "wg12", "wg10", "ds_z0", "ds_z1", "gr1_y1", "first_sib", "gr0_y0",
    "os_x0", "gr0_z", "st0", "os_x1", "st1", "da_out", "os_z0", "os_z1", "bw_in", "gr1_z", "bw1", "bw3",
    "gr0_end", "da_fwd", "bw0", "bw2", "back", "in_y", "df0", "df1", "da_sib", "df_z0", "in_z", "out_y",
    "df_z1", "out_z", "block", "in_sum", "tg0", "gr1_y0", "tg1", "gg_out", "out_sum", "give", "tok_home",
    "gr1_end", "gg_sum", "tok_end", "block_end", "gg_end", "given",
)


TEAM_SCRATCH = (
    ((512, 1024), BF), ((2, 32, 1024), BF), ((2, 32, 1024), BF), ((512, 1024), BF),
    ((4, 4, 2, 32, 1024), BF), ((3, 704, 1024), BF), ((3, 512, 1024), BF), ((4, 8, 8, 128), F32), ((8, 1024), F32),
    ((1024, 1024), BF), ((1024, 256), F32), ((512, 256), F32),
    ((1024, 128), BF), ((1024, 128), BF), ((1024, 128), BF), ((1024, 128), BF), ((2, 1024, 1024), BF),
    ((1024, 128), F32), ((1024, 128), BF), ((512, 1024), BF), ((1024, 1024), BF), ((1024, 1024), BF),
    ((3, 1024, 384), BF), ((3, 1024, 256), BF), ((3, 512, 384), BF),
    ((512, 1024), BF), ((512, 1024), BF), ((3, 2, 64, 1024), BF), ((3, 2, 64, 1024), BF), ((3, 2, 64, 1024), BF),
    ((2, 3, 144, 1024), BF), ((3, 144, 1024), BF), ((3, 144, 1024), BF),
    ((2, 64, 1024), F32), ((2, 64, 1024), BF), ((2, 2, 4, 64, 1024), BF), ((2, 2, 4, 64, 128), BF),
    ((1024, 128), F32), ((1024, 128), F32), ((1024, 128), F32), ((1024, 256), BF), ((512, 256), BF),
    ((512, 1024), BF), ((3, 2, 64, 1024), BF),
    ((4, 96, 1024), BF), ((2, 96, 1024), BF), ((96, 1024), BF), ((96, 1024), BF), ((96, 1024), BF), ((96, 1024), BF),
    ((2, 64, 1024), F32), ((2, 2, 32, 1024), BF), ((2, 2, 32, 1024), BF), ((2, 2, 32, 1024), BF),
    ((2, 2, 32, 1024), BF),
    ((8, 384), F32), ((8, 8, 384), F32), ((8, 384), F32), ((3, 8, 384), F32), ((8, 128), F32), ((24, 128), F32), ((1024, 8), F32), ((8, 1024), F32),
)


def rotary_lanes(rows):
    width = HEAD_DIM // 2
    freq = (ROPE_BASE ** (-np.arange(width, dtype=np.float32) * np.float32(2.0 / HEAD_DIM))).astype(np.float32)
    angle = (np.arange(rows, dtype=np.float32)[:, None] * freq).astype(np.float32).astype(np.float64)
    cosine, sine = np.cos(angle), np.sin(angle)
    return (
        np.tile(np.concatenate([cosine, cosine], 1), (1, 2)).astype(np.float32),
        np.tile(np.concatenate([-sine, sine], 1), (1, 2)).astype(np.float32),
    )


def on_team(tokens, segments, lengths, attn_in, attn_out, gains, ffn_weights, cotangent):
    batches, block_len, halves, width = tokens.shape
    rows = segments.shape[1]
    cosine, sine = rotary_lanes(2 * rows)
    args = (
        tokens.transpose(0, 2, 1, 3),
        cotangent.transpose(0, 2, 1, 3),
        attn_in,
        attn_out,
        gains[None],
        ffn_weights.transpose(1, 0, 2),
        segments.transpose(0, 2, 1),
        lengths,
        jnp.asarray(cosine),
        jnp.asarray(sine),
    )
    vmem = pl.BlockSpec(memory_space=pltpu.VMEM)
    outs = pl.pallas_call(
        block_kernel,
        out_shape=(
            jax.ShapeDtypeStruct((2, 2, 32, 1024), BF),
            jax.ShapeDtypeStruct((2, 2, 32, 1024), BF),
            jax.ShapeDtypeStruct((64, 1024), BF),
            jax.ShapeDtypeStruct((32, 1024), BF),
            jax.ShapeDtypeStruct((1, 68), F32),
            jax.ShapeDtypeStruct((3, 144, 1024), F32),
        ),
        in_specs=[vmem] * 7 + [pl.BlockSpec(memory_space=pltpu.SMEM)] + [vmem] * 2,
        out_specs=(vmem,) * 6,
        scratch_shapes=[pltpu.VMEM(shape, kind) for shape, kind in TEAM_SCRATCH]
        + [pltpu.SemaphoreType.DMA((COPIES,))],
        compiler_params=pltpu.CompilerParams(
            collective_id=0, has_side_effects=True, vmem_limit_bytes=VMEM_BYTES
        ),
    )(*args)
    block, token_grad, in_grad, out_grad, gain_grad, unit_grad = outs
    return (
        block.transpose(0, 2, 1, 3),
        token_grad.transpose(0, 2, 1, 3).astype(F32),
        in_grad.astype(F32),
        out_grad.astype(F32),
        gain_grad[0],
        unit_grad.transpose(1, 0, 2),
    )


VMEM_BYTES = 62 << 20


def solution(mesh):
    dp, ctx = mesh.devices.shape
    if ctx == 2 * KV_HEADS:
        ring = "ctx"
        every = ("dp", "ctx")
        team, run = mesh, on_team
    else:
        ring = ("s", "q", "g")
        every = EVERY
        team = Mesh(mesh.devices.reshape(dp, 2, ctx // (2 * KV_HEADS), KV_HEADS), EVERY)
        run = on_device
    placed = (
        P("dp", ring, None, None),
        P("dp", None, None),
        P("dp"),
        P(every, None),
        P(every, None),
        P(every),
        P(every, None, None),
        P("dp", ring, None, None),
    )
    return jax.shard_map(
        run,
        mesh=team,
        in_specs=placed,
        out_specs=(
            P("dp", ring, None, None),
            P("dp", ring, None, None),
            P(every, None),
            P(every, None),
            P(every),
            P(every, None, None),
        ),
        check_vma=False,
    )
```

```python
import jax
import jax.numpy as jnp
import numpy as np
from jax import lax
from jax.experimental import pallas as pl
from jax.experimental.pallas import tpu as pltpu
from jax.sharding import Mesh
from jax.sharding import PartitionSpec as P

FF = 4608
HEADS = 16
KV_HEADS = 8
HEAD_DIM = 64
GROUP = HEADS // KV_HEADS
QKV_ROWS = 2048

EPS = 1e-05
ROPE_BASE = 1000000.0
MASKED = -1e30
BF = jnp.bfloat16
F32 = jnp.float32


def root_mean(values):
    return lax.rsqrt(jnp.mean(values * values, axis=-1, keepdims=True) + EPS)


def rotate(values, cosine, sine):
    width = values.shape[-1] // 2
    first = values[..., :width]
    second = values[..., width:]
    return jnp.concatenate(
        [first * cosine - second * sine, second * cosine + first * sine], axis=-1
    )


def tables(positions):
    width = HEAD_DIM // 2
    freq = ROPE_BASE ** (-jnp.arange(width, dtype=F32) * 2.0 / HEAD_DIM)
    angle = positions.astype(F32)[..., None] * freq
    return (jnp.cos(angle), jnp.sin(angle))


def prepare(query_raw, key_raw, query_gain, key_gain, cosine, sine):
    query_norm = query_raw * root_mean(query_raw) * query_gain
    key_norm = key_raw * root_mean(key_raw) * key_gain
    return (
        rotate(query_norm, cosine[:, None], sine[:, None]),
        rotate(key_norm, cosine, sine),
    )


def norm_back(grad, normed, scale_rows, gain):
    weighted = grad * gain
    inner = jnp.mean(weighted * normed, axis=-1, keepdims=True)
    return (scale_rows * (weighted - normed * inner), jnp.sum(grad * normed, axis=0))


def dot(a, b, ca, cb):
    return lax.dot_general(a, b, (((ca,), (cb,)), ((), ())), preferred_element_type=F32)


TEAM = ("dp", "s", "q")
EVERY = ("dp", "s", "q", "g")


def spread(local, block_len):
    mine = lax.all_to_all(local, "s", 0, 0, tiled=True)
    return lax.all_gather(mine, "g", axis=0, tiled=False)


def on_device(tokens, segments, lengths, attn_in, attn_out, gains, ffn_weights, cotangent):
    batches, block_len, halves, width = tokens.shape
    seq = lax.axis_index("s")
    quarter = lax.axis_index("q")
    head = lax.axis_index("g")
    quarters = lax.axis_size("q")
    heads = lax.axis_size("g")
    ctx_count = 2 * quarters * heads
    scale = HEAD_DIM ** (-0.5)
    weight_in = lax.all_gather(attn_in, EVERY, axis=0, tiled=True)
    weight_out = lax.all_gather(attn_out, EVERY, axis=0, tiled=True)
    gain_all = lax.all_gather(gains, EVERY, axis=0, tiled=True).astype(F32)
    attn_gain = gain_all[:width]
    ffn_gain = gain_all[width : 2 * width]
    query_gain = gain_all[2 * width : 2 * width + HEAD_DIM]
    key_gain = gain_all[2 * width + HEAD_DIM :]
    head_rows = (GROUP + 2) * HEAD_DIM
    out_rows = GROUP * HEAD_DIM
    weight_head = lax.dynamic_slice_in_dim(weight_in, head * head_rows, head_rows, 0)
    weight_mix = lax.dynamic_slice_in_dim(weight_out, head * out_rows, out_rows, 0)

    inputs = spread(tokens, block_len)
    count = inputs.size // width
    inputs = inputs.reshape(count, width).astype(F32)
    cot = spread(cotangent, block_len).reshape(count, width).astype(F32)

    def places(which):
        owner_g = jnp.arange(heads, dtype=jnp.int32)[:, None, None, None]
        owner_s = jnp.arange(2, dtype=jnp.int32)[None, :, None, None]
        row = jnp.arange(block_len, dtype=jnp.int32)[None, None, :, None]
        half = jnp.arange(2, dtype=jnp.int32)[None, None, None, :]
        owner = owner_s * (quarters * heads) + which * heads + owner_g
        block = jnp.where(half == 0, owner, 2 * ctx_count - 1 - owner)
        return (
            (block * block_len + row).reshape(count),
            jnp.broadcast_to((owner * block_len + row) * 2 + half, (heads, 2, block_len, 2)).reshape(count),
        )

    docs = lax.dynamic_index_in_dim(segments, seq, 0, False).reshape(-1)
    length = lax.dynamic_index_in_dim(lengths, seq, 0, False)
    place, slot = places(quarter)
    key_place, key_slot = jax.vmap(places)(jnp.arange(quarters, dtype=jnp.int32))
    key_place = key_place.reshape(-1)
    query_doc = docs[slot]
    key_doc = docs[key_slot.reshape(-1)]
    causal = key_place[None, :] <= place[:, None]
    live = (key_place[None, :] < length) | (key_place[None, :] == place[:, None])
    mask = causal & live & (query_doc[:, None] == key_doc[None, :])
    valid = (place < length).astype(F32)[:, None]

    first_scale = root_mean(inputs)
    first_normed = inputs * first_scale
    first = (first_normed * attn_gain).astype(BF)
    projected = dot(first, weight_head, 1, 1).reshape(count, GROUP + 2, HEAD_DIM)
    cosine, sine = tables(place)

    def prepare_here(query_raw, key_raw, gain_query, gain_key):
        return prepare(query_raw, key_raw, gain_query, gain_key, cosine, sine)

    (query_rot, key_rot), prepare_pull = jax.vjp(
        prepare_here, projected[:, :GROUP], projected[:, GROUP], query_gain, key_gain
    )
    queries = query_rot.astype(BF)
    pair = jnp.stack([key_rot.astype(BF), projected[:, GROUP + 1].astype(BF)])
    pair = lax.all_gather(pair, "q", axis=1, tiled=True)
    keys, values = pair[0], pair[1]

    scores = jnp.einsum("qjd,kd->jqk", queries, keys, preferred_element_type=F32) * scale
    scores = jnp.where(mask[None], scores, MASKED)
    peak = jnp.max(scores, axis=-1, keepdims=True)
    expo = jnp.where(mask[None], jnp.exp(scores - peak), 0.0)
    weights = expo / jnp.sum(expo, axis=-1, keepdims=True)
    attended = jnp.einsum("jqk,kd->qjd", weights.astype(BF), values, preferred_element_type=F32)
    mixed_here = attended.astype(BF).reshape(count, out_rows)
    mixed = lax.all_gather(mixed_here, "g", axis=1, tiled=True)
    state = inputs + dot(mixed, weight_out, 1, 0)
    second_scale = root_mean(state)
    second_normed = state * second_scale
    second = (second_normed * ffn_gain).astype(BF)
    grad_out = cot * valid
    grad_low = grad_out.astype(BF)

    units = lax.all_gather(ffn_weights, TEAM, axis=0, tiled=True)
    unit_gate, unit_up, unit_down = units[:, 0], units[:, 1], units[:, 2]
    gate = dot(second, unit_gate, 1, 1)
    upward = dot(second, unit_up, 1, 1)
    sigmoid = jax.nn.sigmoid(gate)
    hidden = (gate * sigmoid * upward).astype(BF)
    d_hidden = dot(grad_low, unit_down, 1, 1)
    d_gate = (d_hidden * upward * sigmoid * (1.0 + gate * (1.0 - sigmoid))).astype(BF)
    d_up = (d_hidden * gate * sigmoid).astype(BF)
    d_second = dot(d_gate, unit_gate, 1, 0) + dot(d_up, unit_up, 1, 0)
    own = count // heads

    def gathered(values):
        return lax.psum_scatter(values.astype(BF), "g", scatter_dimension=0, tiled=True).astype(F32)

    def own_rows(values):
        return lax.dynamic_slice_in_dim(values, head * own, own, 0)

    def home(values):
        back = values.reshape(2, block_len, halves, width)
        return lax.all_to_all(back, "s", 0, 0, tiled=True)

    ffn_sum = gathered(dot(hidden, unit_down, 1, 0))
    block_out = home((own_rows(state) + ffn_sum).astype(BF))
    ffn_grad = lax.psum_scatter(
        jnp.stack([dot(d_gate, second, 0, 0), dot(d_up, second, 0, 0), dot(hidden, grad_low, 0, 0)], axis=1),
        TEAM,
        scatter_dimension=0,
        tiled=True,
    )
    norm_grad, ffn_gain_grad = norm_back(
        gathered(d_second), own_rows(second_normed), own_rows(second_scale), ffn_gain
    )
    state_grad = own_rows(grad_out) + norm_grad
    attended_grad = lax.all_gather(state_grad.astype(BF), "g", axis=0, tiled=True)
    mixed_grad = dot(attended_grad, weight_mix, 1, 1).astype(BF)
    out_term = dot(mixed_here, attended_grad, 0, 0)
    mixed_grad = mixed_grad.reshape(count, GROUP, HEAD_DIM)
    delta = jnp.sum(mixed_grad.astype(F32) * attended, axis=-1).T[:, :, None]
    pulled = jnp.einsum("qjd,kd->jqk", mixed_grad, values, preferred_element_type=F32)
    score_grad = (weights * (pulled - delta)).astype(BF)
    query_grad = jnp.einsum("jqk,kd->qjd", score_grad, keys, preferred_element_type=F32) * scale
    key_grad = jnp.einsum("jqk,qjd->kd", score_grad, queries, preferred_element_type=F32) * scale
    value_grad = jnp.einsum("jqk,qjd->kd", weights.astype(BF), mixed_grad, preferred_element_type=F32)
    if quarters > 1:
        key_grad = lax.psum_scatter(key_grad, "q", scatter_dimension=0, tiled=True)
        value_grad = lax.psum_scatter(value_grad, "q", scatter_dimension=0, tiled=True)
    query_raw_grad, key_raw_grad, query_gain_grad, key_gain_grad = prepare_pull((query_grad, key_grad))
    projected_grad = jnp.concatenate(
        [query_raw_grad.reshape(count, out_rows), key_raw_grad, value_grad], axis=1
    ).astype(BF)
    first_grad = gathered(dot(projected_grad, weight_head, 1, 0))
    in_term = dot(projected_grad, first, 0, 0)
    input_norm_grad, attn_gain_grad = norm_back(
        first_grad, own_rows(first_normed), own_rows(first_scale), attn_gain
    )
    tokens_grad = home(state_grad + input_norm_grad)
    gain_term = jnp.concatenate([attn_gain_grad, ffn_gain_grad, query_gain_grad, key_gain_grad])

    def placed(term, rows):
        whole = jnp.zeros((rows, width), F32)
        return lax.dynamic_update_slice_in_dim(whole, term, head * term.shape[0], 0)

    return (
        block_out,
        tokens_grad,
        lax.psum_scatter(placed(in_term, QKV_ROWS), EVERY, scatter_dimension=0, tiled=True),
        lax.psum_scatter(placed(out_term, HEADS * HEAD_DIM), EVERY, scatter_dimension=0, tiled=True),
        lax.psum_scatter(gain_term, EVERY, scatter_dimension=0, tiled=True),
        ffn_grad,
    )


LANES = 128
HALF_LANES = 64


def _nt(a, b):
    return lax.dot_general(a, b, (((1,), (1,)), ((), ())), preferred_element_type=F32)


def _nn(a, b):
    return lax.dot_general(a, b, (((1,), (0,)), ((), ())), preferred_element_type=F32)


def _tn(a, b):
    return lax.dot_general(a, b, (((0,), (0,)), ((), ())), preferred_element_type=F32)


MESH = pl.DeviceIdType.MESH
COPIES = 400


class Wires:
    def __init__(self, sems):
        self.sems = sems
        self.used = 0
        self.pending = []

    def sem(self):
        self.used += 1
        return self.sems.at[self.used - 1]

    def send(self, src, dst, to, arrives):
        copy = pltpu.make_async_remote_copy(
            src_ref=src, dst_ref=dst, send_sem=self.sem(), recv_sem=arrives,
            device_id=to, device_id_type=MESH,
        )
        copy.start()
        self.pending.append(copy)
        return copy

    def local(self, src, dst, arrives):
        copy = pltpu.make_async_copy(src, dst, arrives)
        copy.start()
        return copy

    def arrived(self, ref, sem):
        pltpu.make_async_copy(ref, ref, sem).wait()

    def finish(self, copies=None):
        copies = list(self.pending if copies is None else copies)
        for copy in copies:
            copy.wait_send()
        done = {id(copy) for copy in copies}
        self.pending = [copy for copy in self.pending if id(copy) not in done]


def block_kernel(
    tok, cot, win, wout, gain_in, wffn, segments, lengths, cos_t, sin_t,
    o_block, o_tokens, o_in, o_out, o_gain, o_ffn,
    x, rel_t, rel_c, w2, wall, wfa, wfb, gb, grow, first2, raw, po,
    q0, q1, kk, vv, prob, att, mxs, mix, sec2, dy2, acta, actb, asend,
    dsb, osb, dsr, osr, rsz, gr, gs, gt, dstate, dmb, daf, dmix,
    dkk, dvv, dqq, dpj, dpx, dfb, dfr, igs, agr, agz, agt, agh, ago,
    bos, obs, bor, tgs, tgr, gg, ggq, gsum, ggt, gain, gflat, doc_col, doc_row, sems,
):
    dp = lax.axis_index("dp")
    c = lax.axis_index("ctx")
    zh = lax.div(c, 8)
    g = lax.rem(c, 8)
    j = lax.div(g, 2)
    k = lax.rem(c, 2)
    chips = (j, j + 1 - 2 * lax.rem(j, 2), j + 2 - 4 * lax.div(j, 2), 3 - j)
    cores = (k, 1 - k)

    def quad(d, e):
        return (dp, zh * 8 + 2 * chips[d] + cores[e])

    sib = quad(0, 1)
    czp = lax.rem(c + 8, 16)
    zp = (dp, lax.rem(c + 8, 16))
    zps = (dp, 8 * (1 - zh) + 2 * j + 1 - k)
    yp = (1 - dp, c)
    diag = (1 - dp, lax.rem(c + 8, 16))
    team = 2 * dp + zh
    team_y = 2 * (1 - dp) + zh
    team_z = 2 * dp + 1 - zh
    team_d = 3 - team
    w = Wires(sems)
    others = [(d, e) for d in range(4) for e in range(2) if (d, e) != (0, 0)]

    zl, xx = lax.div(j, 2), lax.rem(j, 2)
    keeper = (xx, 8 * k + 4 * dp + 2 * zh + zl)
    owner_of = (zl, 8 * xx + 4 * k + 2 * dp + zh)
    alone = jnp.logical_and(keeper[0] == dp, keeper[1] == c)
    apart = jnp.logical_not(alone)

    barrier = pltpu.get_barrier_semaphore()
    peers = [quad(d, e) for d, e in others] + [zp, zps, yp, diag]
    for peer in peers:
        pl.semaphore_signal(barrier, inc=1, device_id=peer, device_id_type=MESH)

    limit = lengths[zh]
    docs = segments[zh].astype(F32).astype(BF)
    line = lax.broadcasted_iota(jnp.int32, (512, 512), 0)
    cell = lax.broadcasted_iota(jnp.int32, (512, 512), 1)
    same_place = (line == cell).astype(F32).astype(BF)
    mirrored = (line + 480 - 2 * (line - lax.rem(line, 32)) == cell).astype(F32).astype(BF)
    for half, order in enumerate((same_place, mirrored)):
        ids = jnp.broadcast_to(docs[half : half + 1, :], (16, 512))
        key = lax.broadcasted_iota(jnp.int32, (1, 512), 1) + 512 * half
        doc_row[0:1, 512 * half : 512 * (half + 1)] = jnp.where(key < limit, _nn(ids, order)[0:1, :], -1.0)
        doc_col[512 * half : 512 * (half + 1), :] = _nt(order, ids)[:, 0:8]
    gain[...] = jnp.zeros_like(gain)
    gain[0:1, 0:68] = gain_in[...].astype(F32)

    @pl.when(apart)
    def _():
        pl.semaphore_signal(barrier, inc=1, device_id=keeper, device_id_type=MESH)
        pl.semaphore_signal(barrier, inc=1, device_id=owner_of, device_id_type=MESH)
        pl.semaphore_wait(barrier, len(peers) + 2)

    @pl.when(alone)
    def _():
        pl.semaphore_wait(barrier, len(peers))

    def many(*shape):
        return [many(*shape[1:]) for _ in range(shape[0])] if shape else w.sem()

    def piece(chip):
        return chip + k * (3 - 2 * chip)

    def row_block(owner, half):
        return owner + half * (15 - 2 * owner)

    my_rows = pl.multiple_of(512 * k, 512)
    other_rows = pl.multiple_of(512 * (1 - k), 512)
    own_head, sib_head = pl.ds(0, 256), pl.ds(256, 256)
    mine = piece(j)
    steps = {}

    def step(name):
        def keep(body):
            steps[name] = body
            return body
        return keep

    def rows_of(buf, offset):
        def at(half, start, count):
            return buf.at[pl.ds(pl.multiple_of(offset * half + start, 32), count)]
        return at

    def rows_steps(name, source, relay, at):
        s_rel, s_here, s_z, s_d = many(2), w.sem(), many(2), w.sem()
        passed = []

        def scatter(src, owner, e, which):
            half = cores[e]
            dst = at(half, pl.multiple_of(row_block(owner, half) * 32, 32), 32)
            w.send(src, dst, quad(2, e), s_z[which])
            w.send(src, dst, quad(1, e), s_here)
            if e == 0:
                w.local(src, dst, s_here)
            else:
                w.send(src, dst, sib, s_here)

        def halves(e):
            @step(f"{name}_out{e}")
            def _():
                w.send(source.at[1 - zh, cores[e]], relay.at[cores[e]], zp, s_rel[e])

            @step(f"{name}_own{e}")
            def _():
                scatter(source.at[zh, cores[e]], c, e, 0)

            @step(f"{name}_rel{e}")
            def _():
                w.arrived(relay.at[cores[e]], s_rel[e])
                scatter(relay.at[cores[e]], czp, e, 1)

            @step(f"{name}_fwd{e}")
            def _():
                first = (zh if e == 0 else 1 - zh) * 8 + 2 * chips[2]
                rows = at(k, pl.multiple_of(32 * (first + k * (14 - 2 * first)), 64), 64)
                w.arrived(rows, s_z[e])
                passed.append(w.send(rows, rows, quad(1, 0), s_d))

        halves(0)
        halves(1)
        return s_here, s_d, passed

    s_x, s_xd, _ = rows_steps("tok", tok, rel_t, rows_of(x, 0))
    s_c, s_cd, cot_passed = rows_steps("cot", cot, rel_c, rows_of(dy2, 512))

    def head_rows(t):
        return w2.at[pl.ds(pl.multiple_of(64 * t, 64), 64)]

    def exchange(name, src, at, keep):
        sem = many(4)

        @step(f"{name}_start")
        def _():
            w.send(src, at(team), zp, sem[1])
            w.send(src, at(team), yp, sem[0])
            if keep:
                w.local(src, at(team), sem[3])

        @step(f"{name}_pass")
        def _():
            w.arrived(at(team_z), sem[1])
            w.send(at(team_z), at(team_z), yp, sem[2])

        def end():
            w.arrived(at(team_y), sem[0])
            w.arrived(at(team_d), sem[2])
            if keep:
                w.arrived(at(team), sem[3])

        return end

    s_move, s_w2, s_gq, s_wq, s_ws = w.sem(), w.sem(), w.sem(), many(3), w.sem()
    gains_end = exchange("gain", gain, lambda t: gb.at[t, g], True)
    heads_end = exchange("win", head_rows(team), head_rows, False)
    wout_end = exchange("wout", wout, lambda t: wall.at[t, j, k], True)
    move = pltpu.make_async_remote_copy(
        src_ref=win, dst_ref=head_rows(lax.rem(g, 4)), send_sem=w.sem(), recv_sem=s_move,
        device_id=keeper, device_id_type=MESH,
    )

    @step("move")
    def _():
        pl.when(apart)(move.start)
        pl.when(alone)(lambda: pltpu.make_async_copy(win, head_rows(team), s_move).start())

    @step("moved")
    def _():
        w.arrived(head_rows(team), s_move)

    @step("gain_end")
    def _():
        gains_end()
        for d, e in others:
            w.send(gb.at[:, g], gb.at[:, g], quad(d, e), s_gq)

    @step("win_end")
    def _():
        heads_end()
        w.send(w2.at[own_head], w2.at[sib_head], sib, s_w2)

    @step("wout_end")
    def _():
        wout_end()
        for d in (2, 1):
            w.send(wall.at[:, j, k], wall.at[:, j, k], quad(d, 0), s_wq[d - 1])

    @step("wout_fwd")
    def _():
        w.arrived(wall.at[:, chips[2], k], s_wq[1])
        w.send(wall.at[:, chips[2], k], wall.at[:, chips[2], k], quad(1, 0), s_wq[2])

    @step("wout_sib")
    def _():
        for d in (1, 3):
            w.arrived(wall.at[:, j, k], s_wq[d - 1])
        w.send(wall.at[:, :, k], wall.at[:, :, k], sib, s_ws)

    parts = ((0, 80, wfa, acta, 320, 384), (80, 64, wfb, actb, 256, 256))
    s_f = many(2, 2, 4, 3)
    held = [[], []]

    def source(part, kind):
        return wffn.at[kind, pl.ds(parts[part][0], parts[part][1])]

    def unit(part, kind, far, slot):
        _, rows, buf, _, _, second = parts[part]
        return buf.at[kind, pl.ds(second * far + rows * slot, rows)]

    def unit_steps(part):
        sem = s_f[part]

        @step(f"u{part}_own")
        def _():
            for kind in range(3):
                w.local(source(part, kind), unit(part, kind, 0, 0), sem[0][0][kind])
                w.send(source(part, kind), unit(part, kind, 1, 0), sib, sem[1][0][kind])
                if part == 0:
                    wfa[kind, 320:384, :] = jnp.zeros((64, 1024), BF)

        @step(f"u{part}_y")
        def _():
            for kind in range(3):
                w.send(source(part, kind), unit(part, kind, 0, 1), yp, sem[0][1][kind])

        def from_z(kind):
            @step(f"u{part}_z{kind}")
            def _():
                w.send(source(part, kind), unit(part, kind, 0, 2), zp, sem[0][2][kind])

            @step(f"u{part}_f{kind}")
            def _():
                here = unit(part, kind, 0, 2)
                w.arrived(here, sem[0][2][kind])
                held[part].append(w.send(here, unit(part, kind, 0, 3), yp, sem[0][3][kind]))
                held[part].append(w.send(here, unit(part, kind, 1, 2), sib, sem[1][2][kind]))

        def ready(slot):
            @step(f"u{part}_s{slot}")
            def _():
                for kind in range(3):
                    here = unit(part, kind, 0, slot)
                    w.arrived(here, sem[0][slot][kind])
                    held[part].append(w.send(here, unit(part, kind, 1, slot), sib, sem[1][slot][kind]))

        for kind in range(3):
            from_z(kind)
        ready(1)
        ready(3)

        @step(f"u{part}_all")
        def _():
            for kind in range(3):
                w.arrived(unit(part, kind, 0, 0), sem[0][0][kind])
                for slot in range(4):
                    w.arrived(unit(part, kind, 1, slot), sem[1][slot][kind])

    unit_steps(0)
    unit_steps(1)

    lane = lax.broadcasted_iota(jnp.int32, (1, LANES), 1)
    low_row = lane < HALF_LANES

    @step("gains")
    def _():
        w.arrived(gb.at[:, pl.ds(0, 7)], s_gq)
        chunks = [jnp.zeros((1, LANES), F32) for _ in range(18)]
        for i in range(32):
            row = gb[i // 8, i % 8, 0:1, :]
            place, shift = divmod(68 * i, LANES)
            moved = pltpu.roll(row, shift, 1) if shift else row
            chunks[place] = chunks[place] + jnp.where(lane >= shift, moved, 0.0)
            if shift + 68 > LANES:
                chunks[place + 1] = chunks[place + 1] + jnp.where(lane < shift, moved, 0.0)
        for n in range(8):
            grow[0:1, LANES * n : LANES * (n + 1)] = chunks[n]
            grow[1:2, LANES * n : LANES * (n + 1)] = chunks[8 + n]
        flipped = pltpu.roll(chunks[16], HALF_LANES, 1)
        grow[2:3, 0:LANES] = jnp.where(low_row, chunks[16], flipped)
        grow[2:3, LANES : 2 * LANES] = jnp.where(low_row, flipped, chunks[16])

    def attn_gain():
        return grow[0:1, :]

    def ffn_gain():
        return grow[1:2, :]

    def query_gain():
        return grow[2:3, 0:LANES]

    def key_gain():
        return grow[2:3, LANES : 2 * LANES]

    s_raw, s_first = w.sem(), w.sem()

    @step("project")
    def _():
        w.arrived(x.at[pl.ds(0, 256)], s_x)
        w.arrived(x.at[pl.ds(0, 128)], s_xd)
        w.arrived(w2.at[sib_head], s_w2)
        weight = attn_gain()

        def rows_of_256(t, carry):
            rows = pl.multiple_of(t * 256, 256)
            values = x[pl.ds(rows, 256), :].astype(F32)
            scale = lax.rsqrt(jnp.mean(values * values, axis=1, keepdims=True) + EPS)
            first = (values * scale * weight).astype(BF)
            here = pl.multiple_of(my_rows + rows, 256)
            first2[pl.ds(here, 256), :] = first
            po[pl.ds(rows, 256), :] = _nt(first, w2[sib_head, :])
            raw[pl.ds(here, 256), :] = _nt(first, w2[own_head, :])
            return carry

        lax.fori_loop(0, 2, rows_of_256, 0)
        w.send(po, raw.at[pl.ds(my_rows, 512)], sib, s_raw)

    @step("first_sib")
    def _():
        w.send(first2.at[pl.ds(my_rows, 512)], first2.at[pl.ds(my_rows, 512)], sib, s_first)

    low = lax.broadcasted_iota(jnp.int32, (256, LANES), 1) < HALF_LANES
    quarter = lax.rem(lax.broadcasted_iota(jnp.int32, (256, LANES), 1), HALF_LANES) < 32

    def swap(v):
        return jnp.where(quarter, pltpu.roll(v, 96, 1), pltpu.roll(v, 32, 1))

    def head_sum(v):
        first = jnp.sum(jnp.where(low, v, 0.0), axis=1, keepdims=True)
        second = jnp.sum(jnp.where(low, 0.0, v), axis=1, keepdims=True)
        return jnp.where(low, first, second)

    def inverse_root(v):
        return lax.rsqrt(head_sum(v * v) * (1.0 / HEAD_DIM) + EPS)

    @step("rotate")
    def _():
        w.arrived(raw.at[pl.ds(0, 512)], s_raw)
        query_weight, key_weight = query_gain(), key_gain()

        def rotate_rows(t, carry):
            rows = pl.ds(pl.multiple_of(t * 256, 256), 256)
            cosine, sine = cos_t[rows, :], sin_t[rows, :]
            query = raw[rows, 0:LANES]
            both = raw[rows, LANES : 2 * LANES]
            query = query * inverse_root(query) * query_weight
            query = (query * cosine + swap(query) * sine) * (HEAD_DIM**-0.5)
            q0[rows, :] = jnp.where(low, query, 0.0).astype(BF)
            q1[rows, :] = jnp.where(low, 0.0, query).astype(BF)
            key = both * inverse_root(both) * key_weight
            key = key * cosine + swap(key) * sine
            kk[rows, :] = jnp.where(low, key, pltpu.roll(key, HALF_LANES, 1)).astype(BF)
            vv[rows, :] = jnp.where(low, pltpu.roll(both, HALF_LANES, 1), both).astype(BF)
            return carry

        lax.fori_loop(0, 4, rotate_rows, 0)

    s_mix, s_md, s_mz = w.sem(), w.sem(), many(2)
    head_lanes = pl.ds(pl.multiple_of(LANES * g, LANES), LANES)
    z_lanes = pl.ds(pl.multiple_of(256 * chips[2], 256), 256)
    late = []

    def forward_tile(t):
        @step(f"at{t}")
        def _():
            lo, n = 256 * t, 256 * (t + 1)
            place = lax.broadcasted_iota(jnp.int32, (256, n), 0) + lo
            key_place = lax.broadcasted_iota(jnp.int32, (256, n), 1)
            same = doc_col[lo : lo + 256, 0:1] == doc_row[0:1, 0:n]
            mask = (same & (key_place <= place)) | (key_place == place)
            outs = []
            for h, q in enumerate((q0, q1)):
                scores = jnp.where(mask, _nt(q[lo : lo + 256, :], kk[0:n, :]), MASKED)
                peak = jnp.max(scores, axis=1, keepdims=True)
                expo = jnp.exp(scores - peak)
                weights = (expo * (1.0 / jnp.sum(expo, axis=1, keepdims=True))).astype(BF)
                prob[h, lo : lo + 256, 0:n] = weights
                outs.append(_nn(weights, vv[0:n, :]))
            attended = jnp.where(low, outs[0], outs[1])
            att[lo : lo + 256, :] = attended
            mxs[lo : lo + 256, :] = attended.astype(BF)
            half = t // 2
            dst = mix.at[pl.ds(256 * (t % 2), 256), head_lanes]
            src = mxs.at[pl.ds(lo, 256)]
            w.send(src, dst, (dp, zh * 8 + 2 * chips[2] + half), s_mz[t % 2])
            w.send(src, dst, (dp, zh * 8 + 2 * chips[1] + half), s_mix)
            away = pltpu.make_async_remote_copy(
                src_ref=src, dst_ref=dst, send_sem=w.sem(), recv_sem=s_mix, device_id=sib, device_id_type=MESH
            )
            pl.when(k == half)(lambda: pltpu.make_async_copy(src, dst, s_mix).start())
            pl.when(k != half)(away.start)
            late.append((half, away))

    def pass_mixed(r):
        @step(f"mix_fwd{r}")
        def _():
            part = mix.at[pl.ds(256 * r, 256), z_lanes]
            w.arrived(part, s_mz[r])
            w.send(part, part, quad(1, 0), s_md)

    for t in range(4):
        forward_tile(t)
    pass_mixed(0)
    pass_mixed(1)

    s_dy, s_sec = w.sem(), w.sem()

    @step("dy")
    def _():
        w.arrived(dy2.at[pl.ds(0, 256)], s_c)
        w.arrived(dy2.at[pl.ds(0, 128)], s_cd)
        w.finish(cot_passed)

        def drop_rows(t, carry):
            rows = pl.ds(pl.multiple_of(my_rows + t * 128, 128), 128)
            place = lax.broadcasted_iota(jnp.int32, (128, 1), 0) + (my_rows + t * 128)
            kept = (place < limit).astype(F32).astype(BF)
            dy2[rows, :] = dy2[rows, :] * kept
            return carry

        lax.fori_loop(0, 4, drop_rows, 0)
        w.send(dy2.at[pl.ds(my_rows, 512)], dy2.at[pl.ds(my_rows, 512)], sib, s_dy)

    def attended_rows(rows):
        total = None
        for n in range(4):
            term = _nn(mix[rows, 256 * n : 256 * (n + 1)], wall[n].reshape(256, 1024))
            total = term if total is None else total + term
        return total

    @step("second")
    def _():
        w.arrived(wall.at[:, :, 0], s_ws)
        w.arrived(mix.at[pl.ds(0, 256)], s_mix)
        w.arrived(mix.at[:, pl.ds(0, 256)], s_md)
        weight = ffn_gain()

        def project_out(t, carry):
            rows = pl.ds(pl.multiple_of(t * 256, 256), 256)
            state = x[rows, :].astype(F32) + attended_rows(rows)
            scale = lax.rsqrt(jnp.mean(state * state, axis=1, keepdims=True) + EPS)
            here = pl.ds(pl.multiple_of(my_rows + t * 256, 256), 256)
            sec2[here, :] = (state * scale * weight).astype(BF)
            return carry

        lax.fori_loop(0, 2, project_out, 0)
        w.send(sec2.at[pl.ds(my_rows, 512)], sec2.at[pl.ds(my_rows, 512)], sib, s_sec)

    class Sum:
        def __init__(self, name, buf, into, which):
            self.buf, self.into, self.which = buf, into, which
            self.sems = many(3, 2)
            for t in range(2):
                if name == "os":
                    step(f"{name}_x{t}")(lambda t=t: self.over_x(t))
                step(f"{name}_z{t}")(lambda t=t: self.over_z(t))

        def rows(self, d, t):
            return pl.ds(pl.multiple_of(256 * t + 64 * piece(chips[d]), 64), 64)

        def over_x(self, t):
            for d, slot in ((3, 1), (1, 0)):
                w.send(self.buf.at[self.rows(d, t)], self.into.at[slot, t], quad(1, 0), self.sems[slot][t])

        def over_z(self, t):
            w.arrived(self.into.at[1, t], self.sems[1][t])
            total = self.buf[self.rows(2, t), :].astype(F32) + self.into[1, t].astype(F32)
            rsz[self.which, t] = total.astype(BF)
            w.send(rsz.at[self.which, t], self.into.at[2, t], quad(2, 0), self.sems[2][t])

        def result(self, t):
            total = self.buf[self.rows(0, t), :].astype(F32)
            for slot in (0, 2):
                w.arrived(self.into.at[slot, t], self.sems[slot][t])
                total = total + self.into[slot, t].astype(F32)
            return total

    sum_ds, sum_os, sum_df = Sum("ds", dsb, dsr, 0), Sum("os", osb, osr, 1), Sum("df", dfb, dfr, 2)

    s_act, s_gr, s_near, s_gt = many(2), many(2, 3), many(2), many(2, 3)
    acted = []

    def part_steps(part):
        start, rows_kept, buf, acts, count, second = parts[part]
        span = pl.ds(start, rows_kept)

        def feed_forward(t):
            @step(f"ff{part}{t}")
            def _():
                if part == 1 and t == 0:
                    w.finish(acted)
                rows = pl.ds(pl.multiple_of(my_rows + 256 * t, 256), 256)
                here = pl.ds(256 * t, 256)
                gate = _nt(sec2[rows, :], buf[0])
                up = _nt(sec2[rows, :], buf[1])
                d_hidden = _nt(dy2[rows, :], buf[2])
                sigmoid = 1.0 / (1.0 + jnp.exp(-gate))
                silu = gate * sigmoid
                d_gate = (d_hidden * up * (sigmoid + silu * (1.0 - sigmoid))).astype(BF)
                d_up = (d_hidden * silu).astype(BF)
                hidden = (silu * up).astype(BF)
                for n, value in enumerate((d_gate, d_up, hidden)):
                    acts[n, rows, :] = value[:, 0:second]
                    asend[n, here, 0:count] = value[:, second : second + count]
                lanes = pl.ds(0, second)
                acted.append(w.send(asend.at[:, here, lanes], acts.at[:, rows], sib, s_act[part]))
                d_second = _nn(d_gate, buf[0]) + _nn(d_up, buf[1])
                result = _nn(hidden, buf[2])
                if part == 1:
                    d_second = d_second + dsb[here, :].astype(F32)
                    result = result + osb[here, :].astype(F32)
                dsb[here, :] = d_second.astype(BF)
                osb[here, :] = result.astype(BF)
                if part == 1:
                    sum_ds.over_x(t)

        @step(f"wg{part}_in")
        def _():
            w.finish(held[part])
            w.arrived(acts.at[:, pl.ds(0, 512)], s_act[part])
            if part == 0:
                w.arrived(sec2.at[pl.ds(0, 512)], s_sec)
                w.arrived(dy2.at[pl.ds(0, 512)], s_dy)

        def weight_grads(kind):
            @step(f"wg{part}{kind}")
            def _():
                right = dy2 if kind == 2 else sec2

                def columns(n, carry):
                    cols = pl.ds(pl.multiple_of(n * 512, 512), 512)
                    buf[kind, 0:count, cols] = _tn(acts[kind], right[:, cols])[0:count, :].astype(BF)
                    return carry

                lax.fori_loop(0, 2, columns, 0)

        def pass_grads(kind):
            @step(f"gr{part}_y{kind}")
            def _():
                rows = buf.at[kind, pl.ds(rows_kept * 3, rows_kept)]
                w.send(rows, gr.at[1, kind, span], yp, s_gr[part][kind])

            @step(f"gr{part}_z{kind}")
            def _():
                w.arrived(gr.at[1, kind, span], s_gr[part][kind])
                gs[kind, span, :] = (
                    buf[kind, 2 * rows_kept : 3 * rows_kept, :].astype(F32) + gr[1, kind, span, :].astype(F32)
                ).astype(BF)
                w.send(gs.at[kind, span], gt.at[kind, span], zp, s_gt[part][kind])

        @step(f"gr{part}_near")
        def _():
            w.send(buf.at[:, pl.ds(rows_kept, rows_kept)], gr.at[0, :, span], yp, s_near[part])

        @step(f"gr{part}_end")
        def _():
            w.arrived(gr.at[0, :, span], s_near[part])
            for kind in range(3):
                w.arrived(gt.at[kind, span], s_gt[part][kind])
                o_ffn[kind, span, :] = (
                    buf[kind, 0:rows_kept, :].astype(F32)
                    + gr[0, kind, span, :].astype(F32) + gt[kind, span, :].astype(F32)
                )

        feed_forward(0)
        feed_forward(1)
        for kind in range(3):
            weight_grads(kind)
            pass_grads(kind)

    part_steps(0)
    part_steps(1)

    s_dm, s_da, s_das = w.sem(), many(3), w.sem()
    terms = {"ffn": jnp.zeros((1, 1024), F32), "attn": jnp.zeros((1, 1024), F32)}

    def state_steps(t):
        @step(f"st{t}")
        def _():
            start = 256 * t + 64 * mine
            rows = pl.ds(pl.multiple_of(start, 64), 64)
            state = x[rows, :].astype(F32) + attended_rows(rows)
            bos[t] = state
            scale = lax.rsqrt(jnp.mean(state * state, axis=1, keepdims=True) + EPS)
            normed = state * scale
            total = sum_ds.result(t)
            terms["ffn"] = terms["ffn"] + jnp.sum(total * normed, axis=0, keepdims=True)
            weighted = total * ffn_gain()
            inner = jnp.mean(weighted * normed, axis=1, keepdims=True)
            grad = dy2[pl.ds(pl.multiple_of(my_rows + start, 64), 64), :].astype(F32) + scale * (weighted - normed * inner)
            dstate[t] = grad
            low_grad = grad.astype(BF)
            daf[k, t, mine] = low_grad
            for n in range(4):
                dmb[t, :, 256 * n : 256 * (n + 1)] = _nt(low_grad, wall[n].reshape(256, 1024)).astype(BF)
            for d, e in others:
                lanes = pl.ds(pl.multiple_of(LANES * (2 * chips[d] + cores[e]), LANES), LANES)
                w.send(dmb.at[t, :, lanes], dmix.at[k, t, mine], quad(d, e), s_dm)
            w.local(dmb.at[t, :, head_lanes], dmix.at[k, t, mine], s_dm)

    state_steps(0)
    state_steps(1)

    @step("da_out")
    def _():
        for d in (2, 1):
            w.send(daf.at[k, :, mine], daf.at[k, :, mine], quad(d, 0), s_da[d - 1])

    @step("da_fwd")
    def _():
        far = piece(chips[2])
        w.arrived(daf.at[k, :, far], s_da[1])
        w.send(daf.at[k, :, far], daf.at[k, :, far], quad(1, 0), s_da[2])

    @step("da_sib")
    def _():
        for d in (1, 3):
            w.arrived(daf.at[k, :, mine], s_da[d - 1])
        w.send(daf.at[k], daf.at[k], sib, s_das)

    home = zh + k * (1 - 2 * zh)

    def send_home(buf, into, sem):
        w.send(buf.at[1 - home, 0], into.at[zh, k], zp, sem)
        w.send(buf.at[1 - home, 1], into.at[zh, k], zps, sem)
        w.send(buf.at[home, 1], into.at[zh, k], sib, sem)
        w.local(buf.at[home, 0], into.at[zh, k], sem)

    s_bo, s_tg = w.sem(), w.sem()

    @step("block")
    def _():
        for t in range(2):
            total = bos[t] + sum_os.result(t)
            obs[t] = total.astype(BF).reshape(2, 32, 1024)
        send_home(obs, bor, s_bo)

    @step("block_end")
    def _():
        w.arrived(bor, s_bo)
        o_block[...] = bor[...]

    @step("bw_in")
    def _():
        w.arrived(dmix, s_dm)
        dkk[...] = jnp.zeros_like(dkk)
        dvv[...] = jnp.zeros_like(dvv)

    def backward_tile(t):
        @step(f"bw{t}")
        def _():
            lo, n = 256 * t, 256 * (t + 1)
            d_out = dmix[...].reshape(1024, LANES)[lo : lo + 256, :].astype(F32)
            product = d_out * att[lo : lo + 256, :]
            results = []
            for h, q in enumerate((q0, q1)):
                here = low if h == 0 else jnp.logical_not(low)
                d_head = jnp.where(here, d_out, 0.0).astype(BF)
                delta = jnp.sum(jnp.where(here, product, 0.0), axis=1, keepdims=True)
                weights = prob[h, lo : lo + 256, 0:n]
                pulled = _nt(d_head, vv[0:n, :])
                d_scores = (weights.astype(F32) * (pulled - delta)).astype(BF)
                results.append(_nn(d_scores, kk[0:n, :]))
                dkk[0:n, :] += _tn(d_scores, q[lo : lo + 256, :])
                dvv[0:n, :] += _tn(weights, d_head)
            dqq[lo : lo + 256, :] = jnp.where(low, results[0], results[1]) * (HEAD_DIM**-0.5)

    for t in range(4):
        backward_tile(t)
    s_dpx = w.sem()

    @step("back")
    def _():
        query_weight, key_weight = query_gain(), key_gain()

        def back_rows(t, carry):
            query_sum, key_sum = carry
            rows = pl.ds(pl.multiple_of(t * 256, 256), 256)
            cosine, sine = cos_t[rows, :], sin_t[rows, :]
            query = raw[rows, 0:LANES]
            both = raw[rows, LANES : 2 * LANES]

            def through(values, grads, gain_row):
                scale = inverse_root(values)
                normed = values * scale
                grads = grads * cosine - swap(grads) * sine
                weighted = grads * gain_row
                inner = head_sum(weighted * normed) * (1.0 / HEAD_DIM)
                return scale * (weighted - normed * inner), jnp.sum(grads * normed, axis=0, keepdims=True)

            query_back, query_term = through(query, dqq[rows, :], query_weight)
            d_key = dkk[rows, :]
            d_key = d_key + pltpu.roll(d_key, HALF_LANES, 1)
            key_back, key_term = through(both, d_key, key_weight)
            d_value = dvv[rows, :]
            d_value = d_value + pltpu.roll(d_value, HALF_LANES, 1)
            dpj[rows, 0:LANES] = query_back.astype(BF)
            dpj[rows, LANES : 2 * LANES] = jnp.where(low, key_back, d_value).astype(BF)
            return query_sum + query_term, key_sum + key_term

        zero_row = jnp.zeros((1, LANES), F32)
        query_sum, key_sum = lax.fori_loop(0, 4, back_rows, (zero_row, zero_row))
        w.send(dpj.at[pl.ds(other_rows, 512)], dpx, sib, s_dpx)
        gg[:, 2 * LANES : 3 * LANES] = jnp.zeros((8, LANES), F32)
        gg[0:1, 2 * LANES : 3 * LANES] = query_sum + pltpu.roll(query_sum, HALF_LANES, 1)
        gg[1:2, 2 * LANES : 3 * LANES] = key_sum

    def first_steps(t):
        @step(f"df{t}")
        def _():
            if t == 0:
                w.arrived(dpx, s_dpx)
            here = pl.ds(256 * t, 256)
            rows = pl.ds(pl.multiple_of(my_rows + 256 * t, 256), 256)
            dfb[here, :] = (_nn(dpj[rows, :], w2[own_head, :]) + _nn(dpx[here, :], w2[sib_head, :])).astype(BF)
            sum_df.over_x(t)

    first_steps(0)
    first_steps(1)
    returned = []

    def term_steps(name, rows, value, result):
        sem = many(4)

        @step(f"{name}_y")
        def _():
            term = value()
            count = rows.stop - rows.start
            for p in range(4):
                igs[p, rows, :] = term[count * p : count * (p + 1), :].astype(BF)
            at = pl.ds(rows.start, count)
            w.send(igs.at[team_d, at], agr.at[1, at], yp, sem[1])
            w.send(igs.at[team_y, at], agr.at[0, at], yp, sem[0])

        at = pl.ds(rows.start, rows.stop - rows.start)

        @step(f"{name}_z")
        def _():
            w.arrived(agr.at[1, at], sem[1])
            agz[rows, :] = (igs[team_z, rows, :].astype(F32) + agr[1, rows, :].astype(F32)).astype(BF)
            w.send(agz.at[at], agt.at[at], zp, sem[2])

        @step(f"{name}_sum")
        def _():
            w.arrived(agr.at[0, at], sem[0])
            w.arrived(agt.at[at], sem[2])
            agh[rows, :] = (
                igs[team, rows, :].astype(F32) + agr[0, rows, :].astype(F32) + agt[rows, :].astype(F32)
            ).astype(BF)

        back = pltpu.make_async_remote_copy(
            src_ref=agh.at[at], dst_ref=ago.at[at], send_sem=w.sem(), recv_sem=sem[3],
            device_id=owner_of, device_id_type=MESH,
        )
        returned.append(back)

        @step(f"{name}_give")
        def _():
            pl.when(apart)(back.start)
            pl.when(alone)(lambda: pltpu.make_async_copy(agh.at[at], ago.at[at], sem[3]).start())

        @step(f"{name}_end")
        def _():
            w.arrived(ago.at[at], sem[3])
            result[...] = ago[rows, :]

    def in_value():
        w.arrived(first2.at[pl.ds(0, 512)], s_first)
        return _tn(dpj[...], first2[...])

    def out_value():
        w.arrived(daf.at[0], s_das)
        return _tn(mxs[...], daf[...].reshape(1024, 1024))

    term_steps("in", slice(0, 64), in_value, o_in)
    term_steps("out", slice(64, 96), out_value, o_out)

    def token_steps(t):
        @step(f"tg{t}")
        def _():
            rows = pl.ds(pl.multiple_of(256 * t + 64 * mine, 64), 64)
            values = x[rows, :].astype(F32)
            scale = lax.rsqrt(jnp.mean(values * values, axis=1, keepdims=True) + EPS)
            normed = values * scale
            total = sum_df.result(t)
            terms["attn"] = terms["attn"] + jnp.sum(total * normed, axis=0, keepdims=True)
            weighted = total * attn_gain()
            inner = jnp.mean(weighted * normed, axis=1, keepdims=True)
            grad = dstate[t] + scale * (weighted - normed * inner)
            tgs[t] = grad.astype(BF).reshape(2, 32, 1024)

    token_steps(0)
    token_steps(1)

    @step("tok_home")
    def _():
        send_home(tgs, tgr, s_tg)

    @step("tok_end")
    def _():
        w.arrived(tgr, s_tg)
        o_tokens[...] = tgr[...]

    s_gg, s_gt4 = w.sem(), many(3)

    @step("gg_out")
    def _():
        for n in range(8):
            gg[n : n + 1, 0:LANES] = terms["attn"][:, LANES * n : LANES * (n + 1)]
            gg[n : n + 1, LANES : 2 * LANES] = terms["ffn"][:, LANES * n : LANES * (n + 1)]
        for d, e in others:
            w.send(gg, ggq.at[g], quad(d, e), s_gg)
        w.local(gg, ggq.at[g], s_gg)

    @step("gg_sum")
    def _():
        w.arrived(ggq, s_gg)
        total = ggq[0]
        for n in range(1, 8):
            total = total + ggq[n]
        gsum[...] = total
        for n, peer in enumerate((yp, zp, diag)):
            w.send(gsum, ggt.at[n], peer, s_gt4[n])

    @step("gg_end")
    def _():
        total = gsum[...]
        for n in range(3):
            w.arrived(ggt.at[n], s_gt4[n])
            total = total + ggt[n]
        gflat[0:8, :] = total[:, 0:LANES]
        gflat[8:16, :] = total[:, LANES : 2 * LANES]
        key_part = pltpu.roll(total[1:2, 2 * LANES : 3 * LANES], HALF_LANES, 1)
        gflat[16:17, :] = jnp.where(low_row, total[0:1, 2 * LANES : 3 * LANES], key_part)
        place = 68 * (8 * team + g)
        line, shift = lax.div(place, LANES), lax.rem(place, LANES)
        back = lax.rem(LANES - shift, LANES)
        left = pltpu.roll(gflat[pl.ds(line, 1), :], back, 1)
        right = pltpu.roll(gflat[pl.ds(line + 1, 1), :], back, 1)
        o_gain[...] = jnp.where(lane < LANES - shift, left, right)[:, 0:68]

    for name in ORDER:
        steps.pop(name)()
    assert not steps, sorted(steps)
    w.finish()
    for half, away in late:
        pl.when(k != half)(away.wait_send)
    pl.when(apart)(move.wait_send)
    for back in returned:
        pl.when(apart)(back.wait_send)


ORDER = (
    "tok_out0", "cot_own1", "wout_start", "tok_out1", "cot_own0", "u0_y", "u1_own", "tok_own0", "move",
    "tok_own1", "gain_start", "tok_rel0", "wout_pass", "cot_out0", "cot_fwd0", "tok_rel1", "gain_pass",
    "moved", "cot_out1", "u0_s1", "gain_end", "win_start", "tok_fwd1", "tok_fwd0", "wout_end", "win_pass",
    "u0_z1", "gains", "win_end", "u0_own", "cot_rel1", "project", "u1_y", "u0_z0", "wout_fwd", "cot_rel0",
    "u0_z2", "rotate", "at1", "u0_f1", "at3", "u0_f0", "at0", "at2", "u1_z2", "cot_fwd1", "mix_fwd1", "u0_f2",
    "mix_fwd0", "wout_sib", "u1_f2", "u0_s3", "u1_z1", "u0_all", "u1_z0", "dy", "second", "ff00", "u1_f1",
    "ff01", "first_sib", "u1_f0", "u1_s1", "wg0_in", "wg01", "gr0_y1", "wg00", "u1_s3", "gr0_y0", "u1_all",
    "ff10", "gr0_z1", "ff11", "ds_z0", "wg02", "gr0_z0", "wg1_in", "wg11", "wg12", "gr1_y1", "os_x0",
    "gr0_y2", "wg10", "gr1_y2", "ds_z1", "gr1_y0", "st0", "gr1_z1", "st1", "gr0_near", "gr0_z2", "da_out",
    "os_x1", "bw_in", "bw3", "bw2", "bw1", "gr1_z0", "bw0", "back", "gr1_z2", "os_z0", "os_z1", "da_fwd",
    "in_y", "gr1_near", "df0", "in_z", "da_sib", "df_z0", "df1", "out_y", "block", "in_sum", "df_z1", "tg0",
    "out_z", "in_give", "gr1_end", "tg1", "out_sum", "tok_home", "gg_out", "gg_sum", "in_end", "out_give",
    "block_end", "gr0_end", "tok_end", "gg_end", "out_end",
)


TEAM_SCRATCH = (
    ((512, 1024), BF), ((2, 32, 1024), BF), ((2, 32, 1024), BF), ((512, 1024), BF),
    ((4, 4, 2, 32, 1024), BF), ((3, 704, 1024), BF), ((3, 512, 1024), BF), ((4, 8, 8, 128), F32), ((8, 1024), F32),
    ((1024, 1024), BF), ((1024, 256), F32), ((512, 256), F32),
    ((1024, 128), BF), ((1024, 128), BF), ((1024, 128), BF), ((1024, 128), BF), ((2, 1024, 1024), BF),
    ((1024, 128), F32), ((1024, 128), BF), ((512, 1024), BF), ((1024, 1024), BF), ((1024, 1024), BF),
    ((3, 1024, 384), BF), ((3, 1024, 256), BF), ((3, 512, 384), BF),
    ((512, 1024), BF), ((512, 1024), BF), ((3, 2, 64, 1024), BF), ((3, 2, 64, 1024), BF), ((3, 2, 64, 1024), BF),
    ((2, 3, 144, 1024), BF), ((3, 144, 1024), BF), ((3, 144, 1024), BF),
    ((2, 64, 1024), F32), ((2, 64, 1024), BF), ((2, 2, 4, 64, 1024), BF), ((2, 2, 4, 64, 128), BF),
    ((1024, 128), F32), ((1024, 128), F32), ((1024, 128), F32), ((1024, 256), BF), ((512, 256), BF),
    ((512, 1024), BF), ((3, 2, 64, 1024), BF),
    ((4, 96, 1024), BF), ((2, 96, 1024), BF), ((96, 1024), BF), ((96, 1024), BF), ((96, 1024), BF), ((96, 1024), BF),
    ((2, 64, 1024), F32), ((2, 2, 32, 1024), BF), ((2, 2, 32, 1024), BF), ((2, 2, 32, 1024), BF),
    ((2, 2, 32, 1024), BF),
    ((8, 384), F32), ((8, 8, 384), F32), ((8, 384), F32), ((3, 8, 384), F32), ((8, 128), F32), ((24, 128), F32), ((1024, 8), F32), ((8, 1024), F32),
)


def rotary_lanes(rows):
    width = HEAD_DIM // 2
    freq = (ROPE_BASE ** (-np.arange(width, dtype=np.float32) * np.float32(2.0 / HEAD_DIM))).astype(np.float32)
    angle = (np.arange(rows, dtype=np.float32)[:, None] * freq).astype(np.float32).astype(np.float64)
    cosine, sine = np.cos(angle), np.sin(angle)
    return (
        np.tile(np.concatenate([cosine, cosine], 1), (1, 2)).astype(np.float32),
        np.tile(np.concatenate([-sine, sine], 1), (1, 2)).astype(np.float32),
    )


def on_team(tokens, segments, lengths, attn_in, attn_out, gains, ffn_weights, cotangent):
    batches, block_len, halves, width = tokens.shape
    rows = segments.shape[1]
    cosine, sine = rotary_lanes(2 * rows)
    args = (
        tokens.transpose(0, 2, 1, 3),
        cotangent.transpose(0, 2, 1, 3),
        attn_in,
        attn_out,
        gains[None],
        ffn_weights.transpose(1, 0, 2),
        segments.transpose(0, 2, 1),
        lengths,
        jnp.asarray(cosine),
        jnp.asarray(sine),
    )
    vmem = pl.BlockSpec(memory_space=pltpu.VMEM)
    outs = pl.pallas_call(
        block_kernel,
        out_shape=(
            jax.ShapeDtypeStruct((2, 2, 32, 1024), BF),
            jax.ShapeDtypeStruct((2, 2, 32, 1024), BF),
            jax.ShapeDtypeStruct((64, 1024), BF),
            jax.ShapeDtypeStruct((32, 1024), BF),
            jax.ShapeDtypeStruct((1, 68), F32),
            jax.ShapeDtypeStruct((3, 144, 1024), F32),
        ),
        in_specs=[vmem] * 7 + [pl.BlockSpec(memory_space=pltpu.SMEM)] + [vmem] * 2,
        out_specs=(vmem,) * 6,
        scratch_shapes=[pltpu.VMEM(shape, kind) for shape, kind in TEAM_SCRATCH]
        + [pltpu.SemaphoreType.DMA((COPIES,))],
        compiler_params=pltpu.CompilerParams(
            collective_id=0, has_side_effects=True, vmem_limit_bytes=VMEM_BYTES
        ),
    )(*args)
    block, token_grad, in_grad, out_grad, gain_grad, unit_grad = outs
    return (
        block.transpose(0, 2, 1, 3),
        token_grad.transpose(0, 2, 1, 3).astype(F32),
        in_grad.astype(F32),
        out_grad.astype(F32),
        gain_grad[0],
        unit_grad.transpose(1, 0, 2),
    )


VMEM_BYTES = 62 << 20


def solution(mesh):
    dp, ctx = mesh.devices.shape
    if ctx == 2 * KV_HEADS:
        ring = "ctx"
        every = ("dp", "ctx")
        team, run = mesh, on_team
    else:
        ring = ("s", "q", "g")
        every = EVERY
        team = Mesh(mesh.devices.reshape(dp, 2, ctx // (2 * KV_HEADS), KV_HEADS), EVERY)
        run = on_device
    placed = (
        P("dp", ring, None, None),
        P("dp", None, None),
        P("dp"),
        P(every, None),
        P(every, None),
        P(every),
        P(every, None, None),
        P("dp", ring, None, None),
    )
    return jax.shard_map(
        run,
        mesh=team,
        in_specs=placed,
        out_specs=(
            P("dp", ring, None, None),
            P("dp", ring, None, None),
            P(every, None),
            P(every, None),
            P(every),
            P(every, None, None),
        ),
        check_vma=False,
    )
```

```python
import jax
import jax.numpy as jnp
import numpy as np
from jax import lax
from jax.experimental import pallas as pl
from jax.experimental.pallas import tpu as pltpu
from jax.sharding import Mesh
from jax.sharding import PartitionSpec as P

FF = 4608
HEADS = 16
KV_HEADS = 8
HEAD_DIM = 64
GROUP = HEADS // KV_HEADS
QKV_ROWS = 2048

EPS = 1e-05
ROPE_BASE = 1000000.0
MASKED = -1e30
BF = jnp.bfloat16
F32 = jnp.float32


def root_mean(values):
    return lax.rsqrt(jnp.mean(values * values, axis=-1, keepdims=True) + EPS)


def rotate(values, cosine, sine):
    width = values.shape[-1] // 2
    first = values[..., :width]
    second = values[..., width:]
    return jnp.concatenate(
        [first * cosine - second * sine, second * cosine + first * sine], axis=-1
    )


def tables(positions):
    width = HEAD_DIM // 2
    freq = ROPE_BASE ** (-jnp.arange(width, dtype=F32) * 2.0 / HEAD_DIM)
    angle = positions.astype(F32)[..., None] * freq
    return (jnp.cos(angle), jnp.sin(angle))


def prepare(query_raw, key_raw, query_gain, key_gain, cosine, sine):
    query_norm = query_raw * root_mean(query_raw) * query_gain
    key_norm = key_raw * root_mean(key_raw) * key_gain
    return (
        rotate(query_norm, cosine[:, None], sine[:, None]),
        rotate(key_norm, cosine, sine),
    )


def norm_back(grad, normed, scale_rows, gain):
    weighted = grad * gain
    inner = jnp.mean(weighted * normed, axis=-1, keepdims=True)
    return (scale_rows * (weighted - normed * inner), jnp.sum(grad * normed, axis=0))


def dot(a, b, ca, cb):
    return lax.dot_general(a, b, (((ca,), (cb,)), ((), ())), preferred_element_type=F32)


TEAM = ("dp", "s", "q")
EVERY = ("dp", "s", "q", "g")


def spread(local, block_len):
    mine = lax.all_to_all(local, "s", 0, 0, tiled=True)
    return lax.all_gather(mine, "g", axis=0, tiled=False)


def on_device(tokens, segments, lengths, attn_in, attn_out, gains, ffn_weights, cotangent):
    batches, block_len, halves, width = tokens.shape
    seq = lax.axis_index("s")
    quarter = lax.axis_index("q")
    head = lax.axis_index("g")
    quarters = lax.axis_size("q")
    heads = lax.axis_size("g")
    ctx_count = 2 * quarters * heads
    scale = HEAD_DIM ** (-0.5)
    weight_in = lax.all_gather(attn_in, EVERY, axis=0, tiled=True)
    weight_out = lax.all_gather(attn_out, EVERY, axis=0, tiled=True)
    gain_all = lax.all_gather(gains, EVERY, axis=0, tiled=True).astype(F32)
    attn_gain = gain_all[:width]
    ffn_gain = gain_all[width : 2 * width]
    query_gain = gain_all[2 * width : 2 * width + HEAD_DIM]
    key_gain = gain_all[2 * width + HEAD_DIM :]
    head_rows = (GROUP + 2) * HEAD_DIM
    out_rows = GROUP * HEAD_DIM
    weight_head = lax.dynamic_slice_in_dim(weight_in, head * head_rows, head_rows, 0)
    weight_mix = lax.dynamic_slice_in_dim(weight_out, head * out_rows, out_rows, 0)

    inputs = spread(tokens, block_len)
    count = inputs.size // width
    inputs = inputs.reshape(count, width).astype(F32)
    cot = spread(cotangent, block_len).reshape(count, width).astype(F32)

    def places(which):
        owner_g = jnp.arange(heads, dtype=jnp.int32)[:, None, None, None]
        owner_s = jnp.arange(2, dtype=jnp.int32)[None, :, None, None]
        row = jnp.arange(block_len, dtype=jnp.int32)[None, None, :, None]
        half = jnp.arange(2, dtype=jnp.int32)[None, None, None, :]
        owner = owner_s * (quarters * heads) + which * heads + owner_g
        block = jnp.where(half == 0, owner, 2 * ctx_count - 1 - owner)
        return (
            (block * block_len + row).reshape(count),
            jnp.broadcast_to((owner * block_len + row) * 2 + half, (heads, 2, block_len, 2)).reshape(count),
        )

    docs = lax.dynamic_index_in_dim(segments, seq, 0, False).reshape(-1)
    length = lax.dynamic_index_in_dim(lengths, seq, 0, False)
    place, slot = places(quarter)
    key_place, key_slot = jax.vmap(places)(jnp.arange(quarters, dtype=jnp.int32))
    key_place = key_place.reshape(-1)
    query_doc = docs[slot]
    key_doc = docs[key_slot.reshape(-1)]
    causal = key_place[None, :] <= place[:, None]
    live = (key_place[None, :] < length) | (key_place[None, :] == place[:, None])
    mask = causal & live & (query_doc[:, None] == key_doc[None, :])
    valid = (place < length).astype(F32)[:, None]

    first_scale = root_mean(inputs)
    first_normed = inputs * first_scale
    first = (first_normed * attn_gain).astype(BF)
    projected = dot(first, weight_head, 1, 1).reshape(count, GROUP + 2, HEAD_DIM)
    cosine, sine = tables(place)

    def prepare_here(query_raw, key_raw, gain_query, gain_key):
        return prepare(query_raw, key_raw, gain_query, gain_key, cosine, sine)

    (query_rot, key_rot), prepare_pull = jax.vjp(
        prepare_here, projected[:, :GROUP], projected[:, GROUP], query_gain, key_gain
    )
    queries = query_rot.astype(BF)
    pair = jnp.stack([key_rot.astype(BF), projected[:, GROUP + 1].astype(BF)])
    pair = lax.all_gather(pair, "q", axis=1, tiled=True)
    keys, values = pair[0], pair[1]

    scores = jnp.einsum("qjd,kd->jqk", queries, keys, preferred_element_type=F32) * scale
    scores = jnp.where(mask[None], scores, MASKED)
    peak = jnp.max(scores, axis=-1, keepdims=True)
    expo = jnp.where(mask[None], jnp.exp(scores - peak), 0.0)
    weights = expo / jnp.sum(expo, axis=-1, keepdims=True)
    attended = jnp.einsum("jqk,kd->qjd", weights.astype(BF), values, preferred_element_type=F32)
    mixed_here = attended.astype(BF).reshape(count, out_rows)
    mixed = lax.all_gather(mixed_here, "g", axis=1, tiled=True)
    state = inputs + dot(mixed, weight_out, 1, 0)
    second_scale = root_mean(state)
    second_normed = state * second_scale
    second = (second_normed * ffn_gain).astype(BF)
    grad_out = cot * valid
    grad_low = grad_out.astype(BF)

    units = lax.all_gather(ffn_weights, TEAM, axis=0, tiled=True)
    unit_gate, unit_up, unit_down = units[:, 0], units[:, 1], units[:, 2]
    gate = dot(second, unit_gate, 1, 1)
    upward = dot(second, unit_up, 1, 1)
    sigmoid = jax.nn.sigmoid(gate)
    hidden = (gate * sigmoid * upward).astype(BF)
    d_hidden = dot(grad_low, unit_down, 1, 1)
    d_gate = (d_hidden * upward * sigmoid * (1.0 + gate * (1.0 - sigmoid))).astype(BF)
    d_up = (d_hidden * gate * sigmoid).astype(BF)
    d_second = dot(d_gate, unit_gate, 1, 0) + dot(d_up, unit_up, 1, 0)
    own = count // heads

    def gathered(values):
        return lax.psum_scatter(values.astype(BF), "g", scatter_dimension=0, tiled=True).astype(F32)

    def own_rows(values):
        return lax.dynamic_slice_in_dim(values, head * own, own, 0)

    def home(values):
        back = values.reshape(2, block_len, halves, width)
        return lax.all_to_all(back, "s", 0, 0, tiled=True)

    ffn_sum = gathered(dot(hidden, unit_down, 1, 0))
    block_out = home((own_rows(state) + ffn_sum).astype(BF))
    ffn_grad = lax.psum_scatter(
        jnp.stack([dot(d_gate, second, 0, 0), dot(d_up, second, 0, 0), dot(hidden, grad_low, 0, 0)], axis=1),
        TEAM,
        scatter_dimension=0,
        tiled=True,
    )
    norm_grad, ffn_gain_grad = norm_back(
        gathered(d_second), own_rows(second_normed), own_rows(second_scale), ffn_gain
    )
    state_grad = own_rows(grad_out) + norm_grad
    attended_grad = lax.all_gather(state_grad.astype(BF), "g", axis=0, tiled=True)
    mixed_grad = dot(attended_grad, weight_mix, 1, 1).astype(BF)
    out_term = dot(mixed_here, attended_grad, 0, 0)
    mixed_grad = mixed_grad.reshape(count, GROUP, HEAD_DIM)
    delta = jnp.sum(mixed_grad.astype(F32) * attended, axis=-1).T[:, :, None]
    pulled = jnp.einsum("qjd,kd->jqk", mixed_grad, values, preferred_element_type=F32)
    score_grad = (weights * (pulled - delta)).astype(BF)
    query_grad = jnp.einsum("jqk,kd->qjd", score_grad, keys, preferred_element_type=F32) * scale
    key_grad = jnp.einsum("jqk,qjd->kd", score_grad, queries, preferred_element_type=F32) * scale
    value_grad = jnp.einsum("jqk,qjd->kd", weights.astype(BF), mixed_grad, preferred_element_type=F32)
    if quarters > 1:
        key_grad = lax.psum_scatter(key_grad, "q", scatter_dimension=0, tiled=True)
        value_grad = lax.psum_scatter(value_grad, "q", scatter_dimension=0, tiled=True)
    query_raw_grad, key_raw_grad, query_gain_grad, key_gain_grad = prepare_pull((query_grad, key_grad))
    projected_grad = jnp.concatenate(
        [query_raw_grad.reshape(count, out_rows), key_raw_grad, value_grad], axis=1
    ).astype(BF)
    first_grad = gathered(dot(projected_grad, weight_head, 1, 0))
    in_term = dot(projected_grad, first, 0, 0)
    input_norm_grad, attn_gain_grad = norm_back(
        first_grad, own_rows(first_normed), own_rows(first_scale), attn_gain
    )
    tokens_grad = home(state_grad + input_norm_grad)
    gain_term = jnp.concatenate([attn_gain_grad, ffn_gain_grad, query_gain_grad, key_gain_grad])

    def placed(term, rows):
        whole = jnp.zeros((rows, width), F32)
        return lax.dynamic_update_slice_in_dim(whole, term, head * term.shape[0], 0)

    return (
        block_out,
        tokens_grad,
        lax.psum_scatter(placed(in_term, QKV_ROWS), EVERY, scatter_dimension=0, tiled=True),
        lax.psum_scatter(placed(out_term, HEADS * HEAD_DIM), EVERY, scatter_dimension=0, tiled=True),
        lax.psum_scatter(gain_term, EVERY, scatter_dimension=0, tiled=True),
        ffn_grad,
    )


LANES = 128
HALF_LANES = 64


def _nt(a, b):
    return lax.dot_general(a, b, (((1,), (1,)), ((), ())), preferred_element_type=F32)


def _nn(a, b):
    return lax.dot_general(a, b, (((1,), (0,)), ((), ())), preferred_element_type=F32)


def _tn(a, b):
    return lax.dot_general(a, b, (((0,), (0,)), ((), ())), preferred_element_type=F32)


MESH = pl.DeviceIdType.MESH
COPIES = 400
LEFT_ALONE = 25


class Wires:
    def __init__(self, sems):
        self.sems = sems
        self.used = 0
        self.pending = []
        self.turn, self.born = 0, {}

    def sem(self):
        self.used += 1
        return self.sems.at[self.used - 1]

    def send(self, src, dst, to, arrives):
        copy = pltpu.make_async_remote_copy(
            src_ref=src, dst_ref=dst, send_sem=self.sem(), recv_sem=arrives,
            device_id=to, device_id_type=MESH,
        )
        copy.start()
        self.pending.append(copy)
        self.born[id(copy)] = self.turn
        return copy

    def local(self, src, dst, arrives):
        copy = pltpu.make_async_copy(src, dst, arrives)
        copy.start()
        return copy

    def arrived(self, ref, sem):
        pltpu.make_async_copy(ref, ref, sem).wait()

    def finish(self, copies=None):
        known = {id(copy) for copy in self.pending}
        copies = [copy for copy in (self.pending if copies is None else copies) if id(copy) in known]
        for copy in copies:
            copy.wait_send()
        done = {id(copy) for copy in copies}
        self.pending = [copy for copy in self.pending if id(copy) not in done]


def block_kernel(
    tok, cot, win, wout, gain_in, wffn, segments, lengths, cos_in, sin_in,
    o_block, o_tokens, o_in, o_out, o_gain, o_ffn,
    x, rel_t, rel_c, w2, wall, wfa, wfb, gb, grow, first2, raw, po,
    q0, q1, kk, vv, prob, att, mxs, mix, sec2, dy2, acta, actb, asend,
    dsb, osb, dsr, osr, rsz, gr, gs, gt, dstate, dmb, daf, dmix,
    dkk, dvv, dqq, dpj, dpx, dfb, dfr, igs, agr, agz, agt, agh, ago,
    bos, obs, bor, tgs, tgr, gg, ggq, gsum, ggt, gain, gflat, doc_col, doc_row, cos_t, sin_t, sems,
):
    dp = lax.axis_index("dp")
    c = lax.axis_index("ctx")
    zh = lax.div(c, 8)
    g = lax.rem(c, 8)
    j = lax.div(g, 2)
    k = lax.rem(c, 2)
    chips = (j, j + 1 - 2 * lax.rem(j, 2), j + 2 - 4 * lax.div(j, 2), 3 - j)
    cores = (k, 1 - k)

    def quad(d, e):
        return (dp, zh * 8 + 2 * chips[d] + cores[e])

    sib = quad(0, 1)
    czp = lax.rem(c + 8, 16)
    zp = (dp, lax.rem(c + 8, 16))
    zps = (dp, 8 * (1 - zh) + 2 * j + 1 - k)
    yp = (1 - dp, c)
    diag = (1 - dp, lax.rem(c + 8, 16))
    team = 2 * dp + zh
    team_y = 2 * (1 - dp) + zh
    team_z = 2 * dp + 1 - zh
    team_d = 3 - team
    w = Wires(sems)
    others = [(d, e) for d in range(4) for e in range(2) if (d, e) != (0, 0)]

    zl, xx = lax.div(j, 2), lax.rem(j, 2)
    keeper = (xx, 8 * k + 4 * dp + 2 * zh + zl)
    owner_of = (zl, 8 * xx + 4 * k + 2 * dp + zh)
    alone = jnp.logical_and(keeper[0] == dp, keeper[1] == c)
    apart = jnp.logical_not(alone)

    barrier = pltpu.get_barrier_semaphore()
    peers = [quad(d, e) for d, e in others] + [zp, zps, yp, diag]
    for peer in peers:
        pl.semaphore_signal(barrier, inc=1, device_id=peer, device_id_type=MESH)

    s_cos, s_sin = w.sem(), w.sem()
    w.local(cos_in, cos_t, s_cos)
    w.local(sin_in, sin_t, s_sin)

    limit = lengths[zh]
    docs = segments[zh].astype(F32).astype(BF)
    line = lax.broadcasted_iota(jnp.int32, (512, 512), 0)
    cell = lax.broadcasted_iota(jnp.int32, (512, 512), 1)
    same_place = (line == cell).astype(F32).astype(BF)
    mirrored = (line + 480 - 2 * (line - lax.rem(line, 32)) == cell).astype(F32).astype(BF)
    for half, order in enumerate((same_place, mirrored)):
        ids = jnp.broadcast_to(docs[half : half + 1, :], (16, 512))
        key = lax.broadcasted_iota(jnp.int32, (1, 512), 1) + 512 * half
        doc_row[0:1, 512 * half : 512 * (half + 1)] = jnp.where(key < limit, _nn(ids, order)[0:1, :], -1.0)
        doc_col[512 * half : 512 * (half + 1), :] = _nt(order, ids)[:, 0:8]
    gain[...] = jnp.zeros_like(gain)
    gain[0:1, 0:68] = gain_in[...].astype(F32)

    @pl.when(apart)
    def _():
        pl.semaphore_signal(barrier, inc=1, device_id=keeper, device_id_type=MESH)
        pl.semaphore_signal(barrier, inc=1, device_id=owner_of, device_id_type=MESH)
        pl.semaphore_wait(barrier, len(peers) + 2)

    @pl.when(alone)
    def _():
        pl.semaphore_wait(barrier, len(peers))

    def many(*shape):
        return [many(*shape[1:]) for _ in range(shape[0])] if shape else w.sem()

    def piece(chip):
        return chip + k * (3 - 2 * chip)

    def row_block(owner, half):
        return owner + half * (15 - 2 * owner)

    my_rows = pl.multiple_of(512 * k, 512)
    other_rows = pl.multiple_of(512 * (1 - k), 512)
    own_head, sib_head = pl.ds(0, 256), pl.ds(256, 256)
    mine = piece(j)
    steps = {}

    def step(name):
        def keep(body):
            steps[name] = body
            return body
        return keep

    def rows_of(buf, offset):
        def at(half, start, count):
            return buf.at[pl.ds(pl.multiple_of(offset * half + start, 32), count)]
        return at

    def rows_steps(name, source, relay, at):
        s_rel, s_here, s_z, s_d = many(2), w.sem(), many(2), w.sem()
        passed = []

        def scatter(src, owner, e, which):
            half = cores[e]
            dst = at(half, pl.multiple_of(row_block(owner, half) * 32, 32), 32)
            w.send(src, dst, quad(2, e), s_z[which])
            w.send(src, dst, quad(1, e), s_here)
            if e == 0:
                w.local(src, dst, s_here)
            else:
                w.send(src, dst, sib, s_here)

        def halves(e):
            @step(f"{name}_out{e}")
            def _():
                w.send(source.at[1 - zh, cores[e]], relay.at[cores[e]], zp, s_rel[e])

            @step(f"{name}_own{e}")
            def _():
                scatter(source.at[zh, cores[e]], c, e, 0)

            @step(f"{name}_rel{e}")
            def _():
                w.arrived(relay.at[cores[e]], s_rel[e])
                scatter(relay.at[cores[e]], czp, e, 1)

            @step(f"{name}_fwd{e}")
            def _():
                first = (zh if e == 0 else 1 - zh) * 8 + 2 * chips[2]
                rows = at(k, pl.multiple_of(32 * (first + k * (14 - 2 * first)), 64), 64)
                w.arrived(rows, s_z[e])
                passed.append(w.send(rows, rows, quad(1, 0), s_d))

        halves(0)
        halves(1)
        return s_here, s_d, passed

    s_x, s_xd, _ = rows_steps("tok", tok, rel_t, rows_of(x, 0))
    s_c, s_cd, cot_passed = rows_steps("cot", cot, rel_c, rows_of(dy2, 512))

    def head_rows(t):
        return w2.at[pl.ds(pl.multiple_of(64 * t, 64), 64)]

    def exchange(name, src, at, keep):
        sem = many(4)

        @step(f"{name}_start")
        def _():
            w.send(src, at(team), zp, sem[1])
            w.send(src, at(team), yp, sem[0])
            if keep:
                w.local(src, at(team), sem[3])

        @step(f"{name}_pass")
        def _():
            w.arrived(at(team_z), sem[1])
            w.send(at(team_z), at(team_z), yp, sem[2])

        def end():
            w.arrived(at(team_y), sem[0])
            w.arrived(at(team_d), sem[2])
            if keep:
                w.arrived(at(team), sem[3])

        return end

    s_move, s_w2, s_gq, s_wq, s_ws = w.sem(), w.sem(), w.sem(), many(3), w.sem()
    gains_end = exchange("gain", gain, lambda t: gb.at[t, g], True)
    heads_end = exchange("win", head_rows(team), head_rows, False)
    wout_end = exchange("wout", wout, lambda t: wall.at[t, j, k], True)
    move = pltpu.make_async_remote_copy(
        src_ref=win, dst_ref=head_rows(lax.rem(g, 4)), send_sem=w.sem(), recv_sem=s_move,
        device_id=keeper, device_id_type=MESH,
    )

    @step("move")
    def _():
        pl.when(apart)(move.start)
        pl.when(alone)(lambda: pltpu.make_async_copy(win, head_rows(team), s_move).start())

    @step("moved")
    def _():
        w.arrived(head_rows(team), s_move)

    @step("gain_end")
    def _():
        gains_end()
        for d, e in others:
            w.send(gb.at[:, g], gb.at[:, g], quad(d, e), s_gq)

    @step("win_end")
    def _():
        heads_end()
        w.send(w2.at[own_head], w2.at[sib_head], sib, s_w2)

    @step("wout_end")
    def _():
        wout_end()
        for d in (2, 1):
            w.send(wall.at[:, j, k], wall.at[:, j, k], quad(d, 0), s_wq[d - 1])

    @step("wout_fwd")
    def _():
        w.arrived(wall.at[:, chips[2], k], s_wq[1])
        w.send(wall.at[:, chips[2], k], wall.at[:, chips[2], k], quad(1, 0), s_wq[2])

    @step("wout_sib")
    def _():
        for d in (1, 3):
            w.arrived(wall.at[:, j, k], s_wq[d - 1])
        w.send(wall.at[:, :, k], wall.at[:, :, k], sib, s_ws)

    parts = ((0, 80, wfa, acta, 320, 384), (80, 64, wfb, actb, 256, 256))
    s_f = many(2, 2, 4, 3)
    held = [[], []]

    def source(part, kind):
        return wffn.at[kind, pl.ds(parts[part][0], parts[part][1])]

    def unit(part, kind, far, slot):
        _, rows, buf, _, _, second = parts[part]
        return buf.at[kind, pl.ds(second * far + rows * slot, rows)]

    def unit_steps(part):
        sem = s_f[part]

        @step(f"u{part}_own")
        def _():
            for kind in range(3):
                w.local(source(part, kind), unit(part, kind, 0, 0), sem[0][0][kind])
                w.send(source(part, kind), unit(part, kind, 1, 0), sib, sem[1][0][kind])
                if part == 0:
                    wfa[kind, 320:384, :] = jnp.zeros((64, 1024), BF)

        @step(f"u{part}_y")
        def _():
            for kind in range(3):
                w.send(source(part, kind), unit(part, kind, 0, 1), yp, sem[0][1][kind])

        def from_z(kind):
            @step(f"u{part}_z{kind}")
            def _():
                w.send(source(part, kind), unit(part, kind, 0, 2), zp, sem[0][2][kind])

            @step(f"u{part}_f{kind}")
            def _():
                here = unit(part, kind, 0, 2)
                w.arrived(here, sem[0][2][kind])
                held[part].append(w.send(here, unit(part, kind, 0, 3), yp, sem[0][3][kind]))
                held[part].append(w.send(here, unit(part, kind, 1, 2), sib, sem[1][2][kind]))

        def ready(slot):
            @step(f"u{part}_s{slot}")
            def _():
                for kind in range(3):
                    here = unit(part, kind, 0, slot)
                    w.arrived(here, sem[0][slot][kind])
                    held[part].append(w.send(here, unit(part, kind, 1, slot), sib, sem[1][slot][kind]))

        for kind in range(3):
            from_z(kind)
        ready(1)
        ready(3)

        @step(f"u{part}_all")
        def _():
            for kind in range(3):
                w.arrived(unit(part, kind, 0, 0), sem[0][0][kind])
                for slot in range(4):
                    w.arrived(unit(part, kind, 1, slot), sem[1][slot][kind])

    unit_steps(0)
    unit_steps(1)

    lane = lax.broadcasted_iota(jnp.int32, (1, LANES), 1)
    low_row = lane < HALF_LANES

    @step("gains")
    def _():
        w.arrived(gb.at[:, pl.ds(0, 7)], s_gq)
        chunks = [jnp.zeros((1, LANES), F32) for _ in range(18)]
        for i in range(32):
            row = gb[i // 8, i % 8, 0:1, :]
            place, shift = divmod(68 * i, LANES)
            moved = pltpu.roll(row, shift, 1) if shift else row
            chunks[place] = chunks[place] + jnp.where(lane >= shift, moved, 0.0)
            if shift + 68 > LANES:
                chunks[place + 1] = chunks[place + 1] + jnp.where(lane < shift, moved, 0.0)
        for n in range(8):
            grow[0:1, LANES * n : LANES * (n + 1)] = chunks[n]
            grow[1:2, LANES * n : LANES * (n + 1)] = chunks[8 + n]
        flipped = pltpu.roll(chunks[16], HALF_LANES, 1)
        grow[2:3, 0:LANES] = jnp.where(low_row, chunks[16], flipped)
        grow[2:3, LANES : 2 * LANES] = jnp.where(low_row, flipped, chunks[16])

    def attn_gain():
        return grow[0:1, :]

    def ffn_gain():
        return grow[1:2, :]

    def query_gain():
        return grow[2:3, 0:LANES]

    def key_gain():
        return grow[2:3, LANES : 2 * LANES]

    s_raw, s_first = w.sem(), w.sem()

    @step("project")
    def _():
        w.arrived(x.at[pl.ds(0, 256)], s_x)
        w.arrived(x.at[pl.ds(0, 128)], s_xd)
        w.arrived(w2.at[sib_head], s_w2)
        weight = attn_gain()

        def rows_of_256(t, carry):
            rows = pl.multiple_of(t * 256, 256)
            values = x[pl.ds(rows, 256), :].astype(F32)
            scale = lax.rsqrt(jnp.mean(values * values, axis=1, keepdims=True) + EPS)
            first = (values * scale * weight).astype(BF)
            here = pl.multiple_of(my_rows + rows, 256)
            first2[pl.ds(here, 256), :] = first
            po[pl.ds(rows, 256), :] = _nt(first, w2[sib_head, :])
            raw[pl.ds(here, 256), :] = _nt(first, w2[own_head, :])
            return carry

        lax.fori_loop(0, 2, rows_of_256, 0)
        w.send(po, raw.at[pl.ds(my_rows, 512)], sib, s_raw)

    @step("first_sib")
    def _():
        w.send(first2.at[pl.ds(my_rows, 512)], first2.at[pl.ds(my_rows, 512)], sib, s_first)

    low = lax.broadcasted_iota(jnp.int32, (256, LANES), 1) < HALF_LANES
    quarter = lax.rem(lax.broadcasted_iota(jnp.int32, (256, LANES), 1), HALF_LANES) < 32

    def swap(v):
        return jnp.where(quarter, pltpu.roll(v, 96, 1), pltpu.roll(v, 32, 1))

    def head_sum(v):
        first = jnp.sum(jnp.where(low, v, 0.0), axis=1, keepdims=True)
        second = jnp.sum(jnp.where(low, 0.0, v), axis=1, keepdims=True)
        return jnp.where(low, first, second)

    def inverse_root(v):
        return lax.rsqrt(head_sum(v * v) * (1.0 / HEAD_DIM) + EPS)

    @step("rotate")
    def _():
        w.arrived(raw.at[pl.ds(0, 512)], s_raw)
        w.arrived(cos_t, s_cos)
        w.arrived(sin_t, s_sin)
        query_weight, key_weight = query_gain(), key_gain()

        def rotate_rows(t, carry):
            rows = pl.ds(pl.multiple_of(t * 256, 256), 256)
            cosine, sine = cos_t[rows, :], sin_t[rows, :]
            query = raw[rows, 0:LANES]
            both = raw[rows, LANES : 2 * LANES]
            query = query * inverse_root(query) * query_weight
            query = (query * cosine + swap(query) * sine) * (HEAD_DIM**-0.5)
            q0[rows, :] = jnp.where(low, query, 0.0).astype(BF)
            q1[rows, :] = jnp.where(low, 0.0, query).astype(BF)
            key = both * inverse_root(both) * key_weight
            key = key * cosine + swap(key) * sine
            kk[rows, :] = jnp.where(low, key, pltpu.roll(key, HALF_LANES, 1)).astype(BF)
            vv[rows, :] = jnp.where(low, pltpu.roll(both, HALF_LANES, 1), both).astype(BF)
            return carry

        lax.fori_loop(0, 4, rotate_rows, 0)

    s_mix, s_md, s_mz = w.sem(), w.sem(), many(2)
    head_lanes = pl.ds(pl.multiple_of(LANES * g, LANES), LANES)
    z_lanes = pl.ds(pl.multiple_of(256 * chips[2], 256), 256)
    late = []

    def forward_tile(t):
        @step(f"at{t}")
        def _():
            lo, n = 256 * t, 256 * (t + 1)
            place = lax.broadcasted_iota(jnp.int32, (256, n), 0) + lo
            key_place = lax.broadcasted_iota(jnp.int32, (256, n), 1)
            same = doc_col[lo : lo + 256, 0:1] == doc_row[0:1, 0:n]
            mask = (same & (key_place <= place)) | (key_place == place)
            outs = []
            for h, q in enumerate((q0, q1)):
                scores = jnp.where(mask, _nt(q[lo : lo + 256, :], kk[0:n, :]), MASKED)
                peak = jnp.max(scores, axis=1, keepdims=True)
                expo = jnp.exp(scores - peak)
                weights = (expo * (1.0 / jnp.sum(expo, axis=1, keepdims=True))).astype(BF)
                prob[h, lo : lo + 256, 0:n] = weights
                outs.append(_nn(weights, vv[0:n, :]))
            attended = jnp.where(low, outs[0], outs[1])
            att[lo : lo + 256, :] = attended
            mxs[lo : lo + 256, :] = attended.astype(BF)
            half = t // 2
            dst = mix.at[pl.ds(256 * (t % 2), 256), head_lanes]
            src = mxs.at[pl.ds(lo, 256)]
            w.send(src, dst, (dp, zh * 8 + 2 * chips[2] + half), s_mz[t % 2])
            w.send(src, dst, (dp, zh * 8 + 2 * chips[1] + half), s_mix)
            away = pltpu.make_async_remote_copy(
                src_ref=src, dst_ref=dst, send_sem=w.sem(), recv_sem=s_mix, device_id=sib, device_id_type=MESH
            )
            pl.when(k == half)(lambda: pltpu.make_async_copy(src, dst, s_mix).start())
            pl.when(k != half)(away.start)
            late.append((half, away))

    def pass_mixed(r):
        @step(f"mix_fwd{r}")
        def _():
            part = mix.at[pl.ds(256 * r, 256), z_lanes]
            w.arrived(part, s_mz[r])
            w.send(part, part, quad(1, 0), s_md)

    for t in range(4):
        forward_tile(t)
    pass_mixed(0)
    pass_mixed(1)

    s_dy, s_sec = w.sem(), w.sem()

    @step("dy")
    def _():
        w.arrived(dy2.at[pl.ds(0, 256)], s_c)
        w.arrived(dy2.at[pl.ds(0, 128)], s_cd)
        w.finish(cot_passed)

        def drop_rows(t, carry):
            rows = pl.ds(pl.multiple_of(my_rows + t * 128, 128), 128)
            place = lax.broadcasted_iota(jnp.int32, (128, 1), 0) + (my_rows + t * 128)
            kept = (place < limit).astype(F32).astype(BF)
            dy2[rows, :] = dy2[rows, :] * kept
            return carry

        lax.fori_loop(0, 4, drop_rows, 0)
        w.send(dy2.at[pl.ds(my_rows, 512)], dy2.at[pl.ds(my_rows, 512)], sib, s_dy)

    def attended_rows(rows):
        total = None
        for n in range(4):
            term = _nn(mix[rows, 256 * n : 256 * (n + 1)], wall[n].reshape(256, 1024))
            total = term if total is None else total + term
        return total

    @step("second")
    def _():
        w.arrived(wall.at[:, :, 0], s_ws)
        w.arrived(mix.at[pl.ds(0, 256)], s_mix)
        w.arrived(mix.at[:, pl.ds(0, 256)], s_md)
        weight = ffn_gain()

        def project_out(t, carry):
            rows = pl.ds(pl.multiple_of(t * 256, 256), 256)
            state = x[rows, :].astype(F32) + attended_rows(rows)
            scale = lax.rsqrt(jnp.mean(state * state, axis=1, keepdims=True) + EPS)
            here = pl.ds(pl.multiple_of(my_rows + t * 256, 256), 256)
            sec2[here, :] = (state * scale * weight).astype(BF)
            return carry

        lax.fori_loop(0, 2, project_out, 0)
        w.send(sec2.at[pl.ds(my_rows, 512)], sec2.at[pl.ds(my_rows, 512)], sib, s_sec)

    class Sum:
        def __init__(self, name, buf, into, which):
            self.buf, self.into, self.which = buf, into, which
            self.sems = many(3, 2)
            for t in range(2):
                if name == "os":
                    step(f"{name}_x{t}")(lambda t=t: self.over_x(t))
                step(f"{name}_z{t}")(lambda t=t: self.over_z(t))

        def rows(self, d, t):
            return pl.ds(pl.multiple_of(256 * t + 64 * piece(chips[d]), 64), 64)

        def over_x(self, t):
            for d, slot in ((3, 1), (1, 0)):
                w.send(self.buf.at[self.rows(d, t)], self.into.at[slot, t], quad(1, 0), self.sems[slot][t])

        def over_z(self, t):
            w.arrived(self.into.at[1, t], self.sems[1][t])
            total = self.buf[self.rows(2, t), :].astype(F32) + self.into[1, t].astype(F32)
            rsz[self.which, t] = total.astype(BF)
            w.send(rsz.at[self.which, t], self.into.at[2, t], quad(2, 0), self.sems[2][t])

        def result(self, t):
            total = self.buf[self.rows(0, t), :].astype(F32)
            for slot in (0, 2):
                w.arrived(self.into.at[slot, t], self.sems[slot][t])
                total = total + self.into[slot, t].astype(F32)
            return total

    sum_ds, sum_os, sum_df = Sum("ds", dsb, dsr, 0), Sum("os", osb, osr, 1), Sum("df", dfb, dfr, 2)

    s_act, s_gr, s_near, s_gt = many(2), many(2, 3), many(2), many(2, 3)
    acted = []

    def part_steps(part):
        start, rows_kept, buf, acts, count, second = parts[part]
        span = pl.ds(start, rows_kept)

        def feed_forward(t):
            @step(f"ff{part}{t}")
            def _():
                if part == 1 and t == 0:
                    w.finish(acted)
                rows = pl.ds(pl.multiple_of(my_rows + 256 * t, 256), 256)
                here = pl.ds(256 * t, 256)
                gate = _nt(sec2[rows, :], buf[0])
                up = _nt(sec2[rows, :], buf[1])
                d_hidden = _nt(dy2[rows, :], buf[2])
                sigmoid = 1.0 / (1.0 + jnp.exp(-gate))
                silu = gate * sigmoid
                d_gate = (d_hidden * up * (sigmoid + silu * (1.0 - sigmoid))).astype(BF)
                d_up = (d_hidden * silu).astype(BF)
                hidden = (silu * up).astype(BF)
                for n, value in enumerate((d_gate, d_up, hidden)):
                    acts[n, rows, :] = value[:, 0:second]
                    asend[n, here, 0:count] = value[:, second : second + count]
                lanes = pl.ds(0, second)
                acted.append(w.send(asend.at[:, here, lanes], acts.at[:, rows], sib, s_act[part]))
                d_second = _nn(d_gate, buf[0]) + _nn(d_up, buf[1])
                result = _nn(hidden, buf[2])
                if part == 1:
                    d_second = d_second + dsb[here, :].astype(F32)
                    result = result + osb[here, :].astype(F32)
                dsb[here, :] = d_second.astype(BF)
                osb[here, :] = result.astype(BF)
                if part == 1:
                    sum_ds.over_x(t)

        @step(f"wg{part}_in")
        def _():
            w.finish(held[part])
            w.arrived(acts.at[:, pl.ds(0, 512)], s_act[part])
            if part == 0:
                w.arrived(sec2.at[pl.ds(0, 512)], s_sec)
                w.arrived(dy2.at[pl.ds(0, 512)], s_dy)

        def weight_grads(kind):
            @step(f"wg{part}{kind}")
            def _():
                right = dy2 if kind == 2 else sec2

                def columns(n, carry):
                    cols = pl.ds(pl.multiple_of(n * 512, 512), 512)
                    buf[kind, 0:count, cols] = _tn(acts[kind], right[:, cols])[0:count, :].astype(BF)
                    return carry

                lax.fori_loop(0, 2, columns, 0)

        def pass_grads(kind):
            @step(f"gr{part}_y{kind}")
            def _():
                rows = buf.at[kind, pl.ds(rows_kept * 3, rows_kept)]
                w.send(rows, gr.at[1, kind, span], yp, s_gr[part][kind])

            @step(f"gr{part}_z{kind}")
            def _():
                w.arrived(gr.at[1, kind, span], s_gr[part][kind])
                gs[kind, span, :] = (
                    buf[kind, 2 * rows_kept : 3 * rows_kept, :].astype(F32) + gr[1, kind, span, :].astype(F32)
                ).astype(BF)
                w.send(gs.at[kind, span], gt.at[kind, span], zp, s_gt[part][kind])

        @step(f"gr{part}_near")
        def _():
            w.send(buf.at[:, pl.ds(rows_kept, rows_kept)], gr.at[0, :, span], yp, s_near[part])

        @step(f"gr{part}_end")
        def _():
            w.arrived(gr.at[0, :, span], s_near[part])
            for kind in range(3):
                w.arrived(gt.at[kind, span], s_gt[part][kind])
                o_ffn[kind, span, :] = (
                    buf[kind, 0:rows_kept, :].astype(F32)
                    + gr[0, kind, span, :].astype(F32) + gt[kind, span, :].astype(F32)
                )

        feed_forward(0)
        feed_forward(1)
        for kind in range(3):
            weight_grads(kind)
            pass_grads(kind)

    part_steps(0)
    part_steps(1)

    s_dm, s_da, s_das = w.sem(), many(3), w.sem()
    terms = {"ffn": jnp.zeros((1, 1024), F32), "attn": jnp.zeros((1, 1024), F32)}

    def state_steps(t):
        @step(f"st{t}")
        def _():
            start = 256 * t + 64 * mine
            rows = pl.ds(pl.multiple_of(start, 64), 64)
            state = x[rows, :].astype(F32) + attended_rows(rows)
            bos[t] = state
            scale = lax.rsqrt(jnp.mean(state * state, axis=1, keepdims=True) + EPS)
            normed = state * scale
            total = sum_ds.result(t)
            terms["ffn"] = terms["ffn"] + jnp.sum(total * normed, axis=0, keepdims=True)
            weighted = total * ffn_gain()
            inner = jnp.mean(weighted * normed, axis=1, keepdims=True)
            grad = dy2[pl.ds(pl.multiple_of(my_rows + start, 64), 64), :].astype(F32) + scale * (weighted - normed * inner)
            dstate[t] = grad
            low_grad = grad.astype(BF)
            daf[k, t, mine] = low_grad
            for n in range(4):
                dmb[t, :, 256 * n : 256 * (n + 1)] = _nt(low_grad, wall[n].reshape(256, 1024)).astype(BF)
            for d, e in others:
                lanes = pl.ds(pl.multiple_of(LANES * (2 * chips[d] + cores[e]), LANES), LANES)
                w.send(dmb.at[t, :, lanes], dmix.at[k, t, mine], quad(d, e), s_dm)
            w.local(dmb.at[t, :, head_lanes], dmix.at[k, t, mine], s_dm)

    state_steps(0)
    state_steps(1)

    @step("da_out")
    def _():
        for d in (2, 1):
            w.send(daf.at[k, :, mine], daf.at[k, :, mine], quad(d, 0), s_da[d - 1])

    @step("da_fwd")
    def _():
        far = piece(chips[2])
        w.arrived(daf.at[k, :, far], s_da[1])
        w.send(daf.at[k, :, far], daf.at[k, :, far], quad(1, 0), s_da[2])

    @step("da_sib")
    def _():
        for d in (1, 3):
            w.arrived(daf.at[k, :, mine], s_da[d - 1])
        w.send(daf.at[k], daf.at[k], sib, s_das)

    home = zh + k * (1 - 2 * zh)

    def send_home(buf, into, sem):
        w.send(buf.at[1 - home, 0], into.at[zh, k], zp, sem)
        w.send(buf.at[1 - home, 1], into.at[zh, k], zps, sem)
        w.send(buf.at[home, 1], into.at[zh, k], sib, sem)
        w.local(buf.at[home, 0], into.at[zh, k], sem)

    s_bo, s_tg = w.sem(), w.sem()

    @step("block")
    def _():
        for t in range(2):
            total = bos[t] + sum_os.result(t)
            obs[t] = total.astype(BF).reshape(2, 32, 1024)
        send_home(obs, bor, s_bo)

    @step("block_end")
    def _():
        w.arrived(bor, s_bo)
        o_block[...] = bor[...]

    @step("bw_in")
    def _():
        w.arrived(dmix, s_dm)
        dkk[...] = jnp.zeros_like(dkk)
        dvv[...] = jnp.zeros_like(dvv)

    def backward_tile(t):
        @step(f"bw{t}")
        def _():
            lo, n = 256 * t, 256 * (t + 1)
            d_out = dmix[...].reshape(1024, LANES)[lo : lo + 256, :].astype(F32)
            product = d_out * att[lo : lo + 256, :]
            results = []
            for h, q in enumerate((q0, q1)):
                here = low if h == 0 else jnp.logical_not(low)
                d_head = jnp.where(here, d_out, 0.0).astype(BF)
                delta = jnp.sum(jnp.where(here, product, 0.0), axis=1, keepdims=True)
                weights = prob[h, lo : lo + 256, 0:n]
                pulled = _nt(d_head, vv[0:n, :])
                d_scores = (weights.astype(F32) * (pulled - delta)).astype(BF)
                results.append(_nn(d_scores, kk[0:n, :]))
                dkk[0:n, :] += _tn(d_scores, q[lo : lo + 256, :])
                dvv[0:n, :] += _tn(weights, d_head)
            dqq[lo : lo + 256, :] = jnp.where(low, results[0], results[1]) * (HEAD_DIM**-0.5)

    for t in range(4):
        backward_tile(t)
    s_dpx = w.sem()

    @step("back")
    def _():
        query_weight, key_weight = query_gain(), key_gain()

        def back_rows(t, carry):
            query_sum, key_sum = carry
            rows = pl.ds(pl.multiple_of(t * 256, 256), 256)
            cosine, sine = cos_t[rows, :], sin_t[rows, :]
            query = raw[rows, 0:LANES]
            both = raw[rows, LANES : 2 * LANES]

            def through(values, grads, gain_row):
                scale = inverse_root(values)
                normed = values * scale
                grads = grads * cosine - swap(grads) * sine
                weighted = grads * gain_row
                inner = head_sum(weighted * normed) * (1.0 / HEAD_DIM)
                return scale * (weighted - normed * inner), jnp.sum(grads * normed, axis=0, keepdims=True)

            query_back, query_term = through(query, dqq[rows, :], query_weight)
            d_key = dkk[rows, :]
            d_key = d_key + pltpu.roll(d_key, HALF_LANES, 1)
            key_back, key_term = through(both, d_key, key_weight)
            d_value = dvv[rows, :]
            d_value = d_value + pltpu.roll(d_value, HALF_LANES, 1)
            dpj[rows, 0:LANES] = query_back.astype(BF)
            dpj[rows, LANES : 2 * LANES] = jnp.where(low, key_back, d_value).astype(BF)
            return query_sum + query_term, key_sum + key_term

        zero_row = jnp.zeros((1, LANES), F32)
        query_sum, key_sum = lax.fori_loop(0, 4, back_rows, (zero_row, zero_row))
        w.send(dpj.at[pl.ds(other_rows, 512)], dpx, sib, s_dpx)
        gg[:, 2 * LANES : 3 * LANES] = jnp.zeros((8, LANES), F32)
        gg[0:1, 2 * LANES : 3 * LANES] = query_sum + pltpu.roll(query_sum, HALF_LANES, 1)
        gg[1:2, 2 * LANES : 3 * LANES] = key_sum

    def first_steps(t):
        @step(f"df{t}")
        def _():
            if t == 0:
                w.arrived(dpx, s_dpx)
            here = pl.ds(256 * t, 256)
            rows = pl.ds(pl.multiple_of(my_rows + 256 * t, 256), 256)
            dfb[here, :] = (_nn(dpj[rows, :], w2[own_head, :]) + _nn(dpx[here, :], w2[sib_head, :])).astype(BF)
            sum_df.over_x(t)

    first_steps(0)
    first_steps(1)
    returned = []

    def term_steps(name, rows, value, result):
        sem = many(4)

        @step(f"{name}_y")
        def _():
            term = value()
            count = rows.stop - rows.start
            for p in range(4):
                igs[p, rows, :] = term[count * p : count * (p + 1), :].astype(BF)
            at = pl.ds(rows.start, count)
            w.send(igs.at[team_d, at], agr.at[1, at], yp, sem[1])
            w.send(igs.at[team_y, at], agr.at[0, at], yp, sem[0])

        at = pl.ds(rows.start, rows.stop - rows.start)

        @step(f"{name}_z")
        def _():
            w.arrived(agr.at[1, at], sem[1])
            agz[rows, :] = (igs[team_z, rows, :].astype(F32) + agr[1, rows, :].astype(F32)).astype(BF)
            w.send(agz.at[at], agt.at[at], zp, sem[2])

        @step(f"{name}_sum")
        def _():
            w.arrived(agr.at[0, at], sem[0])
            w.arrived(agt.at[at], sem[2])
            agh[rows, :] = (
                igs[team, rows, :].astype(F32) + agr[0, rows, :].astype(F32) + agt[rows, :].astype(F32)
            ).astype(BF)

        back = pltpu.make_async_remote_copy(
            src_ref=agh.at[at], dst_ref=ago.at[at], send_sem=w.sem(), recv_sem=sem[3],
            device_id=owner_of, device_id_type=MESH,
        )
        returned.append(back)

        @step(f"{name}_give")
        def _():
            pl.when(apart)(back.start)
            pl.when(alone)(lambda: pltpu.make_async_copy(agh.at[at], ago.at[at], sem[3]).start())

        @step(f"{name}_end")
        def _():
            w.arrived(ago.at[at], sem[3])
            result[...] = ago[rows, :]

    def in_value():
        w.arrived(first2.at[pl.ds(0, 512)], s_first)
        return _tn(dpj[...], first2[...])

    def out_value():
        w.arrived(daf.at[0], s_das)
        return _tn(mxs[...], daf[...].reshape(1024, 1024))

    term_steps("in", slice(0, 64), in_value, o_in)
    term_steps("out", slice(64, 96), out_value, o_out)

    def token_steps(t):
        @step(f"tg{t}")
        def _():
            rows = pl.ds(pl.multiple_of(256 * t + 64 * mine, 64), 64)
            values = x[rows, :].astype(F32)
            scale = lax.rsqrt(jnp.mean(values * values, axis=1, keepdims=True) + EPS)
            normed = values * scale
            total = sum_df.result(t)
            terms["attn"] = terms["attn"] + jnp.sum(total * normed, axis=0, keepdims=True)
            weighted = total * attn_gain()
            inner = jnp.mean(weighted * normed, axis=1, keepdims=True)
            grad = dstate[t] + scale * (weighted - normed * inner)
            tgs[t] = grad.astype(BF).reshape(2, 32, 1024)

    token_steps(0)
    token_steps(1)

    @step("tok_home")
    def _():
        send_home(tgs, tgr, s_tg)

    @step("tok_end")
    def _():
        w.arrived(tgr, s_tg)
        o_tokens[...] = tgr[...]

    s_gg, s_gt4 = w.sem(), many(3)

    @step("gg_out")
    def _():
        for n in range(8):
            gg[n : n + 1, 0:LANES] = terms["attn"][:, LANES * n : LANES * (n + 1)]
            gg[n : n + 1, LANES : 2 * LANES] = terms["ffn"][:, LANES * n : LANES * (n + 1)]
        for d, e in others:
            w.send(gg, ggq.at[g], quad(d, e), s_gg)
        w.local(gg, ggq.at[g], s_gg)

    @step("gg_sum")
    def _():
        w.arrived(ggq, s_gg)
        total = ggq[0]
        for n in range(1, 8):
            total = total + ggq[n]
        gsum[...] = total
        for n, peer in enumerate((yp, zp, diag)):
            w.send(gsum, ggt.at[n], peer, s_gt4[n])

    @step("gg_end")
    def _():
        total = gsum[...]
        for n in range(3):
            w.arrived(ggt.at[n], s_gt4[n])
            total = total + ggt[n]
        gflat[0:8, :] = total[:, 0:LANES]
        gflat[8:16, :] = total[:, LANES : 2 * LANES]
        key_part = pltpu.roll(total[1:2, 2 * LANES : 3 * LANES], HALF_LANES, 1)
        gflat[16:17, :] = jnp.where(low_row, total[0:1, 2 * LANES : 3 * LANES], key_part)
        place = 68 * (8 * team + g)
        line, shift = lax.div(place, LANES), lax.rem(place, LANES)
        back = lax.rem(LANES - shift, LANES)
        left = pltpu.roll(gflat[pl.ds(line, 1), :], back, 1)
        right = pltpu.roll(gflat[pl.ds(line + 1, 1), :], back, 1)
        o_gain[...] = jnp.where(lane < LANES - shift, left, right)[:, 0:68]

    for turn, name in enumerate(ORDER):
        w.turn = turn
        steps.pop(name)()
        w.finish([copy for copy in w.pending if w.born[id(copy)] < turn - LEFT_ALONE])
    assert not steps, sorted(steps)
    w.finish()
    for half, away in late:
        pl.when(k != half)(away.wait_send)
    pl.when(apart)(move.wait_send)
    for back in returned:
        pl.when(apart)(back.wait_send)


ORDER = (
    "tok_out0", "cot_own1", "wout_start", "tok_out1", "cot_own0", "u0_y", "u1_own", "tok_own0", "move",
    "tok_own1", "gain_start", "tok_rel0", "wout_pass", "cot_out0", "cot_fwd0", "tok_rel1", "gain_pass",
    "moved", "cot_out1", "u0_s1", "gain_end", "win_start", "tok_fwd1", "tok_fwd0", "wout_end", "win_pass",
    "u0_z1", "gains", "win_end", "u0_own", "cot_rel1", "project", "u1_y", "u0_z0", "wout_fwd", "cot_rel0",
    "u0_z2", "rotate", "at1", "u0_f1", "at3", "u0_f0", "at0", "at2", "u1_z2", "cot_fwd1", "mix_fwd1", "u0_f2",
    "mix_fwd0", "wout_sib", "u1_f2", "u0_s3", "u1_z1", "u0_all", "u1_z0", "dy", "second", "ff00", "u1_f1",
    "ff01", "first_sib", "u1_f0", "u1_s1", "wg0_in", "wg01", "gr0_y1", "wg00", "u1_s3", "gr0_y0", "u1_all",
    "ff10", "gr0_z1", "ff11", "ds_z0", "wg02", "gr0_z0", "wg1_in", "wg11", "wg12", "gr1_y1", "os_x0",
    "gr0_y2", "wg10", "gr1_y2", "ds_z1", "gr1_y0", "st0", "gr1_z1", "st1", "gr0_near", "gr0_z2", "da_out",
    "os_x1", "bw_in", "bw3", "bw2", "bw1", "gr1_z0", "bw0", "back", "gr1_z2", "os_z0", "os_z1", "da_fwd",
    "in_y", "gr1_near", "df0", "in_z", "da_sib", "df_z0", "df1", "out_y", "block", "in_sum", "df_z1", "tg0",
    "out_z", "in_give", "gr1_end", "tg1", "out_sum", "tok_home", "gg_out", "gg_sum", "in_end", "out_give",
    "block_end", "gr0_end", "tok_end", "gg_end", "out_end",
)


TEAM_SCRATCH = (
    ((512, 1024), BF), ((2, 32, 1024), BF), ((2, 32, 1024), BF), ((512, 1024), BF),
    ((4, 4, 2, 32, 1024), BF), ((3, 704, 1024), BF), ((3, 512, 1024), BF), ((4, 8, 8, 128), F32), ((8, 1024), F32),
    ((1024, 1024), BF), ((1024, 256), F32), ((512, 256), F32),
    ((1024, 128), BF), ((1024, 128), BF), ((1024, 128), BF), ((1024, 128), BF), ((2, 1024, 1024), BF),
    ((1024, 128), F32), ((1024, 128), BF), ((512, 1024), BF), ((1024, 1024), BF), ((1024, 1024), BF),
    ((3, 1024, 384), BF), ((3, 1024, 256), BF), ((3, 512, 384), BF),
    ((512, 1024), BF), ((512, 1024), BF), ((3, 2, 64, 1024), BF), ((3, 2, 64, 1024), BF), ((3, 2, 64, 1024), BF),
    ((2, 3, 144, 1024), BF), ((3, 144, 1024), BF), ((3, 144, 1024), BF),
    ((2, 64, 1024), F32), ((2, 64, 1024), BF), ((2, 2, 4, 64, 1024), BF), ((2, 2, 4, 64, 128), BF),
    ((1024, 128), F32), ((1024, 128), F32), ((1024, 128), F32), ((1024, 256), BF), ((512, 256), BF),
    ((512, 1024), BF), ((3, 2, 64, 1024), BF),
    ((4, 96, 1024), BF), ((2, 96, 1024), BF), ((96, 1024), BF), ((96, 1024), BF), ((96, 1024), BF), ((96, 1024), BF),
    ((2, 64, 1024), F32), ((2, 2, 32, 1024), BF), ((2, 2, 32, 1024), BF), ((2, 2, 32, 1024), BF),
    ((2, 2, 32, 1024), BF),
    ((8, 384), F32), ((8, 8, 384), F32), ((8, 384), F32), ((3, 8, 384), F32), ((8, 128), F32), ((24, 128), F32), ((1024, 8), F32), ((8, 1024), F32),
    ((1024, 128), F32), ((1024, 128), F32),
)


def rotary_lanes(rows):
    width = HEAD_DIM // 2
    freq = (ROPE_BASE ** (-np.arange(width, dtype=np.float32) * np.float32(2.0 / HEAD_DIM))).astype(np.float32)
    angle = (np.arange(rows, dtype=np.float32)[:, None] * freq).astype(np.float32).astype(np.float64)
    cosine, sine = np.cos(angle), np.sin(angle)
    return (
        np.tile(np.concatenate([cosine, cosine], 1), (1, 2)).astype(np.float32),
        np.tile(np.concatenate([-sine, sine], 1), (1, 2)).astype(np.float32),
    )


def on_team(tokens, segments, lengths, attn_in, attn_out, gains, ffn_weights, cotangent):
    batches, block_len, halves, width = tokens.shape
    rows = segments.shape[1]
    cosine, sine = rotary_lanes(2 * rows)
    args = (
        tokens.transpose(0, 2, 1, 3),
        cotangent.transpose(0, 2, 1, 3),
        attn_in,
        attn_out,
        gains[None],
        ffn_weights.transpose(1, 0, 2),
        segments.transpose(0, 2, 1),
        lengths,
        jnp.asarray(cosine),
        jnp.asarray(sine),
    )
    vmem = pl.BlockSpec(memory_space=pltpu.VMEM)
    anywhere = pl.BlockSpec(memory_space=pl.ANY)
    outs = pl.pallas_call(
        block_kernel,
        out_shape=(
            jax.ShapeDtypeStruct((2, 2, 32, 1024), BF),
            jax.ShapeDtypeStruct((2, 2, 32, 1024), BF),
            jax.ShapeDtypeStruct((64, 1024), BF),
            jax.ShapeDtypeStruct((32, 1024), BF),
            jax.ShapeDtypeStruct((1, 68), F32),
            jax.ShapeDtypeStruct((3, 144, 1024), F32),
        ),
        in_specs=[vmem] * 5
        + [anywhere, vmem, pl.BlockSpec(memory_space=pltpu.SMEM), anywhere, anywhere],
        out_specs=(vmem,) * 6,
        scratch_shapes=[pltpu.VMEM(shape, kind) for shape, kind in TEAM_SCRATCH]
        + [pltpu.SemaphoreType.DMA((COPIES,))],
        compiler_params=pltpu.CompilerParams(
            collective_id=0, has_side_effects=True, vmem_limit_bytes=VMEM_BYTES
        ),
    )(*args)
    block, token_grad, in_grad, out_grad, gain_grad, unit_grad = outs
    return (
        block.transpose(0, 2, 1, 3),
        token_grad.transpose(0, 2, 1, 3).astype(F32),
        in_grad.astype(F32),
        out_grad.astype(F32),
        gain_grad[0],
        unit_grad.transpose(1, 0, 2),
    )


VMEM_BYTES = 62 << 20


def solution(mesh):
    dp, ctx = mesh.devices.shape
    if ctx == 2 * KV_HEADS:
        ring = "ctx"
        every = ("dp", "ctx")
        team, run = mesh, on_team
    else:
        ring = ("s", "q", "g")
        every = EVERY
        team = Mesh(mesh.devices.reshape(dp, 2, ctx // (2 * KV_HEADS), KV_HEADS), EVERY)
        run = on_device
    placed = (
        P("dp", ring, None, None),
        P("dp", None, None),
        P("dp"),
        P(every, None),
        P(every, None),
        P(every),
        P(every, None, None),
        P("dp", ring, None, None),
    )
    return jax.shard_map(
        run,
        mesh=team,
        in_specs=placed,
        out_specs=(
            P("dp", ring, None, None),
            P("dp", ring, None, None),
            P(every, None),
            P(every, None),
            P(every),
            P(every, None, None),
        ),
        check_vma=False,
    )
```

```python
import jax
import jax.numpy as jnp
import numpy as np
from jax import lax
from jax.experimental import pallas as pl
from jax.experimental.pallas import tpu as pltpu
from jax.sharding import Mesh
from jax.sharding import PartitionSpec as P

FF = 4608
HEADS = 16
KV_HEADS = 8
HEAD_DIM = 64
GROUP = HEADS // KV_HEADS
QKV_ROWS = 2048

EPS = 1e-05
ROPE_BASE = 1000000.0
MASKED = -1e30
BF = jnp.bfloat16
F32 = jnp.float32


def root_mean(values):
    return lax.rsqrt(jnp.mean(values * values, axis=-1, keepdims=True) + EPS)


def rotate(values, cosine, sine):
    width = values.shape[-1] // 2
    first = values[..., :width]
    second = values[..., width:]
    return jnp.concatenate(
        [first * cosine - second * sine, second * cosine + first * sine], axis=-1
    )


def tables(positions):
    width = HEAD_DIM // 2
    freq = ROPE_BASE ** (-jnp.arange(width, dtype=F32) * 2.0 / HEAD_DIM)
    angle = positions.astype(F32)[..., None] * freq
    return (jnp.cos(angle), jnp.sin(angle))


def prepare(query_raw, key_raw, query_gain, key_gain, cosine, sine):
    query_norm = query_raw * root_mean(query_raw) * query_gain
    key_norm = key_raw * root_mean(key_raw) * key_gain
    return (
        rotate(query_norm, cosine[:, None], sine[:, None]),
        rotate(key_norm, cosine, sine),
    )


def norm_back(grad, normed, scale_rows, gain):
    weighted = grad * gain
    inner = jnp.mean(weighted * normed, axis=-1, keepdims=True)
    return (scale_rows * (weighted - normed * inner), jnp.sum(grad * normed, axis=0))


def dot(a, b, ca, cb):
    return lax.dot_general(a, b, (((ca,), (cb,)), ((), ())), preferred_element_type=F32)


TEAM = ("dp", "s", "q")
EVERY = ("dp", "s", "q", "g")


def spread(local, block_len):
    mine = lax.all_to_all(local, "s", 0, 0, tiled=True)
    return lax.all_gather(mine, "g", axis=0, tiled=False)


def on_device(tokens, segments, lengths, attn_in, attn_out, gains, ffn_weights, cotangent):
    batches, block_len, halves, width = tokens.shape
    seq = lax.axis_index("s")
    quarter = lax.axis_index("q")
    head = lax.axis_index("g")
    quarters = lax.axis_size("q")
    heads = lax.axis_size("g")
    ctx_count = 2 * quarters * heads
    scale = HEAD_DIM ** (-0.5)
    weight_in = lax.all_gather(attn_in, EVERY, axis=0, tiled=True)
    weight_out = lax.all_gather(attn_out, EVERY, axis=0, tiled=True)
    gain_all = lax.all_gather(gains, EVERY, axis=0, tiled=True).astype(F32)
    attn_gain = gain_all[:width]
    ffn_gain = gain_all[width : 2 * width]
    query_gain = gain_all[2 * width : 2 * width + HEAD_DIM]
    key_gain = gain_all[2 * width + HEAD_DIM :]
    head_rows = (GROUP + 2) * HEAD_DIM
    out_rows = GROUP * HEAD_DIM
    weight_head = lax.dynamic_slice_in_dim(weight_in, head * head_rows, head_rows, 0)
    weight_mix = lax.dynamic_slice_in_dim(weight_out, head * out_rows, out_rows, 0)

    inputs = spread(tokens, block_len)
    count = inputs.size // width
    inputs = inputs.reshape(count, width).astype(F32)
    cot = spread(cotangent, block_len).reshape(count, width).astype(F32)

    def places(which):
        owner_g = jnp.arange(heads, dtype=jnp.int32)[:, None, None, None]
        owner_s = jnp.arange(2, dtype=jnp.int32)[None, :, None, None]
        row = jnp.arange(block_len, dtype=jnp.int32)[None, None, :, None]
        half = jnp.arange(2, dtype=jnp.int32)[None, None, None, :]
        owner = owner_s * (quarters * heads) + which * heads + owner_g
        block = jnp.where(half == 0, owner, 2 * ctx_count - 1 - owner)
        return (
            (block * block_len + row).reshape(count),
            jnp.broadcast_to((owner * block_len + row) * 2 + half, (heads, 2, block_len, 2)).reshape(count),
        )

    docs = lax.dynamic_index_in_dim(segments, seq, 0, False).reshape(-1)
    length = lax.dynamic_index_in_dim(lengths, seq, 0, False)
    place, slot = places(quarter)
    key_place, key_slot = jax.vmap(places)(jnp.arange(quarters, dtype=jnp.int32))
    key_place = key_place.reshape(-1)
    query_doc = docs[slot]
    key_doc = docs[key_slot.reshape(-1)]
    causal = key_place[None, :] <= place[:, None]
    live = (key_place[None, :] < length) | (key_place[None, :] == place[:, None])
    mask = causal & live & (query_doc[:, None] == key_doc[None, :])
    valid = (place < length).astype(F32)[:, None]

    first_scale = root_mean(inputs)
    first_normed = inputs * first_scale
    first = (first_normed * attn_gain).astype(BF)
    projected = dot(first, weight_head, 1, 1).reshape(count, GROUP + 2, HEAD_DIM)
    cosine, sine = tables(place)

    def prepare_here(query_raw, key_raw, gain_query, gain_key):
        return prepare(query_raw, key_raw, gain_query, gain_key, cosine, sine)

    (query_rot, key_rot), prepare_pull = jax.vjp(
        prepare_here, projected[:, :GROUP], projected[:, GROUP], query_gain, key_gain
    )
    queries = query_rot.astype(BF)
    pair = jnp.stack([key_rot.astype(BF), projected[:, GROUP + 1].astype(BF)])
    pair = lax.all_gather(pair, "q", axis=1, tiled=True)
    keys, values = pair[0], pair[1]

    scores = jnp.einsum("qjd,kd->jqk", queries, keys, preferred_element_type=F32) * scale
    scores = jnp.where(mask[None], scores, MASKED)
    peak = jnp.max(scores, axis=-1, keepdims=True)
    expo = jnp.where(mask[None], jnp.exp(scores - peak), 0.0)
    weights = expo / jnp.sum(expo, axis=-1, keepdims=True)
    attended = jnp.einsum("jqk,kd->qjd", weights.astype(BF), values, preferred_element_type=F32)
    mixed_here = attended.astype(BF).reshape(count, out_rows)
    mixed = lax.all_gather(mixed_here, "g", axis=1, tiled=True)
    state = inputs + dot(mixed, weight_out, 1, 0)
    second_scale = root_mean(state)
    second_normed = state * second_scale
    second = (second_normed * ffn_gain).astype(BF)
    grad_out = cot * valid
    grad_low = grad_out.astype(BF)

    units = lax.all_gather(ffn_weights, TEAM, axis=0, tiled=True)
    unit_gate, unit_up, unit_down = units[:, 0], units[:, 1], units[:, 2]
    gate = dot(second, unit_gate, 1, 1)
    upward = dot(second, unit_up, 1, 1)
    sigmoid = jax.nn.sigmoid(gate)
    hidden = (gate * sigmoid * upward).astype(BF)
    d_hidden = dot(grad_low, unit_down, 1, 1)
    d_gate = (d_hidden * upward * sigmoid * (1.0 + gate * (1.0 - sigmoid))).astype(BF)
    d_up = (d_hidden * gate * sigmoid).astype(BF)
    d_second = dot(d_gate, unit_gate, 1, 0) + dot(d_up, unit_up, 1, 0)
    own = count // heads

    def gathered(values):
        return lax.psum_scatter(values.astype(BF), "g", scatter_dimension=0, tiled=True).astype(F32)

    def own_rows(values):
        return lax.dynamic_slice_in_dim(values, head * own, own, 0)

    def home(values):
        back = values.reshape(2, block_len, halves, width)
        return lax.all_to_all(back, "s", 0, 0, tiled=True)

    ffn_sum = gathered(dot(hidden, unit_down, 1, 0))
    block_out = home((own_rows(state) + ffn_sum).astype(BF))
    ffn_grad = lax.psum_scatter(
        jnp.stack([dot(d_gate, second, 0, 0), dot(d_up, second, 0, 0), dot(hidden, grad_low, 0, 0)], axis=1),
        TEAM,
        scatter_dimension=0,
        tiled=True,
    )
    norm_grad, ffn_gain_grad = norm_back(
        gathered(d_second), own_rows(second_normed), own_rows(second_scale), ffn_gain
    )
    state_grad = own_rows(grad_out) + norm_grad
    attended_grad = lax.all_gather(state_grad.astype(BF), "g", axis=0, tiled=True)
    mixed_grad = dot(attended_grad, weight_mix, 1, 1).astype(BF)
    out_term = dot(mixed_here, attended_grad, 0, 0)
    mixed_grad = mixed_grad.reshape(count, GROUP, HEAD_DIM)
    delta = jnp.sum(mixed_grad.astype(F32) * attended, axis=-1).T[:, :, None]
    pulled = jnp.einsum("qjd,kd->jqk", mixed_grad, values, preferred_element_type=F32)
    score_grad = (weights * (pulled - delta)).astype(BF)
    query_grad = jnp.einsum("jqk,kd->qjd", score_grad, keys, preferred_element_type=F32) * scale
    key_grad = jnp.einsum("jqk,qjd->kd", score_grad, queries, preferred_element_type=F32) * scale
    value_grad = jnp.einsum("jqk,qjd->kd", weights.astype(BF), mixed_grad, preferred_element_type=F32)
    if quarters > 1:
        key_grad = lax.psum_scatter(key_grad, "q", scatter_dimension=0, tiled=True)
        value_grad = lax.psum_scatter(value_grad, "q", scatter_dimension=0, tiled=True)
    query_raw_grad, key_raw_grad, query_gain_grad, key_gain_grad = prepare_pull((query_grad, key_grad))
    projected_grad = jnp.concatenate(
        [query_raw_grad.reshape(count, out_rows), key_raw_grad, value_grad], axis=1
    ).astype(BF)
    first_grad = gathered(dot(projected_grad, weight_head, 1, 0))
    in_term = dot(projected_grad, first, 0, 0)
    input_norm_grad, attn_gain_grad = norm_back(
        first_grad, own_rows(first_normed), own_rows(first_scale), attn_gain
    )
    tokens_grad = home(state_grad + input_norm_grad)
    gain_term = jnp.concatenate([attn_gain_grad, ffn_gain_grad, query_gain_grad, key_gain_grad])

    def placed(term, rows):
        whole = jnp.zeros((rows, width), F32)
        return lax.dynamic_update_slice_in_dim(whole, term, head * term.shape[0], 0)

    return (
        block_out,
        tokens_grad,
        lax.psum_scatter(placed(in_term, QKV_ROWS), EVERY, scatter_dimension=0, tiled=True),
        lax.psum_scatter(placed(out_term, HEADS * HEAD_DIM), EVERY, scatter_dimension=0, tiled=True),
        lax.psum_scatter(gain_term, EVERY, scatter_dimension=0, tiled=True),
        ffn_grad,
    )


LANES = 128
HALF_LANES = 64


def _nt(a, b):
    return lax.dot_general(a, b, (((1,), (1,)), ((), ())), preferred_element_type=F32)


def _nn(a, b):
    return lax.dot_general(a, b, (((1,), (0,)), ((), ())), preferred_element_type=F32)


def _tn(a, b):
    return lax.dot_general(a, b, (((0,), (0,)), ((), ())), preferred_element_type=F32)


MESH = pl.DeviceIdType.MESH
COPIES = 400
LEFT_ALONE = 25


class Wires:
    def __init__(self, sems):
        self.sems = sems
        self.used = 0
        self.pending = []
        self.turn, self.born = 0, {}

    def sem(self):
        self.used += 1
        return self.sems.at[self.used - 1]

    def send(self, src, dst, to, arrives):
        copy = pltpu.make_async_remote_copy(
            src_ref=src, dst_ref=dst, send_sem=self.sem(), recv_sem=arrives,
            device_id=to, device_id_type=MESH,
        )
        copy.start()
        self.pending.append(copy)
        self.born[id(copy)] = self.turn
        return copy

    def local(self, src, dst, arrives):
        copy = pltpu.make_async_copy(src, dst, arrives)
        copy.start()
        return copy

    def arrived(self, ref, sem):
        pltpu.make_async_copy(ref, ref, sem).wait()

    def finish(self, copies=None):
        known = {id(copy) for copy in self.pending}
        copies = [copy for copy in (self.pending if copies is None else copies) if id(copy) in known]
        for copy in copies:
            copy.wait_send()
        done = {id(copy) for copy in copies}
        self.pending = [copy for copy in self.pending if id(copy) not in done]


def block_kernel(
    tok, cot, win, wout, gain_in, wffn, segments, lengths, cos_in, sin_in,
    o_block, o_tokens, o_in, o_out, o_gain, o_ffn,
    x, rel_t, rel_c, w2, wall, wfa, wfb, gb, grow, first2, raw, po,
    q0, q1, kk, vv, prob, att, mxs, mix, sec2, dy2, acta, actb, asend,
    dsb, osb, dsr, osr, rsz, gr, gs, gt, dstate, dmb, daf, dmix,
    dkk, dvv, dqq, dpj, dpx, dfb, dfr, igs, agr, agz, agt, agh, ago,
    bos, obs, bor, tgs, tgr, gg, ggq, gsum, ggt, gain, gflat, doc_col, doc_row, cos_t, sin_t, sems,
):
    dp = lax.axis_index("dp")
    c = lax.axis_index("ctx")
    zh = lax.div(c, 8)
    g = lax.rem(c, 8)
    j = lax.div(g, 2)
    k = lax.rem(c, 2)
    chips = (j, j + 1 - 2 * lax.rem(j, 2), j + 2 - 4 * lax.div(j, 2), 3 - j)
    cores = (k, 1 - k)

    def quad(d, e):
        return (dp, zh * 8 + 2 * chips[d] + cores[e])

    sib = quad(0, 1)
    czp = lax.rem(c + 8, 16)
    zp = (dp, lax.rem(c + 8, 16))
    zps = (dp, 8 * (1 - zh) + 2 * j + 1 - k)
    yp = (1 - dp, c)
    diag = (1 - dp, lax.rem(c + 8, 16))
    team = 2 * dp + zh
    team_y = 2 * (1 - dp) + zh
    team_z = 2 * dp + 1 - zh
    team_d = 3 - team
    w = Wires(sems)
    others = [(d, e) for d in range(4) for e in range(2) if (d, e) != (0, 0)]

    zl, xx = lax.div(j, 2), lax.rem(j, 2)
    keeper = (xx, 8 * k + 4 * dp + 2 * zh + zl)
    owner_of = (zl, 8 * xx + 4 * k + 2 * dp + zh)
    alone = jnp.logical_and(keeper[0] == dp, keeper[1] == c)
    apart = jnp.logical_not(alone)

    barrier = pltpu.get_barrier_semaphore()
    peers = [quad(d, e) for d, e in others] + [zp, zps, yp, diag]
    for peer in peers:
        pl.semaphore_signal(barrier, inc=1, device_id=peer, device_id_type=MESH)

    s_cos, s_sin = w.sem(), w.sem()
    w.local(cos_in, cos_t, s_cos)
    w.local(sin_in, sin_t, s_sin)

    limit = lengths[zh]
    docs = segments[zh].astype(F32).astype(BF)
    line = lax.broadcasted_iota(jnp.int32, (512, 512), 0)
    cell = lax.broadcasted_iota(jnp.int32, (512, 512), 1)
    same_place = (line == cell).astype(F32).astype(BF)
    mirrored = (line + 480 - 2 * (line - lax.rem(line, 32)) == cell).astype(F32).astype(BF)
    for half, order in enumerate((same_place, mirrored)):
        ids = jnp.broadcast_to(docs[half : half + 1, :], (16, 512))
        key = lax.broadcasted_iota(jnp.int32, (1, 512), 1) + 512 * half
        doc_row[0:1, 512 * half : 512 * (half + 1)] = jnp.where(key < limit, _nn(ids, order)[0:1, :], -1.0)
        doc_col[512 * half : 512 * (half + 1), :] = _nt(order, ids)[:, 0:8]
    gain[...] = jnp.zeros_like(gain)
    gain[0:1, 0:68] = gain_in[...].astype(F32)

    @pl.when(apart)
    def _():
        pl.semaphore_signal(barrier, inc=1, device_id=keeper, device_id_type=MESH)
        pl.semaphore_signal(barrier, inc=1, device_id=owner_of, device_id_type=MESH)
        pl.semaphore_wait(barrier, len(peers) + 2)

    @pl.when(alone)
    def _():
        pl.semaphore_wait(barrier, len(peers))

    def many(*shape):
        return [many(*shape[1:]) for _ in range(shape[0])] if shape else w.sem()

    def piece(chip):
        return chip + k * (3 - 2 * chip)

    def row_block(owner, half):
        return owner + half * (15 - 2 * owner)

    my_rows = pl.multiple_of(512 * k, 512)
    other_rows = pl.multiple_of(512 * (1 - k), 512)
    own_head, sib_head = pl.ds(0, 256), pl.ds(256, 256)
    mine = piece(j)
    steps = {}

    def step(name):
        def keep(body):
            steps[name] = body
            return body
        return keep

    def rows_of(buf, offset):
        def at(half, start, count):
            return buf.at[pl.ds(pl.multiple_of(offset * half + start, 32), count)]
        return at

    def rows_steps(name, source, relay, at):
        s_rel, s_here, s_z, s_d = many(2), w.sem(), many(2), w.sem()
        passed = []

        def scatter(src, owner, e, which):
            half = cores[e]
            dst = at(half, pl.multiple_of(row_block(owner, half) * 32, 32), 32)
            w.send(src, dst, quad(2, e), s_z[which])
            w.send(src, dst, quad(1, e), s_here)
            if e == 0:
                w.local(src, dst, s_here)
            else:
                w.send(src, dst, sib, s_here)

        def halves(e):
            @step(f"{name}_out{e}")
            def _():
                w.send(source.at[1 - zh, cores[e]], relay.at[cores[e]], zp, s_rel[e])

            @step(f"{name}_own{e}")
            def _():
                scatter(source.at[zh, cores[e]], c, e, 0)

            @step(f"{name}_rel{e}")
            def _():
                w.arrived(relay.at[cores[e]], s_rel[e])
                scatter(relay.at[cores[e]], czp, e, 1)

            @step(f"{name}_fwd{e}")
            def _():
                first = (zh if e == 0 else 1 - zh) * 8 + 2 * chips[2]
                rows = at(k, pl.multiple_of(32 * (first + k * (14 - 2 * first)), 64), 64)
                w.arrived(rows, s_z[e])
                passed.append(w.send(rows, rows, quad(1, 0), s_d))

        halves(0)
        halves(1)
        return s_here, s_d, passed

    s_x, s_xd, _ = rows_steps("tok", tok, rel_t, rows_of(x, 0))
    s_c, s_cd, cot_passed = rows_steps("cot", cot, rel_c, rows_of(dy2, 512))

    def head_rows(t):
        return w2.at[pl.ds(pl.multiple_of(64 * t, 64), 64)]

    def exchange(name, src, at, keep):
        sem = many(4)

        @step(f"{name}_start")
        def _():
            w.send(src, at(team), zp, sem[1])
            w.send(src, at(team), yp, sem[0])
            if keep:
                w.local(src, at(team), sem[3])

        @step(f"{name}_pass")
        def _():
            w.arrived(at(team_z), sem[1])
            w.send(at(team_z), at(team_z), yp, sem[2])

        def end():
            w.arrived(at(team_y), sem[0])
            w.arrived(at(team_d), sem[2])
            if keep:
                w.arrived(at(team), sem[3])

        return end

    s_move, s_w2, s_gq, s_wq, s_ws = w.sem(), w.sem(), w.sem(), many(3), w.sem()
    gains_end = exchange("gain", gain, lambda t: gb.at[t, g], True)
    heads_end = exchange("win", head_rows(team), head_rows, False)
    wout_end = exchange("wout", wout, lambda t: wall.at[t, j, k], True)
    move = pltpu.make_async_remote_copy(
        src_ref=win, dst_ref=head_rows(lax.rem(g, 4)), send_sem=w.sem(), recv_sem=s_move,
        device_id=keeper, device_id_type=MESH,
    )

    @step("move")
    def _():
        pl.when(apart)(move.start)
        pl.when(alone)(lambda: pltpu.make_async_copy(win, head_rows(team), s_move).start())

    @step("moved")
    def _():
        w.arrived(head_rows(team), s_move)

    @step("gain_end")
    def _():
        gains_end()
        for d, e in others:
            w.send(gb.at[:, g], gb.at[:, g], quad(d, e), s_gq)

    @step("win_end")
    def _():
        heads_end()
        w.send(w2.at[own_head], w2.at[sib_head], sib, s_w2)

    @step("wout_end")
    def _():
        wout_end()
        for d in (2, 1):
            w.send(wall.at[:, j, k], wall.at[:, j, k], quad(d, 0), s_wq[d - 1])

    @step("wout_fwd")
    def _():
        w.arrived(wall.at[:, chips[2], k], s_wq[1])
        w.send(wall.at[:, chips[2], k], wall.at[:, chips[2], k], quad(1, 0), s_wq[2])

    @step("wout_sib")
    def _():
        for d in (1, 3):
            w.arrived(wall.at[:, j, k], s_wq[d - 1])
        w.send(wall.at[:, :, k], wall.at[:, :, k], sib, s_ws)

    parts = ((0, 80, wfa, acta, 320, 384), (80, 64, wfb, actb, 256, 256))
    s_f = many(2, 2, 4, 3)
    held = [[], []]

    def source(part, kind):
        return wffn.at[kind, pl.ds(parts[part][0], parts[part][1])]

    def unit(part, kind, far, slot):
        _, rows, buf, _, _, second = parts[part]
        return buf.at[kind, pl.ds(second * far + rows * slot, rows)]

    def unit_steps(part):
        sem = s_f[part]

        @step(f"u{part}_own")
        def _():
            for kind in range(3):
                w.local(source(part, kind), unit(part, kind, 0, 0), sem[0][0][kind])
                w.send(source(part, kind), unit(part, kind, 1, 0), sib, sem[1][0][kind])
                if part == 0:
                    wfa[kind, 320:384, :] = jnp.zeros((64, 1024), BF)

        @step(f"u{part}_y")
        def _():
            for kind in range(3):
                w.send(source(part, kind), unit(part, kind, 0, 1), yp, sem[0][1][kind])

        def from_z(kind):
            @step(f"u{part}_z{kind}")
            def _():
                w.send(source(part, kind), unit(part, kind, 0, 2), zp, sem[0][2][kind])

            @step(f"u{part}_f{kind}")
            def _():
                here = unit(part, kind, 0, 2)
                w.arrived(here, sem[0][2][kind])
                held[part].append(w.send(here, unit(part, kind, 0, 3), yp, sem[0][3][kind]))
                held[part].append(w.send(here, unit(part, kind, 1, 2), sib, sem[1][2][kind]))

        def ready(slot):
            @step(f"u{part}_s{slot}")
            def _():
                for kind in range(3):
                    here = unit(part, kind, 0, slot)
                    w.arrived(here, sem[0][slot][kind])
                    held[part].append(w.send(here, unit(part, kind, 1, slot), sib, sem[1][slot][kind]))

        for kind in range(3):
            from_z(kind)
        ready(1)
        ready(3)

        @step(f"u{part}_all")
        def _():
            for kind in range(3):
                w.arrived(unit(part, kind, 0, 0), sem[0][0][kind])
                for slot in range(4):
                    w.arrived(unit(part, kind, 1, slot), sem[1][slot][kind])

    unit_steps(0)
    unit_steps(1)

    lane = lax.broadcasted_iota(jnp.int32, (1, LANES), 1)
    low_row = lane < HALF_LANES

    @step("gains")
    def _():
        w.arrived(gb.at[:, pl.ds(0, 7)], s_gq)
        chunks = [jnp.zeros((1, LANES), F32) for _ in range(18)]
        for i in range(32):
            row = gb[i // 8, i % 8, 0:1, :]
            place, shift = divmod(68 * i, LANES)
            moved = pltpu.roll(row, shift, 1) if shift else row
            chunks[place] = chunks[place] + jnp.where(lane >= shift, moved, 0.0)
            if shift + 68 > LANES:
                chunks[place + 1] = chunks[place + 1] + jnp.where(lane < shift, moved, 0.0)
        for n in range(8):
            grow[0:1, LANES * n : LANES * (n + 1)] = chunks[n]
            grow[1:2, LANES * n : LANES * (n + 1)] = chunks[8 + n]
        flipped = pltpu.roll(chunks[16], HALF_LANES, 1)
        grow[2:3, 0:LANES] = jnp.where(low_row, chunks[16], flipped)
        grow[2:3, LANES : 2 * LANES] = jnp.where(low_row, flipped, chunks[16])

    def attn_gain():
        return grow[0:1, :]

    def ffn_gain():
        return grow[1:2, :]

    def query_gain():
        return grow[2:3, 0:LANES]

    def key_gain():
        return grow[2:3, LANES : 2 * LANES]

    s_raw, s_first = w.sem(), w.sem()

    @step("project")
    def _():
        w.arrived(x.at[pl.ds(0, 256)], s_x)
        w.arrived(x.at[pl.ds(0, 128)], s_xd)
        w.arrived(w2.at[sib_head], s_w2)
        weight = attn_gain()

        def rows_of_256(t, carry):
            rows = pl.multiple_of(t * 256, 256)
            values = x[pl.ds(rows, 256), :].astype(F32)
            scale = lax.rsqrt(jnp.mean(values * values, axis=1, keepdims=True) + EPS)
            first = (values * scale * weight).astype(BF)
            here = pl.multiple_of(my_rows + rows, 256)
            first2[pl.ds(here, 256), :] = first
            po[pl.ds(rows, 256), :] = _nt(first, w2[sib_head, :])
            raw[pl.ds(here, 256), :] = _nt(first, w2[own_head, :])
            return carry

        lax.fori_loop(0, 2, rows_of_256, 0)
        w.send(po, raw.at[pl.ds(my_rows, 512)], sib, s_raw)

    @step("first_sib")
    def _():
        w.send(first2.at[pl.ds(my_rows, 512)], first2.at[pl.ds(my_rows, 512)], sib, s_first)

    low = lax.broadcasted_iota(jnp.int32, (256, LANES), 1) < HALF_LANES
    quarter = lax.rem(lax.broadcasted_iota(jnp.int32, (256, LANES), 1), HALF_LANES) < 32

    def swap(v):
        return jnp.where(quarter, pltpu.roll(v, 96, 1), pltpu.roll(v, 32, 1))

    def head_sum(v):
        first = jnp.sum(jnp.where(low, v, 0.0), axis=1, keepdims=True)
        second = jnp.sum(jnp.where(low, 0.0, v), axis=1, keepdims=True)
        return jnp.where(low, first, second)

    def inverse_root(v):
        return lax.rsqrt(head_sum(v * v) * (1.0 / HEAD_DIM) + EPS)

    @step("rotate")
    def _():
        w.arrived(raw.at[pl.ds(0, 512)], s_raw)
        w.arrived(cos_t, s_cos)
        w.arrived(sin_t, s_sin)
        query_weight, key_weight = query_gain(), key_gain()

        def rotate_rows(t, carry):
            rows = pl.ds(pl.multiple_of(t * 256, 256), 256)
            cosine, sine = cos_t[rows, :], sin_t[rows, :]
            query = raw[rows, 0:LANES]
            both = raw[rows, LANES : 2 * LANES]
            query = query * inverse_root(query) * query_weight
            query = (query * cosine + swap(query) * sine) * (HEAD_DIM**-0.5)
            q0[rows, :] = jnp.where(low, query, 0.0).astype(BF)
            q1[rows, :] = jnp.where(low, 0.0, query).astype(BF)
            key = both * inverse_root(both) * key_weight
            key = key * cosine + swap(key) * sine
            kk[rows, :] = jnp.where(low, key, pltpu.roll(key, HALF_LANES, 1)).astype(BF)
            vv[rows, :] = jnp.where(low, pltpu.roll(both, HALF_LANES, 1), both).astype(BF)
            return carry

        lax.fori_loop(0, 4, rotate_rows, 0)

    s_mix, s_md, s_mz = w.sem(), w.sem(), many(2)
    head_lanes = pl.ds(pl.multiple_of(LANES * g, LANES), LANES)
    z_lanes = pl.ds(pl.multiple_of(256 * chips[2], 256), 256)
    late = []

    def forward_tile(t):
        @step(f"at{t}")
        def _():
            lo, n = 256 * t, 256 * (t + 1)
            place = lax.broadcasted_iota(jnp.int32, (256, n), 0) + lo
            key_place = lax.broadcasted_iota(jnp.int32, (256, n), 1)
            same = doc_col[lo : lo + 256, 0:1] == doc_row[0:1, 0:n]
            mask = (same & (key_place <= place)) | (key_place == place)
            outs = []
            for h, q in enumerate((q0, q1)):
                scores = jnp.where(mask, _nt(q[lo : lo + 256, :], kk[0:n, :]), MASKED)
                peak = jnp.max(scores, axis=1, keepdims=True)
                expo = jnp.exp(scores - peak)
                weights = (expo * (1.0 / jnp.sum(expo, axis=1, keepdims=True))).astype(BF)
                prob[h, lo : lo + 256, 0:n] = weights
                outs.append(_nn(weights, vv[0:n, :]))
            attended = jnp.where(low, outs[0], outs[1])
            att[lo : lo + 256, :] = attended
            mxs[lo : lo + 256, :] = attended.astype(BF)
            half = t // 2
            dst = mix.at[pl.ds(256 * (t % 2), 256), head_lanes]
            src = mxs.at[pl.ds(lo, 256)]
            w.send(src, dst, (dp, zh * 8 + 2 * chips[2] + half), s_mz[t % 2])
            w.send(src, dst, (dp, zh * 8 + 2 * chips[1] + half), s_mix)
            away = pltpu.make_async_remote_copy(
                src_ref=src, dst_ref=dst, send_sem=w.sem(), recv_sem=s_mix, device_id=sib, device_id_type=MESH
            )
            pl.when(k == half)(lambda: pltpu.make_async_copy(src, dst, s_mix).start())
            pl.when(k != half)(away.start)
            late.append((half, away))

    def pass_mixed(r):
        @step(f"mix_fwd{r}")
        def _():
            part = mix.at[pl.ds(256 * r, 256), z_lanes]
            w.arrived(part, s_mz[r])
            w.send(part, part, quad(1, 0), s_md)

    for t in range(4):
        forward_tile(t)
    pass_mixed(0)
    pass_mixed(1)

    s_dy, s_sec = w.sem(), w.sem()

    @step("dy")
    def _():
        w.arrived(dy2.at[pl.ds(0, 256)], s_c)
        w.arrived(dy2.at[pl.ds(0, 128)], s_cd)
        w.finish(cot_passed)

        def drop_rows(t, carry):
            rows = pl.ds(pl.multiple_of(my_rows + t * 128, 128), 128)
            place = lax.broadcasted_iota(jnp.int32, (128, 1), 0) + (my_rows + t * 128)
            kept = (place < limit).astype(F32).astype(BF)
            dy2[rows, :] = dy2[rows, :] * kept
            return carry

        lax.fori_loop(0, 4, drop_rows, 0)
        w.send(dy2.at[pl.ds(my_rows, 512)], dy2.at[pl.ds(my_rows, 512)], sib, s_dy)

    def attended_rows(rows):
        total = None
        for n in range(4):
            term = _nn(mix[rows, 256 * n : 256 * (n + 1)], wall[n].reshape(256, 1024))
            total = term if total is None else total + term
        return total

    @step("second")
    def _():
        w.arrived(wall.at[:, :, 0], s_ws)
        w.arrived(mix.at[pl.ds(0, 256)], s_mix)
        w.arrived(mix.at[:, pl.ds(0, 256)], s_md)
        weight = ffn_gain()

        def project_out(t, carry):
            rows = pl.ds(pl.multiple_of(t * 256, 256), 256)
            state = x[rows, :].astype(F32) + attended_rows(rows)
            scale = lax.rsqrt(jnp.mean(state * state, axis=1, keepdims=True) + EPS)
            here = pl.ds(pl.multiple_of(my_rows + t * 256, 256), 256)
            sec2[here, :] = (state * scale * weight).astype(BF)
            return carry

        lax.fori_loop(0, 2, project_out, 0)
        w.send(sec2.at[pl.ds(my_rows, 512)], sec2.at[pl.ds(my_rows, 512)], sib, s_sec)

    class Sum:
        def __init__(self, name, buf, into, which):
            self.buf, self.into, self.which = buf, into, which
            self.sems = many(3, 2)
            for t in range(2):
                if name == "os":
                    step(f"{name}_x{t}")(lambda t=t: self.over_x(t))
                step(f"{name}_z{t}")(lambda t=t: self.over_z(t))

        def rows(self, d, t):
            return pl.ds(pl.multiple_of(256 * t + 64 * piece(chips[d]), 64), 64)

        def over_x(self, t):
            for d, slot in ((3, 1), (1, 0)):
                w.send(self.buf.at[self.rows(d, t)], self.into.at[slot, t], quad(1, 0), self.sems[slot][t])

        def over_z(self, t):
            w.arrived(self.into.at[1, t], self.sems[1][t])
            total = self.buf[self.rows(2, t), :].astype(F32) + self.into[1, t].astype(F32)
            rsz[self.which, t] = total.astype(BF)
            w.send(rsz.at[self.which, t], self.into.at[2, t], quad(2, 0), self.sems[2][t])

        def result(self, t):
            total = self.buf[self.rows(0, t), :].astype(F32)
            for slot in (0, 2):
                w.arrived(self.into.at[slot, t], self.sems[slot][t])
                total = total + self.into[slot, t].astype(F32)
            return total

    sum_ds, sum_os, sum_df = Sum("ds", dsb, dsr, 0), Sum("os", osb, osr, 1), Sum("df", dfb, dfr, 2)

    s_act, s_gr, s_near, s_gt = many(2), many(2, 3), many(2), many(2, 3)
    acted = []

    def part_steps(part):
        start, rows_kept, buf, acts, count, second = parts[part]
        span = pl.ds(start, rows_kept)

        def feed_forward(t):
            @step(f"ff{part}{t}")
            def _():
                if part == 1 and t == 0:
                    w.finish(acted)
                rows = pl.ds(pl.multiple_of(my_rows + 256 * t, 256), 256)
                here = pl.ds(256 * t, 256)
                gate = _nt(sec2[rows, :], buf[0])
                up = _nt(sec2[rows, :], buf[1])
                d_hidden = _nt(dy2[rows, :], buf[2])
                sigmoid = 1.0 / (1.0 + jnp.exp(-gate))
                silu = gate * sigmoid
                d_gate = (d_hidden * up * (sigmoid + silu * (1.0 - sigmoid))).astype(BF)
                d_up = (d_hidden * silu).astype(BF)
                hidden = (silu * up).astype(BF)
                for n, value in enumerate((d_gate, d_up, hidden)):
                    acts[n, rows, :] = value[:, 0:second]
                    asend[n, here, 0:count] = value[:, second : second + count]
                lanes = pl.ds(0, second)
                acted.append(w.send(asend.at[:, here, lanes], acts.at[:, rows], sib, s_act[part]))
                d_second = _nn(d_gate, buf[0]) + _nn(d_up, buf[1])
                result = _nn(hidden, buf[2])
                if part == 1:
                    d_second = d_second + dsb[here, :].astype(F32)
                    result = result + osb[here, :].astype(F32)
                dsb[here, :] = d_second.astype(BF)
                osb[here, :] = result.astype(BF)
                if part == 1:
                    sum_ds.over_x(t)

        @step(f"wg{part}_in")
        def _():
            w.finish(held[part])
            w.arrived(acts.at[:, pl.ds(0, 512)], s_act[part])
            if part == 0:
                w.arrived(sec2.at[pl.ds(0, 512)], s_sec)
                w.arrived(dy2.at[pl.ds(0, 512)], s_dy)

        def weight_grads(kind):
            @step(f"wg{part}{kind}")
            def _():
                right = dy2 if kind == 2 else sec2

                def columns(n, carry):
                    cols = pl.ds(pl.multiple_of(n * 512, 512), 512)
                    buf[kind, 0:count, cols] = _tn(acts[kind], right[:, cols])[0:count, :].astype(BF)
                    return carry

                lax.fori_loop(0, 2, columns, 0)

        def pass_grads(kind):
            @step(f"gr{part}_y{kind}")
            def _():
                rows = buf.at[kind, pl.ds(rows_kept * 3, rows_kept)]
                w.send(rows, gr.at[1, kind, span], yp, s_gr[part][kind])

            @step(f"gr{part}_z{kind}")
            def _():
                w.arrived(gr.at[1, kind, span], s_gr[part][kind])
                gs[kind, span, :] = (
                    buf[kind, 2 * rows_kept : 3 * rows_kept, :].astype(F32) + gr[1, kind, span, :].astype(F32)
                ).astype(BF)
                w.send(gs.at[kind, span], gt.at[kind, span], zp, s_gt[part][kind])

        @step(f"gr{part}_near")
        def _():
            w.send(buf.at[:, pl.ds(rows_kept, rows_kept)], gr.at[0, :, span], yp, s_near[part])

        @step(f"gr{part}_end")
        def _():
            w.arrived(gr.at[0, :, span], s_near[part])
            for kind in range(3):
                w.arrived(gt.at[kind, span], s_gt[part][kind])
                o_ffn[kind, span, :] = (
                    buf[kind, 0:rows_kept, :].astype(F32)
                    + gr[0, kind, span, :].astype(F32) + gt[kind, span, :].astype(F32)
                ).astype(BF)

        feed_forward(0)
        feed_forward(1)
        for kind in range(3):
            weight_grads(kind)
            pass_grads(kind)

    part_steps(0)
    part_steps(1)

    s_dm, s_da, s_das = w.sem(), many(3), w.sem()
    terms = {"ffn": jnp.zeros((1, 1024), F32), "attn": jnp.zeros((1, 1024), F32)}

    def state_steps(t):
        @step(f"st{t}")
        def _():
            start = 256 * t + 64 * mine
            rows = pl.ds(pl.multiple_of(start, 64), 64)
            state = x[rows, :].astype(F32) + attended_rows(rows)
            bos[t] = state
            scale = lax.rsqrt(jnp.mean(state * state, axis=1, keepdims=True) + EPS)
            normed = state * scale
            total = sum_ds.result(t)
            terms["ffn"] = terms["ffn"] + jnp.sum(total * normed, axis=0, keepdims=True)
            weighted = total * ffn_gain()
            inner = jnp.mean(weighted * normed, axis=1, keepdims=True)
            grad = dy2[pl.ds(pl.multiple_of(my_rows + start, 64), 64), :].astype(F32) + scale * (weighted - normed * inner)
            dstate[t] = grad
            low_grad = grad.astype(BF)
            daf[k, t, mine] = low_grad
            for n in range(4):
                dmb[t, :, 256 * n : 256 * (n + 1)] = _nt(low_grad, wall[n].reshape(256, 1024)).astype(BF)
            for d, e in others:
                lanes = pl.ds(pl.multiple_of(LANES * (2 * chips[d] + cores[e]), LANES), LANES)
                w.send(dmb.at[t, :, lanes], dmix.at[k, t, mine], quad(d, e), s_dm)
            w.local(dmb.at[t, :, head_lanes], dmix.at[k, t, mine], s_dm)

    state_steps(0)
    state_steps(1)

    @step("da_out")
    def _():
        for d in (2, 1):
            w.send(daf.at[k, :, mine], daf.at[k, :, mine], quad(d, 0), s_da[d - 1])

    @step("da_fwd")
    def _():
        far = piece(chips[2])
        w.arrived(daf.at[k, :, far], s_da[1])
        w.send(daf.at[k, :, far], daf.at[k, :, far], quad(1, 0), s_da[2])

    @step("da_sib")
    def _():
        for d in (1, 3):
            w.arrived(daf.at[k, :, mine], s_da[d - 1])
        w.send(daf.at[k], daf.at[k], sib, s_das)

    home = zh + k * (1 - 2 * zh)

    def send_home(buf, into, sem):
        w.send(buf.at[1 - home, 0], into.at[zh, k], zp, sem)
        w.send(buf.at[1 - home, 1], into.at[zh, k], zps, sem)
        w.send(buf.at[home, 1], into.at[zh, k], sib, sem)
        w.local(buf.at[home, 0], into.at[zh, k], sem)

    s_bo, s_tg = w.sem(), w.sem()

    @step("block")
    def _():
        for t in range(2):
            total = bos[t] + sum_os.result(t)
            obs[t] = total.astype(BF).reshape(2, 32, 1024)
        send_home(obs, bor, s_bo)

    @step("block_end")
    def _():
        w.arrived(bor, s_bo)
        o_block[...] = bor[...]

    @step("bw_in")
    def _():
        w.arrived(dmix, s_dm)
        dkk[...] = jnp.zeros_like(dkk)
        dvv[...] = jnp.zeros_like(dvv)

    def backward_tile(t):
        @step(f"bw{t}")
        def _():
            lo, n = 256 * t, 256 * (t + 1)
            d_out = dmix[...].reshape(1024, LANES)[lo : lo + 256, :].astype(F32)
            product = d_out * att[lo : lo + 256, :]
            results = []
            for h, q in enumerate((q0, q1)):
                here = low if h == 0 else jnp.logical_not(low)
                d_head = jnp.where(here, d_out, 0.0).astype(BF)
                delta = jnp.sum(jnp.where(here, product, 0.0), axis=1, keepdims=True)
                weights = prob[h, lo : lo + 256, 0:n]
                pulled = _nt(d_head, vv[0:n, :])
                d_scores = (weights.astype(F32) * (pulled - delta)).astype(BF)
                results.append(_nn(d_scores, kk[0:n, :]))
                dkk[0:n, :] += _tn(d_scores, q[lo : lo + 256, :])
                dvv[0:n, :] += _tn(weights, d_head)
            dqq[lo : lo + 256, :] = jnp.where(low, results[0], results[1]) * (HEAD_DIM**-0.5)

    for t in range(4):
        backward_tile(t)
    s_dpx = w.sem()

    @step("back")
    def _():
        query_weight, key_weight = query_gain(), key_gain()

        def back_rows(t, carry):
            query_sum, key_sum = carry
            rows = pl.ds(pl.multiple_of(t * 256, 256), 256)
            cosine, sine = cos_t[rows, :], sin_t[rows, :]
            query = raw[rows, 0:LANES]
            both = raw[rows, LANES : 2 * LANES]

            def through(values, grads, gain_row):
                scale = inverse_root(values)
                normed = values * scale
                grads = grads * cosine - swap(grads) * sine
                weighted = grads * gain_row
                inner = head_sum(weighted * normed) * (1.0 / HEAD_DIM)
                return scale * (weighted - normed * inner), jnp.sum(grads * normed, axis=0, keepdims=True)

            query_back, query_term = through(query, dqq[rows, :], query_weight)
            d_key = dkk[rows, :]
            d_key = d_key + pltpu.roll(d_key, HALF_LANES, 1)
            key_back, key_term = through(both, d_key, key_weight)
            d_value = dvv[rows, :]
            d_value = d_value + pltpu.roll(d_value, HALF_LANES, 1)
            dpj[rows, 0:LANES] = query_back.astype(BF)
            dpj[rows, LANES : 2 * LANES] = jnp.where(low, key_back, d_value).astype(BF)
            return query_sum + query_term, key_sum + key_term

        zero_row = jnp.zeros((1, LANES), F32)
        query_sum, key_sum = lax.fori_loop(0, 4, back_rows, (zero_row, zero_row))
        w.send(dpj.at[pl.ds(other_rows, 512)], dpx, sib, s_dpx)
        gg[:, 2 * LANES : 3 * LANES] = jnp.zeros((8, LANES), F32)
        gg[0:1, 2 * LANES : 3 * LANES] = query_sum + pltpu.roll(query_sum, HALF_LANES, 1)
        gg[1:2, 2 * LANES : 3 * LANES] = key_sum

    def first_steps(t):
        @step(f"df{t}")
        def _():
            if t == 0:
                w.arrived(dpx, s_dpx)
            here = pl.ds(256 * t, 256)
            rows = pl.ds(pl.multiple_of(my_rows + 256 * t, 256), 256)
            dfb[here, :] = (_nn(dpj[rows, :], w2[own_head, :]) + _nn(dpx[here, :], w2[sib_head, :])).astype(BF)
            sum_df.over_x(t)

    first_steps(0)
    first_steps(1)
    returned = []

    def term_steps(name, rows, value, result):
        sem = many(4)

        @step(f"{name}_y")
        def _():
            term = value()
            count = rows.stop - rows.start
            for p in range(4):
                igs[p, rows, :] = term[count * p : count * (p + 1), :].astype(BF)
            at = pl.ds(rows.start, count)
            w.send(igs.at[team_d, at], agr.at[1, at], yp, sem[1])
            w.send(igs.at[team_y, at], agr.at[0, at], yp, sem[0])

        at = pl.ds(rows.start, rows.stop - rows.start)

        @step(f"{name}_z")
        def _():
            w.arrived(agr.at[1, at], sem[1])
            agz[rows, :] = (igs[team_z, rows, :].astype(F32) + agr[1, rows, :].astype(F32)).astype(BF)
            w.send(agz.at[at], agt.at[at], zp, sem[2])

        @step(f"{name}_sum")
        def _():
            w.arrived(agr.at[0, at], sem[0])
            w.arrived(agt.at[at], sem[2])
            agh[rows, :] = (
                igs[team, rows, :].astype(F32) + agr[0, rows, :].astype(F32) + agt[rows, :].astype(F32)
            ).astype(BF)

        back = pltpu.make_async_remote_copy(
            src_ref=agh.at[at], dst_ref=ago.at[at], send_sem=w.sem(), recv_sem=sem[3],
            device_id=owner_of, device_id_type=MESH,
        )
        returned.append(back)

        @step(f"{name}_give")
        def _():
            pl.when(apart)(back.start)
            pl.when(alone)(lambda: pltpu.make_async_copy(agh.at[at], ago.at[at], sem[3]).start())

        @step(f"{name}_end")
        def _():
            w.arrived(ago.at[at], sem[3])
            result[...] = ago[rows, :]

    def in_value():
        w.arrived(first2.at[pl.ds(0, 512)], s_first)
        return _tn(dpj[...], first2[...])

    def out_value():
        w.arrived(daf.at[0], s_das)
        return _tn(mxs[...], daf[...].reshape(1024, 1024))

    term_steps("in", slice(0, 64), in_value, o_in)
    term_steps("out", slice(64, 96), out_value, o_out)

    def token_steps(t):
        @step(f"tg{t}")
        def _():
            rows = pl.ds(pl.multiple_of(256 * t + 64 * mine, 64), 64)
            values = x[rows, :].astype(F32)
            scale = lax.rsqrt(jnp.mean(values * values, axis=1, keepdims=True) + EPS)
            normed = values * scale
            total = sum_df.result(t)
            terms["attn"] = terms["attn"] + jnp.sum(total * normed, axis=0, keepdims=True)
            weighted = total * attn_gain()
            inner = jnp.mean(weighted * normed, axis=1, keepdims=True)
            grad = dstate[t] + scale * (weighted - normed * inner)
            tgs[t] = grad.astype(BF).reshape(2, 32, 1024)

    token_steps(0)
    token_steps(1)

    @step("tok_home")
    def _():
        send_home(tgs, tgr, s_tg)

    @step("tok_end")
    def _():
        w.arrived(tgr, s_tg)
        o_tokens[...] = tgr[...]

    s_gg, s_gt4 = w.sem(), many(3)

    @step("gg_out")
    def _():
        for n in range(8):
            gg[n : n + 1, 0:LANES] = terms["attn"][:, LANES * n : LANES * (n + 1)]
            gg[n : n + 1, LANES : 2 * LANES] = terms["ffn"][:, LANES * n : LANES * (n + 1)]
        for d, e in others:
            w.send(gg, ggq.at[g], quad(d, e), s_gg)
        w.local(gg, ggq.at[g], s_gg)

    @step("gg_sum")
    def _():
        w.arrived(ggq, s_gg)
        total = ggq[0]
        for n in range(1, 8):
            total = total + ggq[n]
        gsum[...] = total
        for n, peer in enumerate((yp, zp, diag)):
            w.send(gsum, ggt.at[n], peer, s_gt4[n])

    @step("gg_end")
    def _():
        total = gsum[...]
        for n in range(3):
            w.arrived(ggt.at[n], s_gt4[n])
            total = total + ggt[n]
        gflat[0:8, :] = total[:, 0:LANES]
        gflat[8:16, :] = total[:, LANES : 2 * LANES]
        key_part = pltpu.roll(total[1:2, 2 * LANES : 3 * LANES], HALF_LANES, 1)
        gflat[16:17, :] = jnp.where(low_row, total[0:1, 2 * LANES : 3 * LANES], key_part)
        place = 68 * (8 * team + g)
        line, shift = lax.div(place, LANES), lax.rem(place, LANES)
        back = lax.rem(LANES - shift, LANES)
        left = pltpu.roll(gflat[pl.ds(line, 1), :], back, 1)
        right = pltpu.roll(gflat[pl.ds(line + 1, 1), :], back, 1)
        o_gain[...] = jnp.where(lane < LANES - shift, left, right)[:, 0:68]

    for turn, name in enumerate(ORDER):
        w.turn = turn
        steps.pop(name)()
        w.finish([copy for copy in w.pending if w.born[id(copy)] < turn - LEFT_ALONE])
    assert not steps, sorted(steps)
    w.finish()
    for half, away in late:
        pl.when(k != half)(away.wait_send)
    pl.when(apart)(move.wait_send)
    for back in returned:
        pl.when(apart)(back.wait_send)


ORDER = (
    "tok_out0", "cot_own1", "wout_start", "tok_out1", "cot_own0", "u0_y", "u1_own", "tok_own0", "move",
    "tok_own1", "gain_start", "tok_rel0", "wout_pass", "cot_out0", "cot_fwd0", "tok_rel1", "gain_pass",
    "moved", "cot_out1", "u0_s1", "gain_end", "win_start", "tok_fwd1", "tok_fwd0", "wout_end", "win_pass",
    "u0_z1", "gains", "win_end", "u0_own", "cot_rel1", "project", "u1_y", "u0_z0", "wout_fwd", "cot_rel0",
    "u0_z2", "rotate", "at1", "u0_f1", "at3", "u0_f0", "at0", "at2", "u1_z2", "cot_fwd1", "mix_fwd1", "u0_f2",
    "mix_fwd0", "wout_sib", "u1_f2", "u0_s3", "u1_z1", "u0_all", "u1_z0", "dy", "second", "ff00", "u1_f1",
    "ff01", "first_sib", "u1_f0", "u1_s1", "wg0_in", "wg01", "gr0_y1", "wg00", "u1_s3", "gr0_y0", "u1_all",
    "ff10", "gr0_z1", "ff11", "ds_z0", "wg02", "gr0_z0", "wg1_in", "wg11", "wg12", "gr1_y1", "os_x0",
    "gr0_y2", "wg10", "gr1_y2", "ds_z1", "gr1_y0", "st0", "gr1_z1", "st1", "gr0_near", "gr0_z2", "da_out",
    "os_x1", "bw_in", "bw3", "bw2", "bw1", "gr1_z0", "bw0", "back", "gr1_z2", "os_z0", "os_z1", "da_fwd",
    "in_y", "gr1_near", "df0", "in_z", "da_sib", "df_z0", "df1", "out_y", "block", "in_sum", "df_z1", "tg0",
    "out_z", "in_give", "gr1_end", "tg1", "out_sum", "tok_home", "gg_out", "gg_sum", "in_end", "out_give",
    "block_end", "gr0_end", "tok_end", "gg_end", "out_end",
)


TEAM_SCRATCH = (
    ((512, 1024), BF), ((2, 32, 1024), BF), ((2, 32, 1024), BF), ((512, 1024), BF),
    ((4, 4, 2, 32, 1024), BF), ((3, 704, 1024), BF), ((3, 512, 1024), BF), ((4, 8, 8, 128), F32), ((8, 1024), F32),
    ((1024, 1024), BF), ((1024, 256), F32), ((512, 256), F32),
    ((1024, 128), BF), ((1024, 128), BF), ((1024, 128), BF), ((1024, 128), BF), ((2, 1024, 1024), BF),
    ((1024, 128), F32), ((1024, 128), BF), ((512, 1024), BF), ((1024, 1024), BF), ((1024, 1024), BF),
    ((3, 1024, 384), BF), ((3, 1024, 256), BF), ((3, 512, 384), BF),
    ((512, 1024), BF), ((512, 1024), BF), ((3, 2, 64, 1024), BF), ((3, 2, 64, 1024), BF), ((3, 2, 64, 1024), BF),
    ((2, 3, 144, 1024), BF), ((3, 144, 1024), BF), ((3, 144, 1024), BF),
    ((2, 64, 1024), F32), ((2, 64, 1024), BF), ((2, 2, 4, 64, 1024), BF), ((2, 2, 4, 64, 128), BF),
    ((1024, 128), F32), ((1024, 128), F32), ((1024, 128), F32), ((1024, 256), BF), ((512, 256), BF),
    ((512, 1024), BF), ((3, 2, 64, 1024), BF),
    ((4, 96, 1024), BF), ((2, 96, 1024), BF), ((96, 1024), BF), ((96, 1024), BF), ((96, 1024), BF), ((96, 1024), BF),
    ((2, 64, 1024), F32), ((2, 2, 32, 1024), BF), ((2, 2, 32, 1024), BF), ((2, 2, 32, 1024), BF),
    ((2, 2, 32, 1024), BF),
    ((8, 384), F32), ((8, 8, 384), F32), ((8, 384), F32), ((3, 8, 384), F32), ((8, 128), F32), ((24, 128), F32), ((1024, 8), F32), ((8, 1024), F32),
    ((1024, 128), F32), ((1024, 128), F32),
)


def rotary_lanes(rows):
    width = HEAD_DIM // 2
    freq = (ROPE_BASE ** (-np.arange(width, dtype=np.float32) * np.float32(2.0 / HEAD_DIM))).astype(np.float32)
    angle = (np.arange(rows, dtype=np.float32)[:, None] * freq).astype(np.float32).astype(np.float64)
    cosine, sine = np.cos(angle), np.sin(angle)
    return (
        np.tile(np.concatenate([cosine, cosine], 1), (1, 2)).astype(np.float32),
        np.tile(np.concatenate([-sine, sine], 1), (1, 2)).astype(np.float32),
    )


def on_team(tokens, segments, lengths, attn_in, attn_out, gains, ffn_weights, cotangent):
    batches, block_len, halves, width = tokens.shape
    rows = segments.shape[1]
    cosine, sine = rotary_lanes(2 * rows)
    args = (
        tokens.transpose(0, 2, 1, 3),
        cotangent.transpose(0, 2, 1, 3),
        attn_in,
        attn_out,
        gains[None],
        ffn_weights.transpose(1, 0, 2),
        segments.transpose(0, 2, 1),
        lengths,
        jnp.asarray(cosine),
        jnp.asarray(sine),
    )
    vmem = pl.BlockSpec(memory_space=pltpu.VMEM)
    anywhere = pl.BlockSpec(memory_space=pl.ANY)
    outs = pl.pallas_call(
        block_kernel,
        out_shape=(
            jax.ShapeDtypeStruct((2, 2, 32, 1024), BF),
            jax.ShapeDtypeStruct((2, 2, 32, 1024), BF),
            jax.ShapeDtypeStruct((64, 1024), BF),
            jax.ShapeDtypeStruct((32, 1024), BF),
            jax.ShapeDtypeStruct((1, 68), F32),
            jax.ShapeDtypeStruct((3, 144, 1024), BF),
        ),
        in_specs=[vmem] * 5
        + [anywhere, vmem, pl.BlockSpec(memory_space=pltpu.SMEM), anywhere, anywhere],
        out_specs=(vmem,) * 6,
        scratch_shapes=[pltpu.VMEM(shape, kind) for shape, kind in TEAM_SCRATCH]
        + [pltpu.SemaphoreType.DMA((COPIES,))],
        compiler_params=pltpu.CompilerParams(
            collective_id=0, has_side_effects=True, vmem_limit_bytes=VMEM_BYTES
        ),
    )(*args)
    block, token_grad, in_grad, out_grad, gain_grad, unit_grad = outs
    return (
        block.transpose(0, 2, 1, 3),
        token_grad.transpose(0, 2, 1, 3).astype(F32),
        in_grad.astype(F32),
        out_grad.astype(F32),
        gain_grad[0],
        unit_grad.transpose(1, 0, 2).astype(F32),
    )


VMEM_BYTES = 62 << 20


def solution(mesh):
    dp, ctx = mesh.devices.shape
    if ctx == 2 * KV_HEADS:
        ring = "ctx"
        every = ("dp", "ctx")
        team, run = mesh, on_team
    else:
        ring = ("s", "q", "g")
        every = EVERY
        team = Mesh(mesh.devices.reshape(dp, 2, ctx // (2 * KV_HEADS), KV_HEADS), EVERY)
        run = on_device
    placed = (
        P("dp", ring, None, None),
        P("dp", None, None),
        P("dp"),
        P(every, None),
        P(every, None),
        P(every),
        P(every, None, None),
        P("dp", ring, None, None),
    )
    return jax.shard_map(
        run,
        mesh=team,
        in_specs=placed,
        out_specs=(
            P("dp", ring, None, None),
            P("dp", ring, None, None),
            P(every, None),
            P(every, None),
            P(every),
            P(every, None, None),
        ),
        check_vma=False,
    )
```
